32 devices in a mesh: dp: 4 (over x, core), ctx: 8 (over z, y).
Axes of the slice: x: 2, y: 2, z: 4, core: 2. Of those that a mesh axis runs over, the one named last changes fastest.
Arguments:
- saved_input: bfloat16 [4, 4096, 1024], P('dp', None, 'ctx'), may hold values from -6 to 6
- out_gate: bfloat16 [4, 4096, 1024], P('dp', None, 'ctx'), may hold values from -6 to 6
- grad_out: bfloat16 [4, 4096, 1024], P('dp', None, 'ctx'), may hold values from -6 to 6
- long_filter: float32 [4096, 1024], P('ctx'), may hold values from -0.1875 to 0.1875
Outputs:
- grad_input: bfloat16 [4, 4096, 1024], P('dp', None, 'ctx')
- grad_filter: float32 [4096, 1024], P('ctx', 'dp')
The draws below stay inside these ranges and needn't reach their ends.
All inputs are finite; a program needn't handle non-finite values.
Results may differ from the reference program's by a relative error of at most 0.0085.
Values may be sent and summed in bfloat16 or wider, within the bound.
No kernel may reach another device: no remote copies, remote signals or barrier semaphores. Data moves between devices by JAX's collectives and lax.ppermute only.
A program may use at most 128 MiB of HBM per device.

```python
import math
import jax
import jax.numpy as jnp
from jax import lax

CHANNELS = 4096
SEQ = 1024
BATCH = 4


def shard_levels(key, dims, split, smallest, largest):
    def one(axis_at, shards_of):
        heights = jax.random.uniform(jax.random.fold_in(jax.random.fold_in(key, 6), axis_at), (shards_of,), jnp.float32, smallest / len(split), largest / len(split))
        return jnp.repeat(jnp.exp(heights), dims[axis_at] // shards_of).reshape((-1,) + (1,) * (len(dims) - axis_at - 1))

    factor_of = one(*split[0])
    for cut in split[1:]:
        factor_of = factor_of * one(*cut)
    return factor_of


def bell_draw(rng, dims, width, most, cuts=(), dtype=jnp.bfloat16):
    drawn = jax.random.normal(rng, dims, jnp.float32) * width
    if len(cuts) > 0:
        drawn = shard_levels(rng, dims, cuts, -0.22, 0.18) * drawn
    return jnp.clip(drawn, min=-most, max=most).astype(dtype)


def setup_inputs(seed: int = 0) -> dict:
    keys = jax.random.split(jax.random.key(seed), 5)
    return {
        "saved_input": bell_draw(keys[0], (BATCH, CHANNELS, SEQ), 1.0, 6.0, ((0, 4), (2, 8))),
        "out_gate": bell_draw(keys[1], (BATCH, CHANNELS, SEQ), 1.0, 6.0, ((0, 4), (2, 8))),
        "grad_out": bell_draw(keys[2], (BATCH, CHANNELS, SEQ), 1.0, 6.0, ((0, 4), (2, 8))),
        "long_filter": bell_draw(keys[3], (CHANNELS, SEQ), SEQ ** -0.5, 0.1875, ((0, 8),), jnp.float32),
    }


def reference(saved_input, out_gate, grad_out, long_filter):
    points = 2 * SEQ
    taps_spec = jnp.fft.fft(long_filter.astype(jnp.float32), n=points, axis=-1)

    def per_sequence(running, pieces):
        input_piece, gate_piece, upper_piece = pieces
        conv_grad = (gate_piece.astype(jnp.float32) * upper_piece.astype(jnp.float32)).astype(jnp.bfloat16)
        conv_grad = lax.optimization_barrier(conv_grad)
        input_spec = jnp.fft.fft(input_piece.astype(jnp.float32), n=points, axis=-1)
        grad_spec = jnp.fft.fft(conv_grad.astype(jnp.float32), n=points, axis=-1)
        back_part = jnp.real(jnp.fft.ifft(jnp.conj(taps_spec) * grad_spec, axis=-1))[:, :SEQ]
        cross_part = jnp.real(jnp.fft.ifft(grad_spec * jnp.conj(input_spec), axis=-1))[:, :SEQ]
        return (running + cross_part, back_part.astype(jnp.bfloat16))
    running = jnp.zeros((CHANNELS, SEQ), jnp.float32)
    running, grad_input = lax.scan(per_sequence, running, (saved_input, out_gate, grad_out))
    grad_filter = running * (1.0 / math.sqrt(BATCH * SEQ))
    return (grad_input, grad_filter)
```

```python
import functools
import math

import jax
import jax.numpy as jnp
import ml_dtypes
import numpy as np
from jax import lax
from jax.experimental import pallas as pl
from jax.experimental.pallas import tpu as pltpu
from jax.sharding import PartitionSpec as P

BLOCKS = 8
GROUPS = 9
TILE = 16
C1 = math.cos(math.pi / 8)
C2 = math.cos(math.pi / 4)
C3 = math.cos(3 * math.pi / 8)
LIMIT = 56 * 1024 * 1024


def transform_tables(width):
    points = 2 * BLOCKS * width
    row = np.arange(width)
    forward = np.zeros((GROUPS, 2 * width, 2 * width), np.float64)
    for r in range(GROUPS):
        angle = 2.0 * np.pi * (np.outer(row, 16 * row + r) % points) / points
        cos, sin = np.cos(angle), np.sin(angle)
        forward[r] = np.block([[cos, -sin], [sin, cos]])
    scale = np.full((GROUPS, 1, 1), 2.0 / points)
    scale[0] = scale[-1] = 1.0 / points
    backward = np.swapaxes(forward, 1, 2) * scale
    return forward.astype(ml_dtypes.bfloat16), backward.astype(ml_dtypes.bfloat16)


def first_stage(b):
    e = [b[p] + b[p + 4] for p in range(4)]
    f = [b[p] - b[p + 4] for p in range(4)]
    e02, e13 = e[0] + e[2], e[1] + e[3]
    fd, fs = C2 * (f[1] - f[3]), C2 * (f[1] + f[3])
    d = [None] + [b[p] - b[8 - p] for p in (1, 2, 3)]
    g = [None] + [b[p] + b[8 - p] for p in (1, 2, 3)]
    d2, g2 = C2 * d[2], C2 * g[2]
    re1, re3 = C1 * d[1] + C3 * d[3], C3 * d[1] - C1 * d[3]
    im1, im3 = C3 * g[1] + C1 * g[3], C1 * g[1] - C3 * g[3]
    up, down = b[0] + d2, b[0] - d2
    bp, bm = b[4] + g2, b[4] - g2
    return [
        (e02 + e13, None),
        (up + re1, -(bp + im1)),
        (f[0] + fd, -(f[2] + fs)),
        (down + re3, bm - im3),
        (e[0] - e[2], e[3] - e[1]),
        (down - re3, -(bm + im3)),
        (f[0] - fd, f[2] - fs),
        (up - re1, bp - im1),
        (e02 - e13, None),
    ]


def last_stage(u):
    re = [pair[0] for pair in u]
    im = [pair[1] for pair in u]
    sum08, dif08 = re[0] + re[8], re[0] - re[8]
    r26, i26 = re[2] + re[6], im[2] - im[6]
    rd, sd = C2 * (re[2] - re[6]), C2 * (im[2] + im[6])
    top, low = sum08 + re[4], sum08 - re[4]
    dp, dm = dif08 + rd, dif08 - rd
    ip, im4 = sd + im[4], sd - im[4]
    even = [
        top + r26,
        dp - ip,
        low - i26,
        dm - im4,
        top - r26,
        dm + im4,
        low + i26,
        dp + ip,
    ]
    a1p, a1m = re[1] + re[7], re[1] - re[7]
    a3p, a3m = re[3] + re[5], re[3] - re[5]
    j1p, j1m = im[1] + im[7], im[1] - im[7]
    j3p, j3m = im[3] + im[5], im[3] - im[5]
    c1, c3 = C1 * a1m + C3 * a3m, C3 * a1m - C1 * a3m
    c2 = C2 * (a1p - a3p)
    s1, s3 = C3 * j1p + C1 * j3p, C1 * j1p - C3 * j3p
    s2 = C2 * (j1m + j3m)
    odd = [
        a1p + a3p,
        c1 - s1,
        c2 - s2,
        c3 - s3,
        j3m - j1m,
        -(c3 + s3),
        -(c2 + s2),
        -(c1 + s1),
    ]
    return [x + y for x, y in zip(even, odd)]


def rows_loop(rows, body):
    @pl.loop(0, rows // TILE)
    def _(step):
        body(pl.ds(pl.multiple_of(step * TILE, TILE), TILE))


def split_rows(load, mid, rows, width):
    def body(at):
        for r, pair in enumerate(first_stage([load(p, at) for p in range(BLOCKS)])):
            mid[r, at, :width] = pair[0].astype(jnp.bfloat16)
            if pair[1] is not None:
                mid[r, at, width:] = pair[1].astype(jnp.bfloat16)

    rows_loop(rows, body)


def spectrum(mid, table, r, width):
    if r in (0, GROUPS - 1):
        return jnp.dot(mid[r, :, :width], table[r, :width, :], preferred_element_type=jnp.float32)
    return jnp.dot(mid[r], table[r], preferred_element_type=jnp.float32)


def invert_group(product, table, r, width, wide):
    if r in (0, GROUPS - 1):
        wide[r, :, :width] = jnp.dot(product, table[r, :, :width], preferred_element_type=jnp.float32)
    else:
        wide[r] = jnp.dot(product, table[r], preferred_element_type=jnp.float32)


def merge_rows(wide, store, rows, width):
    def body(at):
        parts = []
        for r in range(GROUPS):
            im = None if r in (0, GROUPS - 1) else wide[r, at, width:]
            parts.append((wide[r, at, :width], im))
        for p, value in enumerate(last_stage(parts)):
            store(p, at, value)

    rows_loop(rows, body)


def gate_kernel(where, gate, upper, *outs):
    rows = outs[0].shape[0]
    for k, out in enumerate(outs):
        start = pl.multiple_of(lax.rem(where[0] + k, len(outs)) * rows, rows)
        product = gate[pl.ds(start, rows), :].astype(jnp.float32) * upper[pl.ds(start, rows), :].astype(jnp.float32)
        out[...] = product.astype(jnp.bfloat16)


def pick_kernel(where, whole, *outs):
    rows = outs[0].shape[0]
    for k, out in enumerate(outs):
        start = pl.multiple_of(lax.rem(where[0] + k, len(outs)) * rows, rows)
        out[...] = whole[pl.ds(start, rows), :]


def place_kernel(where, *refs):
    out = refs[-1]
    rows, count = refs[0].shape[0], len(refs) - 1
    for k, ref in enumerate(refs[:-1]):
        start = pl.multiple_of(lax.rem(where[0] + count - k, count) * rows, rows)
        out[pl.ds(start, rows), :] = ref[...]


def taps_kernel(taps, forward, out, mid):
    rows, width = (taps.shape[0], taps.shape[1] // BLOCKS)
    split_rows(lambda p, at: taps[at, p * width : (p + 1) * width], mid, rows, width)
    for r in range(GROUPS):
        out[r] = spectrum(mid, forward, r, width).astype(out.dtype)


def ordered(where, refs, held):
    span = refs[0].shape[1]
    for k, ref in enumerate(refs):
        start = pl.multiple_of(lax.rem(where[0] + len(refs) - k, len(refs)) * span, span)
        held[:, pl.ds(start, span)] = ref[...]


def block_of(held, width):
    return lambda p, at: held[at, p * width : (p + 1) * width].astype(jnp.float32)


def block_into(held, width):
    def store(p, at, value):
        held[at, p * width : (p + 1) * width] = value.astype(jnp.bfloat16)

    return store


def back_kernel(count, where, *refs):
    blocks, (taps_spec, forward, backward) = refs[:count], refs[count : count + 3]
    outs, grad_spec = refs[count + 3 : 2 * count + 3], refs[2 * count + 3]
    held, mid, wide = refs[2 * count + 4 :]
    rows, width = held.shape[0], held.shape[1] // BLOCKS
    ordered(where, blocks, held)
    split_rows(block_of(held, width), mid, rows, width)
    for r in range(GROUPS):
        grad = spectrum(mid, forward, r, width)
        grad_spec[r] = grad.astype(grad_spec.dtype)
        taps = taps_spec[r].astype(jnp.float32)
        gr, gi, hr, hi = grad[:, :width], grad[:, width:], taps[:, :width], taps[:, width:]
        product = jnp.concatenate([hr * gr + hi * gi, hr * gi - hi * gr], axis=1)
        invert_group(product.astype(jnp.bfloat16), backward, r, width, wide)
    merge_rows(wide, block_into(held, width), rows, width)
    span = outs[0].shape[1]
    for k, out in enumerate(outs):
        start = pl.multiple_of(lax.rem(where[0] + k, count) * span, span)
        out[...] = held[:, pl.ds(start, span)]


def cross_kernel(count, shares, where, *refs):
    blocks, (grad_spec, forward, backward) = refs[:count], refs[count : count + 3]
    outs = refs[count + 3 : count + 3 + shares]
    held, mid, wide = refs[count + 3 + shares :]
    rows, width = held.shape[0], held.shape[1] // BLOCKS
    ordered(where, blocks, held)
    split_rows(block_of(held, width), mid, rows, width)
    for r in range(GROUPS):
        signal = spectrum(mid, forward, r, width)
        grad = grad_spec[r].astype(jnp.float32)
        gr, gi, xr, xi = grad[:, :width], grad[:, width:], signal[:, :width], signal[:, width:]
        product = jnp.concatenate([gr * xr + gi * xi, gi * xr - gr * xi], axis=1)
        invert_group(product.astype(jnp.bfloat16), backward, r, width, wide)
    merge_rows(wide, block_into(held, width), rows, width)
    part = held.shape[1] // shares
    for k, out in enumerate(outs):
        start = pl.multiple_of(lax.rem(where[1] + k, shares) * part, part)
        out[...] = held[:, pl.ds(start, part)]


def sum_kernel(scale, *refs):
    total = refs[0][...].astype(jnp.float32)
    for ref in refs[1:-1]:
        total = total + ref[...].astype(jnp.float32)
    refs[-1][...] = total * scale


def call(kernel, operands, outs, scratch=(), scalar=True, flops=0):
    specs = [pl.BlockSpec(memory_space=pltpu.VMEM)] * len(operands)
    if scalar:
        specs[0] = pl.BlockSpec(memory_space=pltpu.SMEM)
    size = sum(math.prod(o.shape) * o.dtype.itemsize for o in list(operands) + list(outs))
    return pl.pallas_call(
        kernel,
        out_shape=list(outs),
        in_specs=specs,
        out_specs=[pl.BlockSpec(memory_space=pltpu.VMEM)] * len(outs),
        scratch_shapes=list(scratch),
        compiler_params=pltpu.CompilerParams(vmem_limit_bytes=LIMIT),
        cost_estimate=pl.CostEstimate(flops=flops, bytes_accessed=size, transcendentals=0),
    )(*operands)


def exchange(pieces, axis, size):
    moved = [pieces[0]]
    for k in range(1, size):
        pairs = [(i, (i + k) % size) for i in range(size)]
        moved.append(lax.ppermute(pieces[k], axis, pairs))
    return moved


def on_device(saved_input, out_gate, grad_out, long_filter):
    count, shares = lax.axis_size("ctx"), lax.axis_size("dp")
    channels, span = saved_input.shape[1:]
    rows, length = long_filter.shape
    width = length // BLOCKS
    where = jnp.stack([lax.axis_index("ctx"), lax.axis_index("dp")]).astype(jnp.int32)
    forward, backward = (jnp.asarray(t) for t in transform_tables(width))
    half, full = jnp.bfloat16, jnp.float32
    piece = jax.ShapeDtypeStruct((rows, span), half)
    spec = jax.ShapeDtypeStruct((GROUPS, rows, 2 * width), half)
    held = pltpu.VMEM((rows, length), half)
    mid = pltpu.VMEM((GROUPS, rows, 2 * width), half)
    wide = pltpu.VMEM((GROUPS, rows, 2 * width), full)
    work = 2 * GROUPS * rows * 4 * width * width

    grad_pieces = call(gate_kernel, [where, out_gate[0], grad_out[0]], [piece] * count)
    grad_blocks = exchange(grad_pieces, "ctx", count)
    input_pieces = call(pick_kernel, [where, saved_input[0]], [piece] * count)
    input_blocks = exchange(input_pieces, "ctx", count)
    (taps_spec,) = call(taps_kernel, [long_filter, forward], [spec], [mid], scalar=False, flops=work)
    *back, grad_spec = call(
        functools.partial(back_kernel, count),
        [where, *grad_blocks, taps_spec, forward, backward],
        [piece] * count + [spec],
        [held, mid, wide],
        flops=2 * work,
    )
    back_blocks = exchange(back, "ctx", count)
    share = jax.ShapeDtypeStruct((rows, length // shares), half)
    cross = call(
        functools.partial(cross_kernel, count, shares),
        [where, *input_blocks, grad_spec, forward, backward],
        [share] * shares,
        [held, mid, wide],
        flops=2 * work,
    )
    cross_blocks = exchange(cross, "dp", shares)
    scale = 1.0 / math.sqrt(shares * length)
    (grad_filter,) = call(
        functools.partial(sum_kernel, scale),
        cross_blocks,
        [jax.ShapeDtypeStruct((rows, length // shares), full)],
        scalar=False,
    )
    (grad_input,) = call(place_kernel, [where, *back_blocks], [jax.ShapeDtypeStruct((channels, span), half)])
    return (grad_input[None], grad_filter)


def solution(mesh):
    in_specs = (P("dp", None, "ctx"), P("dp", None, "ctx"), P("dp", None, "ctx"), P("ctx", None))
    out_specs = (P("dp", None, "ctx"), P("ctx", "dp"))
    return jax.shard_map(
        on_device, mesh=mesh, in_specs=in_specs, out_specs=out_specs, check_vma=False
    )
```

```python
import functools
import math

import jax
import jax.numpy as jnp
import ml_dtypes
import numpy as np
from jax import lax
from jax.experimental import pallas as pl
from jax.experimental.pallas import tpu as pltpu
from jax.sharding import PartitionSpec as P

BLOCKS = 8
GROUPS = 9
TILE = 16
C1 = math.cos(math.pi / 8)
C2 = math.cos(math.pi / 4)
C3 = math.cos(3 * math.pi / 8)
LIMIT = 56 * 1024 * 1024


def transform_tables(width):
    points = 2 * BLOCKS * width
    row = np.arange(width)
    forward = np.zeros((GROUPS, 2 * width, 2 * width), np.float64)
    for r in range(GROUPS):
        angle = 2.0 * np.pi * (np.outer(row, 16 * row + r) % points) / points
        cos, sin = np.cos(angle), np.sin(angle)
        forward[r] = np.block([[cos, -sin], [sin, cos]])
    scale = np.full((GROUPS, 1, 1), 2.0 / points)
    scale[0] = scale[-1] = 1.0 / points
    backward = np.swapaxes(forward, 1, 2) * scale
    return forward.astype(ml_dtypes.bfloat16), backward.astype(ml_dtypes.bfloat16)


def first_stage(b):
    e = [b[p] + b[p + 4] for p in range(4)]
    f = [b[p] - b[p + 4] for p in range(4)]
    e02, e13 = e[0] + e[2], e[1] + e[3]
    fd, fs = C2 * (f[1] - f[3]), C2 * (f[1] + f[3])
    d = [None] + [b[p] - b[8 - p] for p in (1, 2, 3)]
    g = [None] + [b[p] + b[8 - p] for p in (1, 2, 3)]
    d2, g2 = C2 * d[2], C2 * g[2]
    re1, re3 = C1 * d[1] + C3 * d[3], C3 * d[1] - C1 * d[3]
    im1, im3 = C3 * g[1] + C1 * g[3], C1 * g[1] - C3 * g[3]
    up, down = b[0] + d2, b[0] - d2
    bp, bm = b[4] + g2, b[4] - g2
    return [
        (e02 + e13, None),
        (up + re1, -(bp + im1)),
        (f[0] + fd, -(f[2] + fs)),
        (down + re3, bm - im3),
        (e[0] - e[2], e[3] - e[1]),
        (down - re3, -(bm + im3)),
        (f[0] - fd, f[2] - fs),
        (up - re1, bp - im1),
        (e02 - e13, None),
    ]


def last_stage(u):
    re = [pair[0] for pair in u]
    im = [pair[1] for pair in u]
    sum08, dif08 = re[0] + re[8], re[0] - re[8]
    r26, i26 = re[2] + re[6], im[2] - im[6]
    rd, sd = C2 * (re[2] - re[6]), C2 * (im[2] + im[6])
    top, low = sum08 + re[4], sum08 - re[4]
    dp, dm = dif08 + rd, dif08 - rd
    ip, im4 = sd + im[4], sd - im[4]
    even = [
        top + r26,
        dp - ip,
        low - i26,
        dm - im4,
        top - r26,
        dm + im4,
        low + i26,
        dp + ip,
    ]
    a1p, a1m = re[1] + re[7], re[1] - re[7]
    a3p, a3m = re[3] + re[5], re[3] - re[5]
    j1p, j1m = im[1] + im[7], im[1] - im[7]
    j3p, j3m = im[3] + im[5], im[3] - im[5]
    c1, c3 = C1 * a1m + C3 * a3m, C3 * a1m - C1 * a3m
    c2 = C2 * (a1p - a3p)
    s1, s3 = C3 * j1p + C1 * j3p, C1 * j1p - C3 * j3p
    s2 = C2 * (j1m + j3m)
    odd = [
        a1p + a3p,
        c1 - s1,
        c2 - s2,
        c3 - s3,
        j3m - j1m,
        -(c3 + s3),
        -(c2 + s2),
        -(c1 + s1),
    ]
    return [x + y for x, y in zip(even, odd)]


def rows_loop(rows, body):
    @pl.loop(0, rows // TILE)
    def _(step):
        body(pl.ds(pl.multiple_of(step * TILE, TILE), TILE))


def split_rows(load, mid, rows, width):
    def body(at):
        for r, pair in enumerate(first_stage([load(p, at) for p in range(BLOCKS)])):
            mid[r, at, :width] = pair[0].astype(jnp.bfloat16)
            if pair[1] is not None:
                mid[r, at, width:] = pair[1].astype(jnp.bfloat16)

    rows_loop(rows, body)


def spectrum(mid, table, r, width):
    if r in (0, GROUPS - 1):
        return jnp.dot(mid[r, :, :width], table[r, :width, :], preferred_element_type=jnp.float32)
    return jnp.dot(mid[r], table[r], preferred_element_type=jnp.float32)


def invert_group(product, table, r, width, wide):
    if r in (0, GROUPS - 1):
        wide[r, :, :width] = jnp.dot(product, table[r, :, :width], preferred_element_type=jnp.float32)
    else:
        wide[r] = jnp.dot(product, table[r], preferred_element_type=jnp.float32)


def merge_rows(wide, store, rows, width):
    def body(at):
        parts = []
        for r in range(GROUPS):
            im = None if r in (0, GROUPS - 1) else wide[r, at, width:]
            parts.append((wide[r, at, :width], im))
        for p, value in enumerate(last_stage(parts)):
            store(p, at, value)

    rows_loop(rows, body)


def gate_kernel(gate, upper, out):
    out[...] = (gate[...].astype(jnp.float32) * upper[...].astype(jnp.float32)).astype(jnp.bfloat16)


def taps_kernel(taps, forward, out, mid):
    rows, width = (taps.shape[0], taps.shape[1] // BLOCKS)
    split_rows(lambda p, at: taps[at, p * width : (p + 1) * width], mid, rows, width)
    for r in range(GROUPS):
        out[r] = spectrum(mid, forward, r, width).astype(out.dtype)


def ordered(blocks, held):
    span = blocks.shape[2]
    for p in range(blocks.shape[0]):
        held[:, p * span : (p + 1) * span] = blocks[p]


def block_of(held, width):
    return lambda p, at: held[at, p * width : (p + 1) * width].astype(jnp.float32)


def block_into(held, width):
    def store(p, at, value):
        held[at, p * width : (p + 1) * width] = value.astype(jnp.bfloat16)

    return store


def back_kernel(blocks, taps_spec, forward, backward, out, grad_spec, held, mid, wide):
    rows, width = held.shape[0], held.shape[1] // BLOCKS
    ordered(blocks, held)
    split_rows(block_of(held, width), mid, rows, width)
    for r in range(GROUPS):
        grad = spectrum(mid, forward, r, width)
        grad_spec[r] = grad.astype(grad_spec.dtype)
        taps = taps_spec[r].astype(jnp.float32)
        gr, gi, hr, hi = grad[:, :width], grad[:, width:], taps[:, :width], taps[:, width:]
        product = jnp.concatenate([hr * gr + hi * gi, hr * gi - hi * gr], axis=1)
        invert_group(product.astype(jnp.bfloat16), backward, r, width, wide)
    merge_rows(wide, block_into(held, width), rows, width)
    span = out.shape[2]
    for p in range(out.shape[0]):
        out[p] = held[:, p * span : (p + 1) * span]


def cross_kernel(where, blocks, grad_spec, forward, backward, *refs):
    outs, (held, mid, wide) = refs[:-3], refs[-3:]
    rows, width = held.shape[0], held.shape[1] // BLOCKS
    ordered(blocks, held)
    split_rows(block_of(held, width), mid, rows, width)
    for r in range(GROUPS):
        signal = spectrum(mid, forward, r, width)
        grad = grad_spec[r].astype(jnp.float32)
        gr, gi, xr, xi = grad[:, :width], grad[:, width:], signal[:, :width], signal[:, width:]
        product = jnp.concatenate([gr * xr + gi * xi, gi * xr - gr * xi], axis=1)
        invert_group(product.astype(jnp.bfloat16), backward, r, width, wide)
    merge_rows(wide, block_into(held, width), rows, width)
    part = held.shape[1] // len(outs)
    for k, out in enumerate(outs):
        start = pl.multiple_of(lax.rem(where[0] + k, len(outs)) * part, part)
        out[...] = held[:, pl.ds(start, part)]


def sum_kernel(scale, *refs):
    total = refs[0][...].astype(jnp.float32)
    for ref in refs[1:-1]:
        total = total + ref[...].astype(jnp.float32)
    refs[-1][...] = total * scale


def call(kernel, operands, outs, scratch=(), scalar=True, flops=0):
    specs = [pl.BlockSpec(memory_space=pltpu.VMEM)] * len(operands)
    if scalar:
        specs[0] = pl.BlockSpec(memory_space=pltpu.SMEM)
    size = sum(math.prod(o.shape) * o.dtype.itemsize for o in list(operands) + list(outs))
    return pl.pallas_call(
        kernel,
        out_shape=list(outs),
        in_specs=specs,
        out_specs=[pl.BlockSpec(memory_space=pltpu.VMEM)] * len(outs),
        scratch_shapes=list(scratch),
        compiler_params=pltpu.CompilerParams(vmem_limit_bytes=LIMIT),
        cost_estimate=pl.CostEstimate(flops=flops, bytes_accessed=size, transcendentals=0),
    )(*operands)


def exchange(pieces, axis, size):
    moved = [pieces[0]]
    for k in range(1, size):
        pairs = [(i, (i + k) % size) for i in range(size)]
        moved.append(lax.ppermute(pieces[k], axis, pairs))
    return moved


def swap(blocks):
    return lax.all_to_all(blocks, "ctx", split_axis=0, concat_axis=0, tiled=True)


def on_device(saved_input, out_gate, grad_out, long_filter):
    count, shares = lax.axis_size("ctx"), lax.axis_size("dp")
    channels, span = saved_input.shape[1:]
    rows, length = long_filter.shape
    width = length // BLOCKS
    where = lax.axis_index("dp").astype(jnp.int32)[None]
    forward, backward = (jnp.asarray(t) for t in transform_tables(width))
    half, full = jnp.bfloat16, jnp.float32
    blocks = jax.ShapeDtypeStruct((count, rows, span), half)
    spec = jax.ShapeDtypeStruct((GROUPS, rows, 2 * width), half)
    held = pltpu.VMEM((rows, length), half)
    mid = pltpu.VMEM((GROUPS, rows, 2 * width), half)
    wide = pltpu.VMEM((GROUPS, rows, 2 * width), full)
    work = 2 * GROUPS * rows * 4 * width * width

    saved_input, out_gate, grad_out = (x.reshape(blocks.shape) for x in (saved_input, out_gate, grad_out))
    (conv_grad,) = call(gate_kernel, [out_gate, grad_out], [blocks], scalar=False)
    grad_blocks = swap(conv_grad)
    input_blocks = swap(saved_input)
    (taps_spec,) = call(taps_kernel, [long_filter, forward], [spec], [mid], scalar=False, flops=work)
    back, grad_spec = call(
        back_kernel,
        [grad_blocks, taps_spec, forward, backward],
        [blocks, spec],
        [held, mid, wide],
        scalar=False,
        flops=2 * work,
    )
    grad_input = swap(back)
    share = jax.ShapeDtypeStruct((rows, length // shares), half)
    cross = call(
        cross_kernel,
        [where, input_blocks, grad_spec, forward, backward],
        [share] * shares,
        [held, mid, wide],
        flops=2 * work,
    )
    cross_blocks = exchange(cross, "dp", shares)
    scale = 1.0 / math.sqrt(shares * length)
    (grad_filter,) = call(
        functools.partial(sum_kernel, scale),
        cross_blocks,
        [jax.ShapeDtypeStruct((rows, length // shares), full)],
        scalar=False,
    )
    return (grad_input.reshape(1, channels, span), grad_filter)


def solution(mesh):
    in_specs = (P("dp", None, "ctx"), P("dp", None, "ctx"), P("dp", None, "ctx"), P("ctx", None))
    out_specs = (P("dp", None, "ctx"), P("ctx", "dp"))
    return jax.shard_map(
        on_device, mesh=mesh, in_specs=in_specs, out_specs=out_specs, check_vma=False
    )
```

```python
import functools
import math

import jax
import jax.numpy as jnp
import ml_dtypes
import numpy as np
from jax import lax
from jax.experimental import pallas as pl
from jax.experimental.pallas import tpu as pltpu
from jax.sharding import PartitionSpec as P

BLOCKS = 8
GROUPS = 9
TILE = 16
C1 = math.cos(math.pi / 8)
C2 = math.cos(math.pi / 4)
C3 = math.cos(3 * math.pi / 8)
LIMIT = 56 * 1024 * 1024


def transform_tables(width):
    points = 2 * BLOCKS * width
    row = np.arange(width)
    forward = np.zeros((GROUPS, 2 * width, 2 * width), np.float64)
    for r in range(GROUPS):
        angle = 2.0 * np.pi * (np.outer(row, 16 * row + r) % points) / points
        cos, sin = np.cos(angle), np.sin(angle)
        forward[r] = np.block([[cos, -sin], [sin, cos]])
    scale = np.full((GROUPS, 1, 1), 2.0 / points)
    scale[0] = scale[-1] = 1.0 / points
    backward = np.swapaxes(forward, 1, 2) * scale
    return forward.astype(ml_dtypes.bfloat16), backward.astype(ml_dtypes.bfloat16)


def first_stage(b):
    e = [b[p] + b[p + 4] for p in range(4)]
    f = [b[p] - b[p + 4] for p in range(4)]
    e02, e13 = e[0] + e[2], e[1] + e[3]
    fd, fs = C2 * (f[1] - f[3]), C2 * (f[1] + f[3])
    d = [None] + [b[p] - b[8 - p] for p in (1, 2, 3)]
    g = [None] + [b[p] + b[8 - p] for p in (1, 2, 3)]
    d2, g2 = C2 * d[2], C2 * g[2]
    re1, re3 = C1 * d[1] + C3 * d[3], C3 * d[1] - C1 * d[3]
    im1, im3 = C3 * g[1] + C1 * g[3], C1 * g[1] - C3 * g[3]
    up, down = b[0] + d2, b[0] - d2
    bp, bm = b[4] + g2, b[4] - g2
    return [
        (e02 + e13, None),
        (up + re1, -(bp + im1)),
        (f[0] + fd, -(f[2] + fs)),
        (down + re3, bm - im3),
        (e[0] - e[2], e[3] - e[1]),
        (down - re3, -(bm + im3)),
        (f[0] - fd, f[2] - fs),
        (up - re1, bp - im1),
        (e02 - e13, None),
    ]


def last_stage(u):
    re = [pair[0] for pair in u]
    im = [pair[1] for pair in u]
    sum08, dif08 = re[0] + re[8], re[0] - re[8]
    r26, i26 = re[2] + re[6], im[2] - im[6]
    rd, sd = C2 * (re[2] - re[6]), C2 * (im[2] + im[6])
    top, low = sum08 + re[4], sum08 - re[4]
    dp, dm = dif08 + rd, dif08 - rd
    ip, im4 = sd + im[4], sd - im[4]
    even = [
        top + r26,
        dp - ip,
        low - i26,
        dm - im4,
        top - r26,
        dm + im4,
        low + i26,
        dp + ip,
    ]
    a1p, a1m = re[1] + re[7], re[1] - re[7]
    a3p, a3m = re[3] + re[5], re[3] - re[5]
    j1p, j1m = im[1] + im[7], im[1] - im[7]
    j3p, j3m = im[3] + im[5], im[3] - im[5]
    c1, c3 = C1 * a1m + C3 * a3m, C3 * a1m - C1 * a3m
    c2 = C2 * (a1p - a3p)
    s1, s3 = C3 * j1p + C1 * j3p, C1 * j1p - C3 * j3p
    s2 = C2 * (j1m + j3m)
    odd = [
        a1p + a3p,
        c1 - s1,
        c2 - s2,
        c3 - s3,
        j3m - j1m,
        -(c3 + s3),
        -(c2 + s2),
        -(c1 + s1),
    ]
    return [x + y for x, y in zip(even, odd)]


def rows_loop(rows, body):
    @pl.loop(0, rows // TILE)
    def _(step):
        body(pl.ds(pl.multiple_of(step * TILE, TILE), TILE))


def split_rows(load, mid, rows, width):
    def body(at):
        for r, pair in enumerate(first_stage([load(p, at) for p in range(BLOCKS)])):
            mid[r, at, :width] = pair[0].astype(jnp.bfloat16)
            if pair[1] is not None:
                mid[r, at, width:] = pair[1].astype(jnp.bfloat16)

    rows_loop(rows, body)


def spectrum(mid, table, r, width):
    if r in (0, GROUPS - 1):
        return jnp.dot(mid[r, :, :width], table[r, :width, :], preferred_element_type=jnp.float32)
    return jnp.dot(mid[r], table[r], preferred_element_type=jnp.float32)


def invert_group(product, table, r, width, wide):
    if r in (0, GROUPS - 1):
        wide[r, :, :width] = jnp.dot(product, table[r, :, :width], preferred_element_type=jnp.float32)
    else:
        wide[r] = jnp.dot(product, table[r], preferred_element_type=jnp.float32)


def merge_rows(wide, store, rows, width):
    def body(at):
        parts = []
        for r in range(GROUPS):
            im = None if r in (0, GROUPS - 1) else wide[r, at, width:]
            parts.append((wide[r, at, :width], im))
        for p, value in enumerate(last_stage(parts)):
            store(p, at, value)

    rows_loop(rows, body)


def piece_at(ref, where, k, rows):
    start = pl.multiple_of(lax.bitwise_xor(where[0], k) * rows, rows)
    return ref.at[pl.ds(start, rows), :]


def gate_kernel(order, where, gate, upper, *refs):
    outs, (left, right, product, sems, out_sems) = refs[: len(order)], refs[len(order) :]
    rows = outs[0].shape[0]
    loads = []
    for i, k in enumerate(order):
        pair = (
            pltpu.make_async_copy(piece_at(gate, where, k, rows), left.at[i], sems.at[0, i]),
            pltpu.make_async_copy(piece_at(upper, where, k, rows), right.at[i], sems.at[1, i]),
        )
        for copy in pair:
            copy.start()
        loads.append(pair)
    stores = []
    for i, out in enumerate(outs):
        for copy in loads[i]:
            copy.wait()
        product[i] = (left[i].astype(jnp.float32) * right[i].astype(jnp.float32)).astype(jnp.bfloat16)
        stores.append(pltpu.make_async_copy(product.at[i], out, out_sems.at[i]))
        stores[-1].start()
    for copy in stores:
        copy.wait()


def pick_kernel(order, where, whole, *refs):
    outs, sems = refs[:-1], refs[-1]
    copies = []
    for i, k in enumerate(order):
        copies.append(pltpu.make_async_copy(piece_at(whole, where, k, outs[0].shape[0]), outs[i], sems.at[i]))
        copies[-1].start()
    for copy in copies:
        copy.wait()


def place_kernel(order, where, *refs):
    pieces, whole, sems = refs[: len(order)], refs[-2], refs[-1]
    copies = []
    for i, k in enumerate(order):
        copies.append(pltpu.make_async_copy(pieces[i], piece_at(whole, where, k, pieces[i].shape[0]), sems.at[i]))
        copies[-1].start()
    for copy in copies:
        copy.wait()


def taps_kernel(taps, forward, out, mid):
    rows, width = (taps.shape[0], taps.shape[1] // BLOCKS)
    split_rows(lambda p, at: taps[at, p * width : (p + 1) * width], mid, rows, width)
    for r in range(GROUPS):
        out[r] = spectrum(mid, forward, r, width).astype(out.dtype)


def ordered(order, where, refs, held):
    span = refs[0].shape[1]
    for k, ref in zip(order, refs):
        start = pl.multiple_of(lax.bitwise_xor(where[0], k) * span, span)
        held[:, pl.ds(start, span)] = ref[...]


def block_of(held, width):
    return lambda p, at: held[at, p * width : (p + 1) * width].astype(jnp.float32)


def block_into(held, width):
    def store(p, at, value):
        held[at, p * width : (p + 1) * width] = value.astype(jnp.bfloat16)

    return store


def back_kernel(order, where, *refs):
    blocks, refs = refs[: len(order)], refs[len(order) :]
    taps_spec, forward, backward, *outs, grad_spec, held, mid, wide = refs
    rows, width = held.shape[0], held.shape[1] // BLOCKS
    ordered(order, where, blocks, held)
    split_rows(block_of(held, width), mid, rows, width)
    for r in range(GROUPS):
        grad = spectrum(mid, forward, r, width)
        grad_spec[r] = grad.astype(grad_spec.dtype)
        taps = taps_spec[r].astype(jnp.float32)
        gr, gi, hr, hi = grad[:, :width], grad[:, width:], taps[:, :width], taps[:, width:]
        product = jnp.concatenate([hr * gr + hi * gi, hr * gi - hi * gr], axis=1)
        invert_group(product.astype(jnp.bfloat16), backward, r, width, wide)
    merge_rows(wide, block_into(held, width), rows, width)
    span = outs[0].shape[1]
    for k, out in zip(order, outs):
        start = pl.multiple_of(lax.bitwise_xor(where[0], k) * span, span)
        out[...] = held[:, pl.ds(start, span)]


def cross_kernel(order, where, *refs):
    blocks, refs = refs[: len(order)], refs[len(order) :]
    grad_spec, forward, backward, *outs, held, mid, wide = refs
    rows, width = held.shape[0], held.shape[1] // BLOCKS
    ordered(order, where, blocks, held)
    split_rows(block_of(held, width), mid, rows, width)
    for r in range(GROUPS):
        signal = spectrum(mid, forward, r, width)
        grad = grad_spec[r].astype(jnp.float32)
        gr, gi, xr, xi = grad[:, :width], grad[:, width:], signal[:, :width], signal[:, width:]
        product = jnp.concatenate([gr * xr + gi * xi, gi * xr - gr * xi], axis=1)
        invert_group(product.astype(jnp.bfloat16), backward, r, width, wide)
    merge_rows(wide, block_into(held, width), rows, width)
    part = held.shape[1] // len(outs)
    for k, out in enumerate(outs):
        start = pl.multiple_of(lax.bitwise_xor(where[1], k) * part, part)
        out[...] = held[:, pl.ds(start, part)]


def sum_kernel(scale, *refs):
    total = refs[0][...].astype(jnp.float32)
    for ref in refs[1:-1]:
        total = total + ref[...].astype(jnp.float32)
    refs[-1][...] = total * scale


def call(kernel, operands, outs, scratch=(), scalar=True, flops=0, stream=False):
    space = pl.ANY if stream else pltpu.VMEM
    specs = [pl.BlockSpec(memory_space=space)] * len(operands)
    if scalar:
        specs[0] = pl.BlockSpec(memory_space=pltpu.SMEM)
    size = sum(math.prod(o.shape) * o.dtype.itemsize for o in list(operands) + list(outs))
    return pl.pallas_call(
        kernel,
        out_shape=list(outs),
        in_specs=specs,
        out_specs=[pl.BlockSpec(memory_space=space)] * len(outs),
        scratch_shapes=list(scratch),
        compiler_params=pltpu.CompilerParams(vmem_limit_bytes=LIMIT),
        cost_estimate=pl.CostEstimate(flops=flops, bytes_accessed=size, transcendentals=0),
    )(*operands)


def far_first(size):
    half = size // 2
    return [k for pair in zip(range(half, size), [*range(1, half), 0]) for k in pair]


def exchange(pieces, order, axis, size):
    moved = []
    for k, piece in zip(order, pieces):
        moved.append(lax.ppermute(piece, axis, [(i, i ^ k) for i in range(size)]) if k else piece)
    return moved


def on_device(saved_input, out_gate, grad_out, long_filter):
    count, shares = lax.axis_size("ctx"), lax.axis_size("dp")
    channels, span = saved_input.shape[1:]
    rows, length = long_filter.shape
    width = length // BLOCKS
    order = far_first(count)
    where = jnp.stack([lax.axis_index("ctx"), lax.axis_index("dp")]).astype(jnp.int32)
    forward, backward = (jnp.asarray(t) for t in transform_tables(width))
    half, full = jnp.bfloat16, jnp.float32
    piece = jax.ShapeDtypeStruct((rows, span), half)
    blocks = jax.ShapeDtypeStruct((count, rows, span), half)
    spec = jax.ShapeDtypeStruct((GROUPS, rows, 2 * width), half)
    held = pltpu.VMEM((rows, length), half)
    mid = pltpu.VMEM((GROUPS, rows, 2 * width), half)
    wide = pltpu.VMEM((GROUPS, rows, 2 * width), full)
    slots = pltpu.VMEM(blocks.shape, half)
    sems = pltpu.SemaphoreType.DMA
    work = 2 * GROUPS * rows * 4 * width * width

    grad_pieces = call(
        functools.partial(gate_kernel, order),
        [where, out_gate[0], grad_out[0]],
        [piece] * count,
        [slots, slots, slots, sems((2, count)), sems((count,))],
        stream=True,
    )
    grad_blocks = exchange(grad_pieces, order, "ctx", count)
    input_pieces = call(
        functools.partial(pick_kernel, order),
        [where, saved_input[0]],
        [piece] * count,
        [sems((count,))],
        stream=True,
    )
    input_blocks = exchange(input_pieces, order, "ctx", count)
    (taps_spec,) = call(taps_kernel, [long_filter, forward], [spec], [mid], scalar=False, flops=work)
    *back, grad_spec = call(
        functools.partial(back_kernel, order),
        [where, *grad_blocks, taps_spec, forward, backward],
        [piece] * count + [spec],
        [held, mid, wide],
        flops=2 * work,
    )
    back_blocks = exchange(back, order, "ctx", count)
    share = jax.ShapeDtypeStruct((rows, length // shares), half)
    cross = call(
        functools.partial(cross_kernel, order),
        [where, *input_blocks, grad_spec, forward, backward],
        [share] * shares,
        [held, mid, wide],
        flops=2 * work,
    )
    cross_blocks = exchange(cross, range(shares), "dp", shares)
    scale = 1.0 / math.sqrt(shares * length)
    (grad_filter,) = call(
        functools.partial(sum_kernel, scale),
        cross_blocks,
        [jax.ShapeDtypeStruct((rows, length // shares), full)],
        scalar=False,
    )
    (grad_input,) = call(
        functools.partial(place_kernel, order),
        [where, *back_blocks],
        [jax.ShapeDtypeStruct((channels, span), half)],
        [sems((count,))],
        stream=True,
    )
    return (grad_input[None], grad_filter)


def solution(mesh):
    in_specs = (P("dp", None, "ctx"), P("dp", None, "ctx"), P("dp", None, "ctx"), P("ctx", None))
    out_specs = (P("dp", None, "ctx"), P("ctx", "dp"))
    return jax.shard_map(
        on_device, mesh=mesh, in_specs=in_specs, out_specs=out_specs, check_vma=False
    )
```

```python
import functools
import math

import jax
import jax.numpy as jnp
import ml_dtypes
import numpy as np
from jax import lax
from jax.experimental import pallas as pl
from jax.experimental.pallas import tpu as pltpu
from jax.sharding import PartitionSpec as P

BLOCKS = 8
GROUPS = 9
TILE = 16
C1 = math.cos(math.pi / 8)
C2 = math.cos(math.pi / 4)
C3 = math.cos(3 * math.pi / 8)
LIMIT = 56 * 1024 * 1024


def transform_tables(width):
    points = 2 * BLOCKS * width
    row = np.arange(width)
    forward = np.zeros((GROUPS, 2 * width, 2 * width), np.float64)
    for r in range(GROUPS):
        angle = 2.0 * np.pi * (np.outer(row, 16 * row + r) % points) / points
        cos, sin = np.cos(angle), np.sin(angle)
        forward[r] = np.block([[cos, -sin], [sin, cos]])
    scale = np.full((GROUPS, 1, 1), 2.0 / points)
    scale[0] = scale[-1] = 1.0 / points
    backward = np.swapaxes(forward, 1, 2) * scale
    return forward.astype(ml_dtypes.bfloat16), backward.astype(ml_dtypes.bfloat16)


def first_stage(b):
    e = [b[p] + b[p + 4] for p in range(4)]
    f = [b[p] - b[p + 4] for p in range(4)]
    e02, e13 = e[0] + e[2], e[1] + e[3]
    fd, fs = C2 * (f[1] - f[3]), C2 * (f[1] + f[3])
    d = [None] + [b[p] - b[8 - p] for p in (1, 2, 3)]
    g = [None] + [b[p] + b[8 - p] for p in (1, 2, 3)]
    d2, g2 = C2 * d[2], C2 * g[2]
    re1, re3 = C1 * d[1] + C3 * d[3], C3 * d[1] - C1 * d[3]
    im1, im3 = C3 * g[1] + C1 * g[3], C1 * g[1] - C3 * g[3]
    up, down = b[0] + d2, b[0] - d2
    bp, bm = b[4] + g2, b[4] - g2
    return [
        (e02 + e13, None),
        (up + re1, -(bp + im1)),
        (f[0] + fd, -(f[2] + fs)),
        (down + re3, bm - im3),
        (e[0] - e[2], e[3] - e[1]),
        (down - re3, -(bm + im3)),
        (f[0] - fd, f[2] - fs),
        (up - re1, bp - im1),
        (e02 - e13, None),
    ]


def last_stage(u):
    re = [pair[0] for pair in u]
    im = [pair[1] for pair in u]
    sum08, dif08 = re[0] + re[8], re[0] - re[8]
    r26, i26 = re[2] + re[6], im[2] - im[6]
    rd, sd = C2 * (re[2] - re[6]), C2 * (im[2] + im[6])
    top, low = sum08 + re[4], sum08 - re[4]
    dp, dm = dif08 + rd, dif08 - rd
    ip, im4 = sd + im[4], sd - im[4]
    even = [
        top + r26,
        dp - ip,
        low - i26,
        dm - im4,
        top - r26,
        dm + im4,
        low + i26,
        dp + ip,
    ]
    a1p, a1m = re[1] + re[7], re[1] - re[7]
    a3p, a3m = re[3] + re[5], re[3] - re[5]
    j1p, j1m = im[1] + im[7], im[1] - im[7]
    j3p, j3m = im[3] + im[5], im[3] - im[5]
    c1, c3 = C1 * a1m + C3 * a3m, C3 * a1m - C1 * a3m
    c2 = C2 * (a1p - a3p)
    s1, s3 = C3 * j1p + C1 * j3p, C1 * j1p - C3 * j3p
    s2 = C2 * (j1m + j3m)
    odd = [
        a1p + a3p,
        c1 - s1,
        c2 - s2,
        c3 - s3,
        j3m - j1m,
        -(c3 + s3),
        -(c2 + s2),
        -(c1 + s1),
    ]
    return [x + y for x, y in zip(even, odd)]


def rows_loop(rows, body):
    @pl.loop(0, rows // TILE)
    def _(step):
        body(pl.ds(pl.multiple_of(step * TILE, TILE), TILE))


def split_rows(load, mid, rows, width):
    def body(at):
        for r, pair in enumerate(first_stage([load(p, at) for p in range(BLOCKS)])):
            mid[r, at, :width] = pair[0].astype(jnp.bfloat16)
            if pair[1] is not None:
                mid[r, at, width:] = pair[1].astype(jnp.bfloat16)

    rows_loop(rows, body)


def spectrum(mid, table, r, width):
    if r in (0, GROUPS - 1):
        return jnp.dot(mid[r, :, :width], table[r, :width, :], preferred_element_type=jnp.float32)
    return jnp.dot(mid[r], table[r], preferred_element_type=jnp.float32)


def invert_group(product, table, r, width, wide):
    if r in (0, GROUPS - 1):
        wide[r, :, :width] = jnp.dot(product, table[r, :, :width], preferred_element_type=jnp.float32)
    else:
        wide[r] = jnp.dot(product, table[r], preferred_element_type=jnp.float32)


def merge_rows(wide, store, rows, width):
    def body(at):
        parts = []
        for r in range(GROUPS):
            im = None if r in (0, GROUPS - 1) else wide[r, at, width:]
            parts.append((wide[r, at, :width], im))
        for p, value in enumerate(last_stage(parts)):
            store(p, at, value)

    rows_loop(rows, body)


def piece_at(ref, where, k, rows):
    start = pl.multiple_of(lax.bitwise_xor(where[0], k) * rows, rows)
    return ref.at[pl.ds(start, rows), :]


def gate_kernel(gate, upper, out):
    out[...] = (gate[...].astype(jnp.float32) * upper[...].astype(jnp.float32)).astype(jnp.bfloat16)


def pick_kernel(order, where, whole, *refs):
    outs, (slots, sems, out_sems) = refs[: len(order)], refs[len(order) :]
    rows = outs[0].shape[0]
    loads, stores = [], []
    for i, k in enumerate(order):
        start = pl.multiple_of(lax.bitwise_xor(where[0], k) * rows, rows)
        loads.append(pltpu.make_async_copy(whole.at[pl.ds(start, rows), :], slots.at[i], sems.at[i]))
        loads[-1].start()
    for i, out in enumerate(outs):
        loads[i].wait()
        stores.append(pltpu.make_async_copy(slots.at[i], out, out_sems.at[i]))
        stores[-1].start()
    for copy in stores:
        copy.wait()


def taps_kernel(taps, forward, out, mid):
    rows, width = (taps.shape[0], taps.shape[1] // BLOCKS)
    split_rows(lambda p, at: taps[at, p * width : (p + 1) * width], mid, rows, width)
    for r in range(GROUPS):
        out[r] = spectrum(mid, forward, r, width).astype(out.dtype)


def ordered(order, where, refs, held):
    span = refs[0].shape[1]
    for k, ref in zip(order, refs):
        start = pl.multiple_of(lax.bitwise_xor(where[0], k) * span, span)
        held[:, pl.ds(start, span)] = ref[...]


def block_of(held, width):
    return lambda p, at: held[at, p * width : (p + 1) * width].astype(jnp.float32)


def block_into(held, width):
    def store(p, at, value):
        held[at, p * width : (p + 1) * width] = value.astype(jnp.bfloat16)

    return store


def back_kernel(blocks, taps_spec, forward, backward, out, grad_spec, held, mid, wide):
    rows, width = held.shape[0], held.shape[1] // BLOCKS
    span = blocks.shape[2]
    for p in range(blocks.shape[0]):
        held[:, p * span : (p + 1) * span] = blocks[p]
    split_rows(block_of(held, width), mid, rows, width)
    for r in range(GROUPS):
        grad = spectrum(mid, forward, r, width)
        grad_spec[r] = grad.astype(grad_spec.dtype)
        taps = taps_spec[r].astype(jnp.float32)
        gr, gi, hr, hi = grad[:, :width], grad[:, width:], taps[:, :width], taps[:, width:]
        product = jnp.concatenate([hr * gr + hi * gi, hr * gi - hi * gr], axis=1)
        invert_group(product.astype(jnp.bfloat16), backward, r, width, wide)
    merge_rows(wide, block_into(held, width), rows, width)
    for p in range(out.shape[0]):
        out[p] = held[:, p * span : (p + 1) * span]


def cross_kernel(order, where, *refs):
    blocks, refs = refs[: len(order)], refs[len(order) :]
    grad_spec, forward, backward, *outs, held, mid, wide = refs
    rows, width = held.shape[0], held.shape[1] // BLOCKS
    ordered(order, where, blocks, held)
    split_rows(block_of(held, width), mid, rows, width)
    for r in range(GROUPS):
        signal = spectrum(mid, forward, r, width)
        grad = grad_spec[r].astype(jnp.float32)
        gr, gi, xr, xi = grad[:, :width], grad[:, width:], signal[:, :width], signal[:, width:]
        product = jnp.concatenate([gr * xr + gi * xi, gi * xr - gr * xi], axis=1)
        invert_group(product.astype(jnp.bfloat16), backward, r, width, wide)
    merge_rows(wide, block_into(held, width), rows, width)
    part = held.shape[1] // len(outs)
    for k, out in enumerate(outs):
        start = pl.multiple_of(lax.bitwise_xor(where[1], k) * part, part)
        out[...] = held[:, pl.ds(start, part)]


def sum_kernel(scale, *refs):
    total = refs[0][...].astype(jnp.float32)
    for ref in refs[1:-1]:
        total = total + ref[...].astype(jnp.float32)
    refs[-1][...] = total * scale


def call(kernel, operands, outs, scratch=(), scalar=True, flops=0, stream=False):
    space = pl.ANY if stream else pltpu.VMEM
    specs = [pl.BlockSpec(memory_space=space)] * len(operands)
    if scalar:
        specs[0] = pl.BlockSpec(memory_space=pltpu.SMEM)
    size = sum(math.prod(o.shape) * o.dtype.itemsize for o in list(operands) + list(outs))
    return pl.pallas_call(
        kernel,
        out_shape=list(outs),
        in_specs=specs,
        out_specs=[pl.BlockSpec(memory_space=space)] * len(outs),
        scratch_shapes=list(scratch),
        compiler_params=pltpu.CompilerParams(vmem_limit_bytes=LIMIT),
        cost_estimate=pl.CostEstimate(flops=flops, bytes_accessed=size, transcendentals=0),
    )(*operands)


def far_first(size):
    half = size // 2
    return [k for pair in zip(range(half, size), [*range(1, half), 0]) for k in pair]


def exchange(pieces, order, axis, size):
    moved = []
    for k, piece in zip(order, pieces):
        moved.append(lax.ppermute(piece, axis, [(i, i ^ k) for i in range(size)]) if k else piece)
    return moved


def swap(blocks):
    return lax.all_to_all(blocks, "ctx", split_axis=0, concat_axis=0, tiled=True)


def on_device(saved_input, out_gate, grad_out, long_filter):
    count, shares = lax.axis_size("ctx"), lax.axis_size("dp")
    channels, span = saved_input.shape[1:]
    rows, length = long_filter.shape
    width = length // BLOCKS
    order = far_first(count)
    where = jnp.stack([lax.axis_index("ctx"), lax.axis_index("dp")]).astype(jnp.int32)
    forward, backward = (jnp.asarray(t) for t in transform_tables(width))
    half, full = jnp.bfloat16, jnp.float32
    piece = jax.ShapeDtypeStruct((rows, span), half)
    blocks = jax.ShapeDtypeStruct((count, rows, span), half)
    spec = jax.ShapeDtypeStruct((GROUPS, rows, 2 * width), half)
    held = pltpu.VMEM((rows, length), half)
    mid = pltpu.VMEM((GROUPS, rows, 2 * width), half)
    wide = pltpu.VMEM((GROUPS, rows, 2 * width), full)
    sems = pltpu.SemaphoreType.DMA
    work = 2 * GROUPS * rows * 4 * width * width

    input_pieces = call(
        functools.partial(pick_kernel, order),
        [where, saved_input[0]],
        [piece] * count,
        [pltpu.VMEM(blocks.shape, half), sems((count,)), sems((count,))],
        stream=True,
    )
    input_blocks = exchange(input_pieces, order, "ctx", count)
    out_gate, grad_out = (x.reshape(blocks.shape) for x in (out_gate, grad_out))
    (conv_grad,) = call(gate_kernel, [out_gate, grad_out], [blocks], scalar=False)
    grad_blocks = swap(conv_grad)
    (taps_spec,) = call(taps_kernel, [long_filter, forward], [spec], [mid], scalar=False, flops=work)
    back, grad_spec = call(
        back_kernel,
        [grad_blocks, taps_spec, forward, backward],
        [blocks, spec],
        [held, mid, wide],
        scalar=False,
        flops=2 * work,
    )
    grad_input = swap(back)
    share = jax.ShapeDtypeStruct((rows, length // shares), half)
    cross = call(
        functools.partial(cross_kernel, order),
        [where, *input_blocks, grad_spec, forward, backward],
        [share] * shares,
        [held, mid, wide],
        flops=2 * work,
    )
    cross_blocks = exchange(cross, range(shares), "dp", shares)
    scale = 1.0 / math.sqrt(shares * length)
    (grad_filter,) = call(
        functools.partial(sum_kernel, scale),
        cross_blocks,
        [jax.ShapeDtypeStruct((rows, length // shares), full)],
        scalar=False,
    )
    return (grad_input.reshape(1, channels, span), grad_filter)


def solution(mesh):
    in_specs = (P("dp", None, "ctx"), P("dp", None, "ctx"), P("dp", None, "ctx"), P("ctx", None))
    out_specs = (P("dp", None, "ctx"), P("ctx", "dp"))
    return jax.shard_map(
        on_device, mesh=mesh, in_specs=in_specs, out_specs=out_specs, check_vma=False
    )
```

```python
import functools
import math

import jax
import jax.numpy as jnp
import ml_dtypes
import numpy as np
from jax import lax
from jax.experimental import pallas as pl
from jax.experimental.pallas import tpu as pltpu
from jax.sharding import PartitionSpec as P

BLOCKS = 8
GROUPS = 9
TILE = 16
C1 = math.cos(math.pi / 8)
C2 = math.cos(math.pi / 4)
C3 = math.cos(3 * math.pi / 8)
LIMIT = 56 * 1024 * 1024


def transform_tables(width):
    points = 2 * BLOCKS * width
    row = np.arange(width)
    forward = np.zeros((GROUPS, 2 * width, 2 * width), np.float64)
    for r in range(GROUPS):
        angle = 2.0 * np.pi * (np.outer(row, 16 * row + r) % points) / points
        cos, sin = np.cos(angle), np.sin(angle)
        forward[r] = np.block([[cos, -sin], [sin, cos]])
    scale = np.full((GROUPS, 1, 1), 2.0 / points)
    scale[0] = scale[-1] = 1.0 / points
    backward = np.swapaxes(forward, 1, 2) * scale
    return forward.astype(ml_dtypes.bfloat16), backward.astype(ml_dtypes.bfloat16)


def first_stage(b):
    e = [b[p] + b[p + 4] for p in range(4)]
    f = [b[p] - b[p + 4] for p in range(4)]
    e02, e13 = e[0] + e[2], e[1] + e[3]
    fd, fs = C2 * (f[1] - f[3]), C2 * (f[1] + f[3])
    d = [None] + [b[p] - b[8 - p] for p in (1, 2, 3)]
    g = [None] + [b[p] + b[8 - p] for p in (1, 2, 3)]
    d2, g2 = C2 * d[2], C2 * g[2]
    re1, re3 = C1 * d[1] + C3 * d[3], C3 * d[1] - C1 * d[3]
    im1, im3 = C3 * g[1] + C1 * g[3], C1 * g[1] - C3 * g[3]
    up, down = b[0] + d2, b[0] - d2
    bp, bm = b[4] + g2, b[4] - g2
    return [
        (e02 + e13, None),
        (up + re1, -(bp + im1)),
        (f[0] + fd, -(f[2] + fs)),
        (down + re3, bm - im3),
        (e[0] - e[2], e[3] - e[1]),
        (down - re3, -(bm + im3)),
        (f[0] - fd, f[2] - fs),
        (up - re1, bp - im1),
        (e02 - e13, None),
    ]


def last_stage(u):
    re = [pair[0] for pair in u]
    im = [pair[1] for pair in u]
    sum08, dif08 = re[0] + re[8], re[0] - re[8]
    r26, i26 = re[2] + re[6], im[2] - im[6]
    rd, sd = C2 * (re[2] - re[6]), C2 * (im[2] + im[6])
    top, low = sum08 + re[4], sum08 - re[4]
    dp, dm = dif08 + rd, dif08 - rd
    ip, im4 = sd + im[4], sd - im[4]
    even = [
        top + r26,
        dp - ip,
        low - i26,
        dm - im4,
        top - r26,
        dm + im4,
        low + i26,
        dp + ip,
    ]
    a1p, a1m = re[1] + re[7], re[1] - re[7]
    a3p, a3m = re[3] + re[5], re[3] - re[5]
    j1p, j1m = im[1] + im[7], im[1] - im[7]
    j3p, j3m = im[3] + im[5], im[3] - im[5]
    c1, c3 = C1 * a1m + C3 * a3m, C3 * a1m - C1 * a3m
    c2 = C2 * (a1p - a3p)
    s1, s3 = C3 * j1p + C1 * j3p, C1 * j1p - C3 * j3p
    s2 = C2 * (j1m + j3m)
    odd = [
        a1p + a3p,
        c1 - s1,
        c2 - s2,
        c3 - s3,
        j3m - j1m,
        -(c3 + s3),
        -(c2 + s2),
        -(c1 + s1),
    ]
    return [x + y for x, y in zip(even, odd)]


def rows_loop(rows, body):
    @pl.loop(0, rows // TILE)
    def _(step):
        body(pl.ds(pl.multiple_of(step * TILE, TILE), TILE))


def split_rows(load, mid, rows, width):
    def body(at):
        for r, pair in enumerate(first_stage([load(p, at) for p in range(BLOCKS)])):
            mid[r, at, :width] = pair[0].astype(jnp.bfloat16)
            if pair[1] is not None:
                mid[r, at, width:] = pair[1].astype(jnp.bfloat16)

    rows_loop(rows, body)


def spectrum(mid, table, r, width):
    if r in (0, GROUPS - 1):
        return jnp.dot(mid[r, :, :width], table[r, :width, :], preferred_element_type=jnp.float32)
    return jnp.dot(mid[r], table[r], preferred_element_type=jnp.float32)


def invert_group(product, table, r, width, wide):
    if r in (0, GROUPS - 1):
        wide[r, :, :width] = jnp.dot(product, table[r, :, :width], preferred_element_type=jnp.float32)
    else:
        wide[r] = jnp.dot(product, table[r], preferred_element_type=jnp.float32)


def merge_rows(wide, store, rows, width):
    def body(at):
        parts = []
        for r in range(GROUPS):
            im = None if r in (0, GROUPS - 1) else wide[r, at, width:]
            parts.append((wide[r, at, :width], im))
        for p, value in enumerate(last_stage(parts)):
            store(p, at, value)

    rows_loop(rows, body)


def piece_at(ref, where, k, rows):
    start = pl.multiple_of(lax.bitwise_xor(where[0], k) * rows, rows)
    return ref.at[pl.ds(start, rows), :]


def gate_kernel(order, where, gate, upper, *refs):
    outs, (left, right, product, sems, out_sems) = refs[: len(order)], refs[len(order) :]
    rows = outs[0].shape[0]
    loads = []
    for i, k in enumerate(order):
        pair = (
            pltpu.make_async_copy(piece_at(gate, where, k, rows), left.at[i], sems.at[0, i]),
            pltpu.make_async_copy(piece_at(upper, where, k, rows), right.at[i], sems.at[1, i]),
        )
        for copy in pair:
            copy.start()
        loads.append(pair)
    stores = []
    for i, out in enumerate(outs):
        for copy in loads[i]:
            copy.wait()
        product[i] = (left[i].astype(jnp.float32) * right[i].astype(jnp.float32)).astype(jnp.bfloat16)
        stores.append(pltpu.make_async_copy(product.at[i], out, out_sems.at[i]))
        stores[-1].start()
    for copy in stores:
        copy.wait()


def place_kernel(order, where, *refs):
    pieces, (whole, slots, sems, out_sems) = refs[: len(order)], refs[len(order) :]
    loads = [pltpu.make_async_copy(piece, slots.at[i], sems.at[i]) for i, piece in enumerate(pieces)]
    for copy in loads:
        copy.start()
    stores = []
    for i, k in enumerate(order):
        loads[i].wait()
        stores.append(pltpu.make_async_copy(slots.at[i], piece_at(whole, where, k, slots.shape[1]), out_sems.at[i]))
        stores[-1].start()
    for copy in stores:
        copy.wait()


def taps_kernel(order, where, whole, taps, forward, *refs):
    outs, (taps_spec, slots, mid, sems, out_sems) = refs[: len(order)], refs[len(order) :]
    rows, width = (taps.shape[0], taps.shape[1] // BLOCKS)
    loads, stores = [], []
    for i, k in enumerate(order):
        loads.append(pltpu.make_async_copy(piece_at(whole, where, k, rows), slots.at[i], sems.at[i]))
        loads[-1].start()
    for i, out in enumerate(outs):
        loads[i].wait()
        stores.append(pltpu.make_async_copy(slots.at[i], out, out_sems.at[i]))
        stores[-1].start()
    split_rows(lambda p, at: taps[at, p * width : (p + 1) * width], mid, rows, width)
    for r in range(GROUPS):
        taps_spec[r] = spectrum(mid, forward, r, width).astype(taps_spec.dtype)
    for copy in stores:
        copy.wait()


def ordered(order, where, refs, held):
    span = refs[0].shape[1]
    for k, ref in zip(order, refs):
        start = pl.multiple_of(lax.bitwise_xor(where[0], k) * span, span)
        held[:, pl.ds(start, span)] = ref[...]


def block_of(held, width):
    return lambda p, at: held[at, p * width : (p + 1) * width].astype(jnp.float32)


def block_into(held, width):
    def store(p, at, value):
        held[at, p * width : (p + 1) * width] = value.astype(jnp.bfloat16)

    return store


def back_kernel(order, back_order, where, *refs):
    blocks, refs = refs[: len(order)], refs[len(order) :]
    taps_spec, forward, backward, *outs, grad_spec, held, mid, wide = refs
    rows, width = held.shape[0], held.shape[1] // BLOCKS
    ordered(order, where, blocks, held)
    split_rows(block_of(held, width), mid, rows, width)
    for r in range(GROUPS):
        grad = spectrum(mid, forward, r, width)
        grad_spec[r] = grad.astype(grad_spec.dtype)
        taps = taps_spec[r].astype(jnp.float32)
        gr, gi, hr, hi = grad[:, :width], grad[:, width:], taps[:, :width], taps[:, width:]
        product = jnp.concatenate([hr * gr + hi * gi, hr * gi - hi * gr], axis=1)
        invert_group(product.astype(jnp.bfloat16), backward, r, width, wide)
    merge_rows(wide, block_into(held, width), rows, width)
    span = outs[0].shape[1]
    for k, out in zip(back_order, outs):
        start = pl.multiple_of(lax.bitwise_xor(where[0], k) * span, span)
        out[...] = held[:, pl.ds(start, span)]


def cross_kernel(order, near, where, *refs):
    blocks, refs = refs[: len(order)], refs[len(order) + near :]
    grad_spec, forward, backward, *outs, held, mid, wide = refs
    outs = outs[near:]
    rows, width = held.shape[0], held.shape[1] // BLOCKS
    ordered(order, where, blocks, held)
    split_rows(block_of(held, width), mid, rows, width)
    for r in range(GROUPS):
        signal = spectrum(mid, forward, r, width)
        grad = grad_spec[r].astype(jnp.float32)
        gr, gi, xr, xi = grad[:, :width], grad[:, width:], signal[:, :width], signal[:, width:]
        product = jnp.concatenate([gr * xr + gi * xi, gi * xr - gr * xi], axis=1)
        invert_group(product.astype(jnp.bfloat16), backward, r, width, wide)
    merge_rows(wide, block_into(held, width), rows, width)
    part = held.shape[1] // len(outs)
    for k, out in enumerate(outs):
        start = pl.multiple_of(lax.bitwise_xor(where[1], k) * part, part)
        out[...] = held[:, pl.ds(start, part)]


def sum_kernel(scale, *refs):
    total = refs[0][...].astype(jnp.float32)
    for ref in refs[1:-1]:
        total = total + ref[...].astype(jnp.float32)
    refs[-1][...] = total * scale


def call(kernel, operands, outs, scratch=(), flops=0, streams=(), out_streams=(), aliases=None):
    def spec(stream):
        return pl.BlockSpec(memory_space=pl.ANY if stream else pltpu.VMEM)

    size = sum(math.prod(o.shape) * o.dtype.itemsize for o in list(operands) + list(outs))
    specs = [spec(i in streams) for i in range(len(operands))]
    if operands[0].dtype == jnp.int32:
        specs[0] = pl.BlockSpec(memory_space=pltpu.SMEM)
    return pl.pallas_call(
        kernel,
        out_shape=list(outs),
        in_specs=specs,
        out_specs=[spec(i in out_streams) for i in range(len(outs))],
        scratch_shapes=list(scratch),
        input_output_aliases=aliases or {},
        compiler_params=pltpu.CompilerParams(vmem_limit_bytes=LIMIT),
        cost_estimate=pl.CostEstimate(flops=flops, bytes_accessed=size, transcendentals=0),
    )(*operands)


def far_first(size):
    return [*range(size // 2, size), *range(1, size // 2), 0]


def mixed(size):
    far = far_first(size)
    return [k for pair in zip(far[: size // 2], far[size // 2 :]) for k in pair]


def exchange(pieces, order, axis, size):
    moved = []
    for k, piece in zip(order, pieces):
        moved.append(lax.ppermute(piece, axis, [(i, i ^ k) for i in range(size)]) if k else piece)
    return moved


def on_device(saved_input, out_gate, grad_out, long_filter):
    count, shares = lax.axis_size("ctx"), lax.axis_size("dp")
    channels, span = saved_input.shape[1:]
    rows, length = long_filter.shape
    width = length // BLOCKS
    order, back_order, near = mixed(count), far_first(count), count // 2
    every = range(count + 8)
    where = jnp.stack([lax.axis_index("ctx"), lax.axis_index("dp")]).astype(jnp.int32)
    forward, backward = (jnp.asarray(t) for t in transform_tables(width))
    half, full = jnp.bfloat16, jnp.float32
    piece = jax.ShapeDtypeStruct((rows, span), half)
    spec = jax.ShapeDtypeStruct((GROUPS, rows, 2 * width), half)
    held = pltpu.VMEM((rows, length), half)
    mid = pltpu.VMEM((GROUPS, rows, 2 * width), half)
    wide = pltpu.VMEM((GROUPS, rows, 2 * width), full)
    slots = pltpu.VMEM((count, rows, span), half)
    sems = pltpu.SemaphoreType.DMA
    work = 2 * GROUPS * rows * 4 * width * width

    grad_pieces = call(
        functools.partial(gate_kernel, order),
        [where, out_gate[0], grad_out[0]],
        [piece] * count,
        [slots, slots, slots, sems((2, count)), sems((count,))],
        streams=every,
        out_streams=every,
    )
    grad_blocks = exchange(grad_pieces, order, "ctx", count)
    *input_pieces, taps_spec = call(
        functools.partial(taps_kernel, order),
        [where, saved_input[0], long_filter, forward],
        [piece] * count + [spec],
        [slots, mid, sems((count,)), sems((count,))],
        flops=work,
        streams=(1,),
        out_streams=range(count),
    )
    input_blocks = exchange(input_pieces, order, "ctx", count)
    *back, grad_spec = call(
        functools.partial(back_kernel, order, back_order),
        [where, *grad_blocks, taps_spec, forward, backward],
        [piece] * count + [spec],
        [held, mid, wide],
        flops=2 * work,
    )
    share = jax.ShapeDtypeStruct((rows, length // shares), half)
    cross = call(
        functools.partial(cross_kernel, order, near),
        [where, *input_blocks, *back[-near:], grad_spec, forward, backward],
        [piece] * near + [share] * shares,
        [held, mid, wide],
        flops=2 * work,
        streams=range(1 + count, 1 + count + near),
        out_streams=range(near),
        aliases={1 + count + i: i for i in range(near)},
    )
    back_blocks = exchange([*back[:-near], *cross[:near]], back_order, "ctx", count)
    cross_blocks = exchange(cross[near:], range(shares), "dp", shares)
    scale = 1.0 / math.sqrt(shares * length)
    (grad_filter,) = call(
        functools.partial(sum_kernel, scale),
        cross_blocks,
        [jax.ShapeDtypeStruct((rows, length // shares), full)],
    )
    (grad_input,) = call(
        functools.partial(place_kernel, back_order),
        [where, *back_blocks],
        [jax.ShapeDtypeStruct((channels, span), half)],
        [slots, sems((count,)), sems((count,))],
        streams=every,
        out_streams=every,
    )
    return (grad_input[None], grad_filter)


def solution(mesh):
    in_specs = (P("dp", None, "ctx"), P("dp", None, "ctx"), P("dp", None, "ctx"), P("ctx", None))
    out_specs = (P("dp", None, "ctx"), P("ctx", "dp"))
    return jax.shard_map(
        on_device, mesh=mesh, in_specs=in_specs, out_specs=out_specs, check_vma=False
    )
```

```python
import functools
import math

import jax
import jax.numpy as jnp
import ml_dtypes
import numpy as np
from jax import lax
from jax.experimental import pallas as pl
from jax.experimental.pallas import tpu as pltpu
from jax.sharding import PartitionSpec as P

BLOCKS = 8
GROUPS = 9
TILE = 16
C1 = math.cos(math.pi / 8)
C2 = math.cos(math.pi / 4)
C3 = math.cos(3 * math.pi / 8)
LIMIT = 56 * 1024 * 1024


def transform_tables(width):
    points = 2 * BLOCKS * width
    row = np.arange(width)
    forward = np.zeros((GROUPS, 2 * width, 2 * width), np.float64)
    for r in range(GROUPS):
        angle = 2.0 * np.pi * (np.outer(row, 16 * row + r) % points) / points
        cos, sin = np.cos(angle), np.sin(angle)
        forward[r] = np.block([[cos, -sin], [sin, cos]])
    scale = np.full((GROUPS, 1, 1), 2.0 / points)
    scale[0] = scale[-1] = 1.0 / points
    backward = np.swapaxes(forward, 1, 2) * scale
    return forward.astype(ml_dtypes.bfloat16), backward.astype(ml_dtypes.bfloat16)


def first_stage(b):
    e = [b[p] + b[p + 4] for p in range(4)]
    f = [b[p] - b[p + 4] for p in range(4)]
    e02, e13 = e[0] + e[2], e[1] + e[3]
    fd, fs = C2 * (f[1] - f[3]), C2 * (f[1] + f[3])
    d = [None] + [b[p] - b[8 - p] for p in (1, 2, 3)]
    g = [None] + [b[p] + b[8 - p] for p in (1, 2, 3)]
    d2, g2 = C2 * d[2], C2 * g[2]
    re1, re3 = C1 * d[1] + C3 * d[3], C3 * d[1] - C1 * d[3]
    im1, im3 = C3 * g[1] + C1 * g[3], C1 * g[1] - C3 * g[3]
    up, down = b[0] + d2, b[0] - d2
    bp, bm = b[4] + g2, b[4] - g2
    return [
        (e02 + e13, None),
        (up + re1, -(bp + im1)),
        (f[0] + fd, -(f[2] + fs)),
        (down + re3, bm - im3),
        (e[0] - e[2], e[3] - e[1]),
        (down - re3, -(bm + im3)),
        (f[0] - fd, f[2] - fs),
        (up - re1, bp - im1),
        (e02 - e13, None),
    ]


def last_stage(u):
    re = [pair[0] for pair in u]
    im = [pair[1] for pair in u]
    sum08, dif08 = re[0] + re[8], re[0] - re[8]
    r26, i26 = re[2] + re[6], im[2] - im[6]
    rd, sd = C2 * (re[2] - re[6]), C2 * (im[2] + im[6])
    top, low = sum08 + re[4], sum08 - re[4]
    dp, dm = dif08 + rd, dif08 - rd
    ip, im4 = sd + im[4], sd - im[4]
    even = [
        top + r26,
        dp - ip,
        low - i26,
        dm - im4,
        top - r26,
        dm + im4,
        low + i26,
        dp + ip,
    ]
    a1p, a1m = re[1] + re[7], re[1] - re[7]
    a3p, a3m = re[3] + re[5], re[3] - re[5]
    j1p, j1m = im[1] + im[7], im[1] - im[7]
    j3p, j3m = im[3] + im[5], im[3] - im[5]
    c1, c3 = C1 * a1m + C3 * a3m, C3 * a1m - C1 * a3m
    c2 = C2 * (a1p - a3p)
    s1, s3 = C3 * j1p + C1 * j3p, C1 * j1p - C3 * j3p
    s2 = C2 * (j1m + j3m)
    odd = [
        a1p + a3p,
        c1 - s1,
        c2 - s2,
        c3 - s3,
        j3m - j1m,
        -(c3 + s3),
        -(c2 + s2),
        -(c1 + s1),
    ]
    return [x + y for x, y in zip(even, odd)]


def rows_loop(rows, body):
    @pl.loop(0, rows // TILE)
    def _(step):
        body(pl.ds(pl.multiple_of(step * TILE, TILE), TILE))


def split_rows(load, mid, rows, width):
    def body(at):
        for r, pair in enumerate(first_stage([load(p, at) for p in range(BLOCKS)])):
            mid[r, at, :width] = pair[0].astype(jnp.bfloat16)
            if pair[1] is not None:
                mid[r, at, width:] = pair[1].astype(jnp.bfloat16)

    rows_loop(rows, body)


def spectrum(mid, table, r, width):
    if r in (0, GROUPS - 1):
        return jnp.dot(mid[r, :, :width], table[r, :width, :], preferred_element_type=jnp.float32)
    return jnp.dot(mid[r], table[r], preferred_element_type=jnp.float32)


def invert_group(product, table, r, width, wide):
    if r in (0, GROUPS - 1):
        wide[r, :, :width] = jnp.dot(product, table[r, :, :width], preferred_element_type=jnp.float32)
    else:
        wide[r] = jnp.dot(product, table[r], preferred_element_type=jnp.float32)


def merge_rows(wide, store, rows, width):
    def body(at):
        parts = []
        for r in range(GROUPS):
            im = None if r in (0, GROUPS - 1) else wide[r, at, width:]
            parts.append((wide[r, at, :width], im))
        for p, value in enumerate(last_stage(parts)):
            store(p, at, value)

    rows_loop(rows, body)


def piece_at(ref, where, k, rows):
    start = pl.multiple_of(lax.bitwise_xor(where[0], k) * rows, rows)
    return ref.at[pl.ds(start, rows), :]


def gate_kernel(order, where, gate, upper, *refs):
    outs, (left, right, product, sems, out_sems) = refs[: len(order)], refs[len(order) :]
    rows = outs[0].shape[0]
    loads = []
    for i, k in enumerate(order):
        pair = (
            pltpu.make_async_copy(piece_at(gate, where, k, rows), left.at[i], sems.at[0, i]),
            pltpu.make_async_copy(piece_at(upper, where, k, rows), right.at[i], sems.at[1, i]),
        )
        for copy in pair:
            copy.start()
        loads.append(pair)
    stores = []
    for i, out in enumerate(outs):
        for copy in loads[i]:
            copy.wait()
        product[i] = (left[i].astype(jnp.float32) * right[i].astype(jnp.float32)).astype(jnp.bfloat16)
        stores.append(pltpu.make_async_copy(product.at[i], out, out_sems.at[i]))
        stores[-1].start()
    for copy in stores:
        copy.wait()


def place_kernel(order, where, *refs):
    pieces, (whole, slots, sems, out_sems) = refs[: len(order)], refs[len(order) :]
    loads = [pltpu.make_async_copy(piece, slots.at[i], sems.at[i]) for i, piece in enumerate(pieces)]
    for copy in loads:
        copy.start()
    stores = []
    for i, k in enumerate(order):
        loads[i].wait()
        stores.append(pltpu.make_async_copy(slots.at[i], piece_at(whole, where, k, slots.shape[1]), out_sems.at[i]))
        stores[-1].start()
    for copy in stores:
        copy.wait()


def taps_kernel(order, where, whole, taps, forward, *refs):
    outs, (taps_spec, slots, mid, sems, out_sems) = refs[: len(order)], refs[len(order) :]
    rows, width = (taps.shape[0], taps.shape[1] // BLOCKS)
    loads, stores = [], []
    for i, k in enumerate(order):
        loads.append(pltpu.make_async_copy(piece_at(whole, where, k, rows), slots.at[i], sems.at[i]))
        loads[-1].start()
    for i, out in enumerate(outs):
        loads[i].wait()
        stores.append(pltpu.make_async_copy(slots.at[i], out, out_sems.at[i]))
        stores[-1].start()
    split_rows(lambda p, at: taps[at, p * width : (p + 1) * width], mid, rows, width)
    for r in range(GROUPS):
        taps_spec[r] = spectrum(mid, forward, r, width).astype(taps_spec.dtype)
    for copy in stores:
        copy.wait()


def ordered(order, where, refs, held):
    span = refs[0].shape[1]
    for k, ref in zip(order, refs):
        start = pl.multiple_of(lax.bitwise_xor(where[0], k) * span, span)
        held[:, pl.ds(start, span)] = ref[...]


def block_of(held, width):
    return lambda p, at: held[at, p * width : (p + 1) * width].astype(jnp.float32)


def block_into(held, width):
    def store(p, at, value):
        held[at, p * width : (p + 1) * width] = value.astype(jnp.bfloat16)

    return store


def back_kernel(order, back_order, late, where, *refs):
    blocks, refs = refs[: len(order)], refs[len(order) + late :]
    taps_spec, forward, backward, *outs, grad_spec, held, mid, wide = refs
    outs = outs[late:]
    rows, width = held.shape[0], held.shape[1] // BLOCKS
    ordered(order, where, blocks, held)
    split_rows(block_of(held, width), mid, rows, width)
    for r in range(GROUPS):
        grad = spectrum(mid, forward, r, width)
        grad_spec[r] = grad.astype(grad_spec.dtype)
        taps = taps_spec[r].astype(jnp.float32)
        gr, gi, hr, hi = grad[:, :width], grad[:, width:], taps[:, :width], taps[:, width:]
        product = jnp.concatenate([hr * gr + hi * gi, hr * gi - hi * gr], axis=1)
        invert_group(product.astype(jnp.bfloat16), backward, r, width, wide)
    merge_rows(wide, block_into(held, width), rows, width)
    span = outs[0].shape[1]
    for k, out in zip(back_order, outs):
        start = pl.multiple_of(lax.bitwise_xor(where[0], k) * span, span)
        out[...] = held[:, pl.ds(start, span)]


def cross_kernel(order, near, where, *refs):
    blocks, refs = refs[: len(order)], refs[len(order) + near :]
    grad_spec, forward, backward, *outs, held, mid, wide = refs
    outs = outs[near:]
    rows, width = held.shape[0], held.shape[1] // BLOCKS
    ordered(order, where, blocks, held)
    split_rows(block_of(held, width), mid, rows, width)
    for r in range(GROUPS):
        signal = spectrum(mid, forward, r, width)
        grad = grad_spec[r].astype(jnp.float32)
        gr, gi, xr, xi = grad[:, :width], grad[:, width:], signal[:, :width], signal[:, width:]
        product = jnp.concatenate([gr * xr + gi * xi, gi * xr - gr * xi], axis=1)
        invert_group(product.astype(jnp.bfloat16), backward, r, width, wide)
    merge_rows(wide, block_into(held, width), rows, width)
    part = held.shape[1] // len(outs)
    for k, out in enumerate(outs):
        start = pl.multiple_of(lax.bitwise_xor(where[1], k) * part, part)
        out[...] = held[:, pl.ds(start, part)]


def sum_kernel(scale, *refs):
    total = refs[0][...].astype(jnp.float32)
    for ref in refs[1:-1]:
        total = total + ref[...].astype(jnp.float32)
    refs[-1][...] = total * scale


def call(kernel, operands, outs, scratch=(), flops=0, streams=(), out_streams=(), aliases=None):
    def spec(stream):
        return pl.BlockSpec(memory_space=pl.ANY if stream else pltpu.VMEM)

    size = sum(math.prod(o.shape) * o.dtype.itemsize for o in list(operands) + list(outs))
    specs = [spec(i in streams) for i in range(len(operands))]
    if operands[0].dtype == jnp.int32:
        specs[0] = pl.BlockSpec(memory_space=pltpu.SMEM)
    return pl.pallas_call(
        kernel,
        out_shape=list(outs),
        in_specs=specs,
        out_specs=[spec(i in out_streams) for i in range(len(outs))],
        scratch_shapes=list(scratch),
        input_output_aliases=aliases or {},
        compiler_params=pltpu.CompilerParams(vmem_limit_bytes=LIMIT),
        cost_estimate=pl.CostEstimate(flops=flops, bytes_accessed=size, transcendentals=0),
    )(*operands)


def far_first(size):
    return [*range(size // 2, size), *range(1, size // 2), 0]


def near_first(size):
    return [*range(1, size), 0]


def mixed(size):
    far = far_first(size)
    return [k for pair in zip(far[: size // 2], far[size // 2 :]) for k in pair]


def exchange(pieces, order, axis, size):
    moved = []
    for k, piece in zip(order, pieces):
        moved.append(lax.ppermute(piece, axis, [(i, i ^ k) for i in range(size)]) if k else piece)
    return moved


def on_device(saved_input, out_gate, grad_out, long_filter):
    count, shares = lax.axis_size("ctx"), lax.axis_size("dp")
    channels, span = saved_input.shape[1:]
    rows, length = long_filter.shape
    width = length // BLOCKS
    order, back_order, near = mixed(count), near_first(count), 0
    late, at = 2, count - 1 - 2
    every = range(count + 8)
    where = jnp.stack([lax.axis_index("ctx"), lax.axis_index("dp")]).astype(jnp.int32)
    forward, backward = (jnp.asarray(t) for t in transform_tables(width))
    half, full = jnp.bfloat16, jnp.float32
    piece = jax.ShapeDtypeStruct((rows, span), half)
    spec = jax.ShapeDtypeStruct((GROUPS, rows, 2 * width), half)
    held = pltpu.VMEM((rows, length), half)
    mid = pltpu.VMEM((GROUPS, rows, 2 * width), half)
    wide = pltpu.VMEM((GROUPS, rows, 2 * width), full)
    slots = pltpu.VMEM((count, rows, span), half)
    sems = pltpu.SemaphoreType.DMA
    work = 2 * GROUPS * rows * 4 * width * width

    grad_pieces = call(
        functools.partial(gate_kernel, order),
        [where, out_gate[0], grad_out[0]],
        [piece] * count,
        [slots, slots, slots, sems((2, count)), sems((count,))],
        streams=every,
        out_streams=every,
    )
    grad_blocks = exchange(grad_pieces, order, "ctx", count)
    *input_pieces, taps_spec = call(
        functools.partial(taps_kernel, order),
        [where, saved_input[0], long_filter, forward],
        [piece] * count + [spec],
        [slots, mid, sems((count,)), sems((count,))],
        flops=work,
        streams=(1,),
        out_streams=range(count),
    )
    *back, grad_spec = call(
        functools.partial(back_kernel, order, back_order, late),
        [where, *grad_blocks, *input_pieces[at : at + late], taps_spec, forward, backward],
        [piece] * (late + count) + [spec],
        [held, mid, wide],
        flops=2 * work,
        streams=range(1 + count, 1 + count + late),
        out_streams=range(late),
        aliases={1 + count + i: i for i in range(late)},
    )
    input_pieces[at : at + late], back = back[:late], back[late:]
    input_blocks = exchange(input_pieces, order, "ctx", count)
    share = jax.ShapeDtypeStruct((rows, length // shares), half)
    cross = call(
        functools.partial(cross_kernel, order, near),
        [where, *input_blocks, *back[count - near :], grad_spec, forward, backward],
        [piece] * near + [share] * shares,
        [held, mid, wide],
        flops=2 * work,
        streams=range(1 + count, 1 + count + near),
        out_streams=range(near),
        aliases={1 + count + i: i for i in range(near)},
    )
    back_blocks = exchange([*back[: count - near], *cross[:near]], back_order, "ctx", count)
    cross_blocks = exchange(cross[near:], range(shares), "dp", shares)
    scale = 1.0 / math.sqrt(shares * length)
    (grad_filter,) = call(
        functools.partial(sum_kernel, scale),
        cross_blocks,
        [jax.ShapeDtypeStruct((rows, length // shares), full)],
    )
    (grad_input,) = call(
        functools.partial(place_kernel, back_order),
        [where, *back_blocks],
        [jax.ShapeDtypeStruct((channels, span), half)],
        [slots, sems((count,)), sems((count,))],
        streams=every,
        out_streams=every,
    )
    return (grad_input[None], grad_filter)


def solution(mesh):
    in_specs = (P("dp", None, "ctx"), P("dp", None, "ctx"), P("dp", None, "ctx"), P("ctx", None))
    out_specs = (P("dp", None, "ctx"), P("ctx", "dp"))
    return jax.shard_map(
        on_device, mesh=mesh, in_specs=in_specs, out_specs=out_specs, check_vma=False
    )
```

```python
import functools
import math

import jax
import jax.numpy as jnp
import ml_dtypes
import numpy as np
from jax import lax
from jax.experimental import pallas as pl
from jax.experimental.pallas import tpu as pltpu
from jax.sharding import PartitionSpec as P

BLOCKS = 8
GROUPS = 9
TILE = 16
C1 = math.cos(math.pi / 8)
C2 = math.cos(math.pi / 4)
C3 = math.cos(3 * math.pi / 8)
LIMIT = 32 * 1024 * 1024


def transform_tables(width):
    points = 2 * BLOCKS * width
    row = np.arange(width)
    forward = np.zeros((GROUPS, 2 * width, 2 * width), np.float64)
    for r in range(GROUPS):
        angle = 2.0 * np.pi * (np.outer(row, 16 * row + r) % points) / points
        cos, sin = np.cos(angle), np.sin(angle)
        forward[r] = np.block([[cos, -sin], [sin, cos]])
    scale = np.full((GROUPS, 1, 1), 2.0 / points)
    scale[0] = scale[-1] = 1.0 / points
    backward = np.swapaxes(forward, 1, 2) * scale
    return forward.astype(ml_dtypes.bfloat16), backward.astype(ml_dtypes.bfloat16)


def first_stage(b):
    e = [b[p] + b[p + 4] for p in range(4)]
    f = [b[p] - b[p + 4] for p in range(4)]
    e02, e13 = e[0] + e[2], e[1] + e[3]
    fd, fs = C2 * (f[1] - f[3]), C2 * (f[1] + f[3])
    d = [None] + [b[p] - b[8 - p] for p in (1, 2, 3)]
    g = [None] + [b[p] + b[8 - p] for p in (1, 2, 3)]
    d2, g2 = C2 * d[2], C2 * g[2]
    re1, re3 = C1 * d[1] + C3 * d[3], C3 * d[1] - C1 * d[3]
    im1, im3 = C3 * g[1] + C1 * g[3], C1 * g[1] - C3 * g[3]
    up, down = b[0] + d2, b[0] - d2
    bp, bm = b[4] + g2, b[4] - g2
    return [
        (e02 + e13, None),
        (up + re1, -(bp + im1)),
        (f[0] + fd, -(f[2] + fs)),
        (down + re3, bm - im3),
        (e[0] - e[2], e[3] - e[1]),
        (down - re3, -(bm + im3)),
        (f[0] - fd, f[2] - fs),
        (up - re1, bp - im1),
        (e02 - e13, None),
    ]


def last_stage(u):
    re = [pair[0] for pair in u]
    im = [pair[1] for pair in u]
    sum08, dif08 = re[0] + re[8], re[0] - re[8]
    r26, i26 = re[2] + re[6], im[2] - im[6]
    rd, sd = C2 * (re[2] - re[6]), C2 * (im[2] + im[6])
    top, low = sum08 + re[4], sum08 - re[4]
    dp, dm = dif08 + rd, dif08 - rd
    ip, im4 = sd + im[4], sd - im[4]
    even = [
        top + r26,
        dp - ip,
        low - i26,
        dm - im4,
        top - r26,
        dm + im4,
        low + i26,
        dp + ip,
    ]
    a1p, a1m = re[1] + re[7], re[1] - re[7]
    a3p, a3m = re[3] + re[5], re[3] - re[5]
    j1p, j1m = im[1] + im[7], im[1] - im[7]
    j3p, j3m = im[3] + im[5], im[3] - im[5]
    c1, c3 = C1 * a1m + C3 * a3m, C3 * a1m - C1 * a3m
    c2 = C2 * (a1p - a3p)
    s1, s3 = C3 * j1p + C1 * j3p, C1 * j1p - C3 * j3p
    s2 = C2 * (j1m + j3m)
    odd = [
        a1p + a3p,
        c1 - s1,
        c2 - s2,
        c3 - s3,
        j3m - j1m,
        -(c3 + s3),
        -(c2 + s2),
        -(c1 + s1),
    ]
    return [x + y for x, y in zip(even, odd)]


def rows_loop(rows, body):
    @pl.loop(0, rows // TILE)
    def _(step):
        body(pl.ds(pl.multiple_of(step * TILE, TILE), TILE))


def split_rows(load, mid, rows, width):
    def body(at):
        for r, pair in enumerate(first_stage([load(p, at) for p in range(BLOCKS)])):
            mid[r, at, :width] = pair[0].astype(jnp.bfloat16)
            if pair[1] is not None:
                mid[r, at, width:] = pair[1].astype(jnp.bfloat16)

    rows_loop(rows, body)


def spectrum(mid, table, r, width):
    if r in (0, GROUPS - 1):
        return jnp.dot(mid[r, :, :width], table[r, :width, :], preferred_element_type=jnp.float32)
    return jnp.dot(mid[r], table[r], preferred_element_type=jnp.float32)


def invert_group(product, table, r, width, wide):
    if r in (0, GROUPS - 1):
        wide[r, :, :width] = jnp.dot(product, table[r, :, :width], preferred_element_type=jnp.float32)
    else:
        wide[r] = jnp.dot(product, table[r], preferred_element_type=jnp.float32)


def merge_rows(wide, store, rows, width):
    def body(at):
        parts = []
        for r in range(GROUPS):
            im = None if r in (0, GROUPS - 1) else wide[r, at, width:]
            parts.append((wide[r, at, :width], im))
        for p, value in enumerate(last_stage(parts)):
            store(p, at, value)

    rows_loop(rows, body)


def piece_at(ref, where, k, rows):
    start = pl.multiple_of(lax.bitwise_xor(where[0], k) * rows, rows)
    return ref.at[pl.ds(start, rows), :]


def gate_kernel(order, where, gate, upper, *refs):
    outs, (left, right, product, sems, out_sems) = refs[: len(order)], refs[len(order) :]
    rows = outs[0].shape[0]
    loads = []
    for i, k in enumerate(order):
        pair = (
            pltpu.make_async_copy(piece_at(gate, where, k, rows), left.at[i], sems.at[0, i]),
            pltpu.make_async_copy(piece_at(upper, where, k, rows), right.at[i], sems.at[1, i]),
        )
        for copy in pair:
            copy.start()
        loads.append(pair)
    stores = []
    for i, out in enumerate(outs):
        for copy in loads[i]:
            copy.wait()
        product[i] = (left[i].astype(jnp.float32) * right[i].astype(jnp.float32)).astype(jnp.bfloat16)
        stores.append(pltpu.make_async_copy(product.at[i], out, out_sems.at[i]))
        stores[-1].start()
    for copy in stores:
        copy.wait()


def taps_kernel(order, where, whole, taps, forward, *refs):
    outs, (taps_spec, slots, mid, sems, out_sems) = refs[: len(order)], refs[len(order) :]
    rows, width = (taps.shape[0], taps.shape[1] // BLOCKS)
    loads, stores = [], []
    for i, k in enumerate(order):
        loads.append(pltpu.make_async_copy(piece_at(whole, where, k, rows), slots.at[i], sems.at[i]))
        loads[-1].start()
    for i, out in enumerate(outs):
        loads[i].wait()
        stores.append(pltpu.make_async_copy(slots.at[i], out, out_sems.at[i]))
        stores[-1].start()
    split_rows(lambda p, at: taps[at, p * width : (p + 1) * width], mid, rows, width)
    for r in range(GROUPS):
        taps_spec[r] = spectrum(mid, forward, r, width).astype(taps_spec.dtype)
    for copy in stores:
        copy.wait()


def ordered(order, where, refs, held):
    span = refs[0].shape[1]
    for k, ref in zip(order, refs):
        start = pl.multiple_of(lax.bitwise_xor(where[0], k) * span, span)
        held[:, pl.ds(start, span)] = ref[...]


def block_of(held, width):
    return lambda p, at: held[at, p * width : (p + 1) * width].astype(jnp.float32)


def block_into(held, width):
    def store(p, at, value):
        held[at, p * width : (p + 1) * width] = value.astype(jnp.bfloat16)

    return store


def back_kernel(order, late, where, *refs):
    blocks, refs = refs[: len(order)], refs[len(order) + late :]
    taps_spec, forward, backward, *_, out, grad_spec, held, mid, wide = refs
    rows, width = held.shape[0], held.shape[1] // BLOCKS
    ordered(order, where, blocks, held)
    split_rows(block_of(held, width), mid, rows, width)
    for r in range(GROUPS):
        grad = spectrum(mid, forward, r, width)
        grad_spec[r] = grad.astype(grad_spec.dtype)
        taps = taps_spec[r].astype(jnp.float32)
        gr, gi, hr, hi = grad[:, :width], grad[:, width:], taps[:, :width], taps[:, width:]
        product = jnp.concatenate([hr * gr + hi * gi, hr * gi - hi * gr], axis=1)
        invert_group(product.astype(jnp.bfloat16), backward, r, width, wide)
    merge_rows(wide, block_into(held, width), rows, width)
    span = out.shape[2]
    for p in range(out.shape[0]):
        out[p] = held[:, p * span : (p + 1) * span]


def cross_kernel(order, where, *refs):
    blocks, refs = refs[: len(order)], refs[len(order) :]
    grad_spec, forward, backward, *outs, held, mid, wide = refs
    rows, width = held.shape[0], held.shape[1] // BLOCKS
    ordered(order, where, blocks, held)
    split_rows(block_of(held, width), mid, rows, width)
    for r in range(GROUPS):
        signal = spectrum(mid, forward, r, width)
        grad = grad_spec[r].astype(jnp.float32)
        gr, gi, xr, xi = grad[:, :width], grad[:, width:], signal[:, :width], signal[:, width:]
        product = jnp.concatenate([gr * xr + gi * xi, gi * xr - gr * xi], axis=1)
        invert_group(product.astype(jnp.bfloat16), backward, r, width, wide)
    merge_rows(wide, block_into(held, width), rows, width)
    part = held.shape[1] // len(outs)
    for k, out in zip(far_first(len(outs)), outs):
        start = pl.multiple_of(lax.bitwise_xor(where[1], k) * part, part)
        out[...] = held[:, pl.ds(start, part)]


def call(kernel, operands, outs, scratch=(), flops=0, streams=(), out_streams=(), aliases=None):
    def spec(stream):
        return pl.BlockSpec(memory_space=pl.ANY if stream else pltpu.VMEM)

    size = sum(math.prod(o.shape) * o.dtype.itemsize for o in list(operands) + list(outs))
    specs = [spec(i in streams) for i in range(len(operands))]
    if operands[0].dtype == jnp.int32:
        specs[0] = pl.BlockSpec(memory_space=pltpu.SMEM)
    return pl.pallas_call(
        kernel,
        out_shape=list(outs),
        in_specs=specs,
        out_specs=[spec(i in out_streams) for i in range(len(outs))],
        scratch_shapes=list(scratch),
        input_output_aliases=aliases or {},
        compiler_params=pltpu.CompilerParams(vmem_limit_bytes=LIMIT),
        cost_estimate=pl.CostEstimate(flops=flops, bytes_accessed=size, transcendentals=0),
    )(*operands)


def far_first(size):
    return [*range(size // 2, size), *range(1, size // 2), 0]


def mixed(size):
    far = far_first(size)
    return [k for pair in zip(far[: size // 2], far[size // 2 :]) for k in pair]


def exchange(pieces, order, axis, size):
    moved = []
    for k, piece in zip(order, pieces):
        moved.append(lax.ppermute(piece, axis, [(i, i ^ k) for i in range(size)]) if k else piece)
    return moved


def on_device(saved_input, out_gate, grad_out, long_filter):
    count, shares = lax.axis_size("ctx"), lax.axis_size("dp")
    channels, span = saved_input.shape[1:]
    rows, length = long_filter.shape
    width = length // BLOCKS
    order, late = mixed(count), 2
    at = count - 1 - late
    every = range(count + 8)
    where = jnp.stack([lax.axis_index("ctx"), lax.axis_index("dp")]).astype(jnp.int32)
    forward, backward = (jnp.asarray(t) for t in transform_tables(width))
    half, full = jnp.bfloat16, jnp.float32
    piece = jax.ShapeDtypeStruct((rows, span), half)
    spec = jax.ShapeDtypeStruct((GROUPS, rows, 2 * width), half)
    held = pltpu.VMEM((rows, length), half)
    mid = pltpu.VMEM((GROUPS, rows, 2 * width), half)
    wide = pltpu.VMEM((GROUPS, rows, 2 * width), full)
    slots = pltpu.VMEM((count, rows, span), half)
    sems = pltpu.SemaphoreType.DMA
    work = 2 * GROUPS * rows * 4 * width * width

    grad_pieces = call(
        functools.partial(gate_kernel, order),
        [where, out_gate[0], grad_out[0]],
        [piece] * count,
        [slots, slots, slots, sems((2, count)), sems((count,))],
        streams=every,
        out_streams=every,
    )
    grad_blocks = exchange(grad_pieces, order, "ctx", count)
    *input_pieces, taps_spec = call(
        functools.partial(taps_kernel, order),
        [where, saved_input[0], long_filter, forward],
        [piece] * count + [spec],
        [slots, mid, sems((count,)), sems((count,))],
        flops=work,
        streams=(1,),
        out_streams=range(count),
    )
    *input_pieces[at : at + late], back, grad_spec = call(
        functools.partial(back_kernel, order, late),
        [where, *grad_blocks, *input_pieces[at : at + late], taps_spec, forward, backward],
        [piece] * late + [jax.ShapeDtypeStruct((count, rows, span), half), spec],
        [held, mid, wide],
        flops=2 * work,
        streams=range(1 + count, 1 + count + late),
        out_streams=range(late),
        aliases={1 + count + i: i for i in range(late)},
    )
    input_blocks = exchange(input_pieces, order, "ctx", count)
    grad_input = lax.all_to_all(back, "ctx", split_axis=0, concat_axis=0, tiled=True)
    share = jax.ShapeDtypeStruct((rows, length // shares), half)
    cross = call(
        functools.partial(cross_kernel, order),
        [where, *input_blocks, grad_spec, forward, backward],
        [share] * shares,
        [held, mid, wide],
        flops=2 * work,
    )
    cross_blocks = exchange(cross, far_first(shares), "dp", shares)
    scale = 1.0 / math.sqrt(shares * length)
    grad_filter = sum(x.astype(full) for x in cross_blocks) * scale
    return (grad_input.reshape(1, channels, span), grad_filter)


def solution(mesh):
    in_specs = (P("dp", None, "ctx"), P("dp", None, "ctx"), P("dp", None, "ctx"), P("ctx", None))
    out_specs = (P("dp", None, "ctx"), P("ctx", "dp"))
    return jax.shard_map(
        on_device, mesh=mesh, in_specs=in_specs, out_specs=out_specs, check_vma=False
    )
```

```python
import functools
import math

import jax
import jax.numpy as jnp
import ml_dtypes
import numpy as np
from jax import lax
from jax.experimental import pallas as pl
from jax.experimental.pallas import tpu as pltpu
from jax.sharding import PartitionSpec as P

BLOCKS = 8
GROUPS = 9
TILE = 16
C1 = math.cos(math.pi / 8)
C2 = math.cos(math.pi / 4)
C3 = math.cos(3 * math.pi / 8)
LIMIT = 32 * 1024 * 1024


def transform_tables(width):
    points = 2 * BLOCKS * width
    row = np.arange(width)
    forward = np.zeros((GROUPS, 2 * width, 2 * width), np.float64)
    for r in range(GROUPS):
        angle = 2.0 * np.pi * (np.outer(row, 16 * row + r) % points) / points
        cos, sin = np.cos(angle), np.sin(angle)
        forward[r] = np.block([[cos, -sin], [sin, cos]])
    scale = np.full((GROUPS, 1, 1), 2.0 / points)
    scale[0] = scale[-1] = 1.0 / points
    backward = np.swapaxes(forward, 1, 2) * scale
    return forward.astype(ml_dtypes.bfloat16), backward.astype(ml_dtypes.bfloat16)


def first_stage(b):
    e = [b[p] + b[p + 4] for p in range(4)]
    f = [b[p] - b[p + 4] for p in range(4)]
    e02, e13 = e[0] + e[2], e[1] + e[3]
    fd, fs = C2 * (f[1] - f[3]), C2 * (f[1] + f[3])
    d = [None] + [b[p] - b[8 - p] for p in (1, 2, 3)]
    g = [None] + [b[p] + b[8 - p] for p in (1, 2, 3)]
    d2, g2 = C2 * d[2], C2 * g[2]
    re1, re3 = C1 * d[1] + C3 * d[3], C3 * d[1] - C1 * d[3]
    im1, im3 = C3 * g[1] + C1 * g[3], C1 * g[1] - C3 * g[3]
    up, down = b[0] + d2, b[0] - d2
    bp, bm = b[4] + g2, b[4] - g2
    return [
        (e02 + e13, None),
        (up + re1, -(bp + im1)),
        (f[0] + fd, -(f[2] + fs)),
        (down + re3, bm - im3),
        (e[0] - e[2], e[3] - e[1]),
        (down - re3, -(bm + im3)),
        (f[0] - fd, f[2] - fs),
        (up - re1, bp - im1),
        (e02 - e13, None),
    ]


def last_stage(u):
    re = [pair[0] for pair in u]
    im = [pair[1] for pair in u]
    sum08, dif08 = re[0] + re[8], re[0] - re[8]
    r26, i26 = re[2] + re[6], im[2] - im[6]
    rd, sd = C2 * (re[2] - re[6]), C2 * (im[2] + im[6])
    top, low = sum08 + re[4], sum08 - re[4]
    dp, dm = dif08 + rd, dif08 - rd
    ip, im4 = sd + im[4], sd - im[4]
    even = [
        top + r26,
        dp - ip,
        low - i26,
        dm - im4,
        top - r26,
        dm + im4,
        low + i26,
        dp + ip,
    ]
    a1p, a1m = re[1] + re[7], re[1] - re[7]
    a3p, a3m = re[3] + re[5], re[3] - re[5]
    j1p, j1m = im[1] + im[7], im[1] - im[7]
    j3p, j3m = im[3] + im[5], im[3] - im[5]
    c1, c3 = C1 * a1m + C3 * a3m, C3 * a1m - C1 * a3m
    c2 = C2 * (a1p - a3p)
    s1, s3 = C3 * j1p + C1 * j3p, C1 * j1p - C3 * j3p
    s2 = C2 * (j1m + j3m)
    odd = [
        a1p + a3p,
        c1 - s1,
        c2 - s2,
        c3 - s3,
        j3m - j1m,
        -(c3 + s3),
        -(c2 + s2),
        -(c1 + s1),
    ]
    return [x + y for x, y in zip(even, odd)]


def rows_loop(rows, body):
    @pl.loop(0, rows // TILE)
    def _(step):
        body(pl.ds(pl.multiple_of(step * TILE, TILE), TILE))


def split_rows(load, mid, rows, width):
    def body(at):
        for r, pair in enumerate(first_stage([load(p, at) for p in range(BLOCKS)])):
            mid[r, at, :width] = pair[0].astype(jnp.bfloat16)
            if pair[1] is not None:
                mid[r, at, width:] = pair[1].astype(jnp.bfloat16)

    rows_loop(rows, body)


def spectrum(mid, table, r, width):
    if r in (0, GROUPS - 1):
        return jnp.dot(mid[r, :, :width], table[r, :width, :], preferred_element_type=jnp.float32)
    return jnp.dot(mid[r], table[r], preferred_element_type=jnp.float32)


def invert_group(product, table, r, width, wide):
    if r in (0, GROUPS - 1):
        wide[r, :, :width] = jnp.dot(product, table[r, :, :width], preferred_element_type=jnp.float32)
    else:
        wide[r] = jnp.dot(product, table[r], preferred_element_type=jnp.float32)


def merge_rows(wide, store, rows, width):
    def body(at):
        parts = []
        for r in range(GROUPS):
            im = None if r in (0, GROUPS - 1) else wide[r, at, width:]
            parts.append((wide[r, at, :width], im))
        for p, value in enumerate(last_stage(parts)):
            store(p, at, value)

    rows_loop(rows, body)


def piece_at(ref, where, k, rows):
    start = pl.multiple_of(lax.bitwise_xor(where[0], k) * rows, rows)
    return ref.at[pl.ds(start, rows), :]


def gate_kernel(order, where, gate, upper, whole, *refs):
    outs, picks, refs = refs[: len(order)], refs[len(order) : 2 * len(order)], refs[2 * len(order) :]
    left, right, sems, pick_sems = refs
    rows = outs[0].shape[0]
    loads, moves = [], []
    for i, k in enumerate(order):
        pair = (
            pltpu.make_async_copy(piece_at(gate, where, k, rows), left.at[i], sems.at[0, i]),
            pltpu.make_async_copy(piece_at(upper, where, k, rows), right.at[i], sems.at[1, i]),
        )
        for copy in pair:
            copy.start()
        loads.append(pair)
    for i, k in enumerate(order):
        moves.append(pltpu.make_async_copy(piece_at(whole, where, k, rows), picks[i], pick_sems.at[i]))
        moves[-1].start()
    for i, out in enumerate(outs):
        for copy in loads[i]:
            copy.wait()
        out[...] = (left[i].astype(jnp.float32) * right[i].astype(jnp.float32)).astype(jnp.bfloat16)
    for copy in moves:
        copy.wait()


def place_kernel(order, where, *refs):
    pieces, whole = refs[:-1], refs[-1]
    for k, piece in zip(order, pieces):
        whole[lax.bitwise_xor(where[0], k)] = piece[...]


def taps_kernel(taps, forward, taps_spec, mid):
    rows, width = (taps.shape[0], taps.shape[1] // BLOCKS)
    split_rows(lambda p, at: taps[at, p * width : (p + 1) * width], mid, rows, width)
    for r in range(GROUPS):
        taps_spec[r] = spectrum(mid, forward, r, width).astype(taps_spec.dtype)


def ordered(order, where, refs, held):
    span = refs[0].shape[1]
    for k, ref in zip(order, refs):
        start = pl.multiple_of(lax.bitwise_xor(where[0], k) * span, span)
        held[:, pl.ds(start, span)] = ref[...]


def block_of(held, width):
    return lambda p, at: held[at, p * width : (p + 1) * width].astype(jnp.float32)


def block_into(held, width):
    def store(p, at, value):
        held[at, p * width : (p + 1) * width] = value.astype(jnp.bfloat16)

    return store


def back_kernel(order, back_order, late, where, *refs):
    blocks, refs = refs[: len(order)], refs[len(order) + late :]
    taps_spec, forward, backward, *outs, grad_spec, held, mid, wide = refs
    outs = outs[late:]
    rows, width = held.shape[0], held.shape[1] // BLOCKS
    ordered(order, where, blocks, held)
    split_rows(block_of(held, width), mid, rows, width)
    for r in range(GROUPS):
        grad = spectrum(mid, forward, r, width)
        grad_spec[r] = grad.astype(grad_spec.dtype)
        taps = taps_spec[r].astype(jnp.float32)
        gr, gi, hr, hi = grad[:, :width], grad[:, width:], taps[:, :width], taps[:, width:]
        product = jnp.concatenate([hr * gr + hi * gi, hr * gi - hi * gr], axis=1)
        invert_group(product.astype(jnp.bfloat16), backward, r, width, wide)
    merge_rows(wide, block_into(held, width), rows, width)
    span = outs[0].shape[1]
    for k, out in zip(back_order, outs):
        start = pl.multiple_of(lax.bitwise_xor(where[0], k) * span, span)
        out[...] = held[:, pl.ds(start, span)]


def cross_kernel(order, where, *refs):
    blocks, refs = refs[: len(order)], refs[len(order) :]
    grad_spec, forward, backward, *outs, held, mid, wide = refs
    rows, width = held.shape[0], held.shape[1] // BLOCKS
    ordered(order, where, blocks, held)
    split_rows(block_of(held, width), mid, rows, width)
    for r in range(GROUPS):
        signal = spectrum(mid, forward, r, width)
        grad = grad_spec[r].astype(jnp.float32)
        gr, gi, xr, xi = grad[:, :width], grad[:, width:], signal[:, :width], signal[:, width:]
        product = jnp.concatenate([gr * xr + gi * xi, gi * xr - gr * xi], axis=1)
        invert_group(product.astype(jnp.bfloat16), backward, r, width, wide)
    merge_rows(wide, block_into(held, width), rows, width)
    part = held.shape[1] // len(outs)
    for k, out in zip(far_first(len(outs)), outs):
        start = pl.multiple_of(lax.bitwise_xor(where[1], k) * part, part)
        out[...] = held[:, pl.ds(start, part)]


def call(kernel, operands, outs, scratch=(), flops=0, streams=(), out_streams=(), aliases=None, hbm=()):
    def spec(stream):
        return pl.BlockSpec(memory_space=pl.ANY if stream else pltpu.VMEM)

    size = sum(math.prod(o.shape) * o.dtype.itemsize for o in list(operands) + list(outs))
    specs = [spec(i in streams) for i in range(len(operands))]
    for i in hbm:
        specs[i] = pl.BlockSpec(memory_space=pltpu.HBM)
    if operands[0].dtype == jnp.int32:
        specs[0] = pl.BlockSpec(memory_space=pltpu.SMEM)
    outputs = pl.pallas_call(
        kernel,
        out_shape=list(outs),
        in_specs=specs,
        out_specs=[spec(i in out_streams) for i in range(len(outs))],
        scratch_shapes=list(scratch),
        input_output_aliases=aliases or {},
        compiler_params=pltpu.CompilerParams(vmem_limit_bytes=LIMIT),
        cost_estimate=pl.CostEstimate(flops=flops, bytes_accessed=size, transcendentals=0),
    )(*operands)
    return list(outputs)


def far_first(size):
    return [*range(size // 2, size), *range(1, size // 2), 0]


def mixed(size):
    far = far_first(size)
    return [k for pair in zip(far[: size // 2], far[size // 2 :]) for k in pair]


def back_mixed(size):
    half = size // 2
    pairs = [k for pair in zip(range(1, half), range(half, size)) for k in pair]
    return [*pairs[:-2], size - 2, size - 1, half - 1, 0]


def exchange(pieces, order, axis, size):
    moved = []
    for k, piece in zip(order, pieces):
        moved.append(lax.ppermute(piece, axis, [(i, i ^ k) for i in range(size)]) if k else piece)
    return moved


def on_device(saved_input, out_gate, grad_out, long_filter):
    count, shares = lax.axis_size("ctx"), lax.axis_size("dp")
    channels, span = saved_input.shape[1:]
    rows, length = long_filter.shape
    width = length // BLOCKS
    order, back_order, late = mixed(count), back_mixed(count), 2
    at = count - 1 - late
    every = range(count + 8)
    where = jnp.stack([lax.axis_index("ctx"), lax.axis_index("dp")]).astype(jnp.int32)
    forward, backward = (jnp.asarray(t) for t in transform_tables(width))
    half, full = jnp.bfloat16, jnp.float32
    piece = jax.ShapeDtypeStruct((rows, span), half)
    spec = jax.ShapeDtypeStruct((GROUPS, rows, 2 * width), half)
    held = pltpu.VMEM((rows, length), half)
    mid = pltpu.VMEM((GROUPS, rows, 2 * width), half)
    wide = pltpu.VMEM((GROUPS, rows, 2 * width), full)
    slots = pltpu.VMEM((count, rows, span), half)
    sems = pltpu.SemaphoreType.DMA
    work = 2 * GROUPS * rows * 4 * width * width

    pieces = call(
        functools.partial(gate_kernel, order),
        [where, *(pltpu.with_memory_space_constraint(x[0], pltpu.HBM) for x in (out_gate, grad_out, saved_input))],
        [piece] * (2 * count),
        [slots, slots, sems((2, count)), sems((count,))],
        hbm=(1, 2, 3),
    )
    grad_pieces, input_pieces = pieces[:count], pieces[count:]
    grad_blocks = exchange(grad_pieces, order, "ctx", count)
    (taps_spec,) = call(taps_kernel, [long_filter, forward], [spec], [mid], flops=work)
    passed = [*input_pieces[at : at + late]]
    *back, grad_spec = call(
        functools.partial(back_kernel, order, back_order, late),
        [where, *grad_blocks, *passed, taps_spec, forward, backward],
        [piece] * (late + count) + [spec],
        [held, mid, wide],
        flops=2 * work,
        streams=range(1 + count, 1 + count + late),
        out_streams=range(late),
        aliases={1 + count + i: i for i in range(late)},
    )
    input_pieces[at : at + late], back = back[:late], back[late:]
    input_blocks = exchange(input_pieces, order, "ctx", count)
    back_blocks = exchange(back, back_order, "ctx", count)
    share = jax.ShapeDtypeStruct((rows, length // shares), half)
    cross = call(
        functools.partial(cross_kernel, order),
        [where, *input_blocks, grad_spec, forward, backward],
        [share] * shares,
        [held, mid, wide],
        flops=2 * work,
    )
    cross_blocks = exchange(cross, far_first(shares), "dp", shares)
    scale = 1.0 / math.sqrt(shares * length)
    grad_filter = sum(x.astype(full) for x in cross_blocks) * scale
    (whole,) = call(
        functools.partial(place_kernel, back_order),
        [where, *back_blocks],
        [jax.ShapeDtypeStruct((count, rows, span), half)],
    )
    return (whole.reshape(1, channels, span), grad_filter)


def solution(mesh):
    in_specs = (P("dp", None, "ctx"), P("dp", None, "ctx"), P("dp", None, "ctx"), P("ctx", None))
    out_specs = (P("dp", None, "ctx"), P("ctx", "dp"))
    return jax.shard_map(
        on_device, mesh=mesh, in_specs=in_specs, out_specs=out_specs, check_vma=False
    )
```

```python
import functools
import math

import jax
import jax.numpy as jnp
import ml_dtypes
import numpy as np
from jax import lax
from jax.experimental import pallas as pl
from jax.experimental.pallas import tpu as pltpu
from jax.sharding import PartitionSpec as P

BLOCKS = 8
GROUPS = 9
TILE = 16
C1 = math.cos(math.pi / 8)
C2 = math.cos(math.pi / 4)
C3 = math.cos(3 * math.pi / 8)
LIMIT = 32 * 1024 * 1024


def transform_tables(width):
    points = 2 * BLOCKS * width
    row = np.arange(width)
    forward = np.zeros((GROUPS, 2 * width, 2 * width), np.float64)
    for r in range(GROUPS):
        angle = 2.0 * np.pi * (np.outer(row, 16 * row + r) % points) / points
        cos, sin = np.cos(angle), np.sin(angle)
        forward[r] = np.block([[cos, -sin], [sin, cos]])
    scale = np.full((GROUPS, 1, 1), 2.0 / points)
    scale[0] = scale[-1] = 1.0 / points
    backward = np.swapaxes(forward, 1, 2) * scale
    return forward.astype(ml_dtypes.bfloat16), backward.astype(ml_dtypes.bfloat16)


def first_stage(b):
    e = [b[p] + b[p + 4] for p in range(4)]
    f = [b[p] - b[p + 4] for p in range(4)]
    e02, e13 = e[0] + e[2], e[1] + e[3]
    fd, fs = C2 * (f[1] - f[3]), C2 * (f[1] + f[3])
    d = [None] + [b[p] - b[8 - p] for p in (1, 2, 3)]
    g = [None] + [b[p] + b[8 - p] for p in (1, 2, 3)]
    d2, g2 = C2 * d[2], C2 * g[2]
    re1, re3 = C1 * d[1] + C3 * d[3], C3 * d[1] - C1 * d[3]
    im1, im3 = C3 * g[1] + C1 * g[3], C1 * g[1] - C3 * g[3]
    up, down = b[0] + d2, b[0] - d2
    bp, bm = b[4] + g2, b[4] - g2
    return [
        (e02 + e13, None),
        (up + re1, -(bp + im1)),
        (f[0] + fd, -(f[2] + fs)),
        (down + re3, bm - im3),
        (e[0] - e[2], e[3] - e[1]),
        (down - re3, -(bm + im3)),
        (f[0] - fd, f[2] - fs),
        (up - re1, bp - im1),
        (e02 - e13, None),
    ]


def last_stage(u):
    re = [pair[0] for pair in u]
    im = [pair[1] for pair in u]
    sum08, dif08 = re[0] + re[8], re[0] - re[8]
    r26, i26 = re[2] + re[6], im[2] - im[6]
    rd, sd = C2 * (re[2] - re[6]), C2 * (im[2] + im[6])
    top, low = sum08 + re[4], sum08 - re[4]
    dp, dm = dif08 + rd, dif08 - rd
    ip, im4 = sd + im[4], sd - im[4]
    even = [
        top + r26,
        dp - ip,
        low - i26,
        dm - im4,
        top - r26,
        dm + im4,
        low + i26,
        dp + ip,
    ]
    a1p, a1m = re[1] + re[7], re[1] - re[7]
    a3p, a3m = re[3] + re[5], re[3] - re[5]
    j1p, j1m = im[1] + im[7], im[1] - im[7]
    j3p, j3m = im[3] + im[5], im[3] - im[5]
    c1, c3 = C1 * a1m + C3 * a3m, C3 * a1m - C1 * a3m
    c2 = C2 * (a1p - a3p)
    s1, s3 = C3 * j1p + C1 * j3p, C1 * j1p - C3 * j3p
    s2 = C2 * (j1m + j3m)
    odd = [
        a1p + a3p,
        c1 - s1,
        c2 - s2,
        c3 - s3,
        j3m - j1m,
        -(c3 + s3),
        -(c2 + s2),
        -(c1 + s1),
    ]
    return [x + y for x, y in zip(even, odd)]


def rows_loop(rows, body):
    @pl.loop(0, rows // TILE)
    def _(step):
        body(pl.ds(pl.multiple_of(step * TILE, TILE), TILE))


def split_rows(load, mid, rows, width):
    def body(at):
        for r, pair in enumerate(first_stage([load(p, at) for p in range(BLOCKS)])):
            mid[r, at, :width] = pair[0].astype(jnp.bfloat16)
            if pair[1] is not None:
                mid[r, at, width:] = pair[1].astype(jnp.bfloat16)

    rows_loop(rows, body)


def spectrum(mid, table, r, width):
    if r in (0, GROUPS - 1):
        return jnp.dot(mid[r, :, :width], table[r, :width, :], preferred_element_type=jnp.float32)
    return jnp.dot(mid[r], table[r], preferred_element_type=jnp.float32)


def invert_group(product, table, r, width, wide):
    if r in (0, GROUPS - 1):
        wide[r, :, :width] = jnp.dot(product, table[r, :, :width], preferred_element_type=jnp.float32)
    else:
        wide[r] = jnp.dot(product, table[r], preferred_element_type=jnp.float32)


def merge_rows(wide, store, rows, width):
    def body(at):
        parts = []
        for r in range(GROUPS):
            im = None if r in (0, GROUPS - 1) else wide[r, at, width:]
            parts.append((wide[r, at, :width], im))
        for p, value in enumerate(last_stage(parts)):
            store(p, at, value)

    rows_loop(rows, body)


def piece_at(ref, where, k, rows):
    start = pl.multiple_of(lax.bitwise_xor(where[0], k) * rows, rows)
    return ref.at[pl.ds(start, rows), :]


def gate_kernel(order, where, gate, upper, *refs):
    outs, (left, right, sems) = refs[: len(order)], refs[len(order) :]
    rows = outs[0].shape[0]
    loads = []
    for i, k in enumerate(order):
        pair = (
            pltpu.make_async_copy(piece_at(gate, where, k, rows), left.at[i], sems.at[0, i]),
            pltpu.make_async_copy(piece_at(upper, where, k, rows), right.at[i], sems.at[1, i]),
        )
        for copy in pair:
            copy.start()
        loads.append(pair)
    for i, out in enumerate(outs):
        for copy in loads[i]:
            copy.wait()
        out[...] = (left[i].astype(jnp.float32) * right[i].astype(jnp.float32)).astype(jnp.bfloat16)


def place_kernel(order, where, *refs):
    pieces, whole = refs[:-1], refs[-1]
    for k, piece in zip(order, pieces):
        whole[lax.bitwise_xor(where[0], k)] = piece[...]


def taps_kernel(taps, forward, taps_spec, mid):
    rows, width = (taps.shape[0], taps.shape[1] // BLOCKS)
    split_rows(lambda p, at: taps[at, p * width : (p + 1) * width], mid, rows, width)
    for r in range(GROUPS):
        taps_spec[r] = spectrum(mid, forward, r, width).astype(taps_spec.dtype)


def ordered(order, where, refs, held):
    span = refs[0].shape[1]
    for k, ref in zip(order, refs):
        start = pl.multiple_of(lax.bitwise_xor(where[0], k) * span, span)
        held[:, pl.ds(start, span)] = ref[...]


def block_of(held, width):
    return lambda p, at: held[at, p * width : (p + 1) * width].astype(jnp.float32)


def block_into(held, width):
    def store(p, at, value):
        held[at, p * width : (p + 1) * width] = value.astype(jnp.bfloat16)

    return store


def back_kernel(order, back_order, where, *refs):
    blocks, refs = refs[: len(order)], refs[len(order) :]
    taps_spec, forward, backward, *outs, grad_spec, held, mid, wide = refs
    rows, width = held.shape[0], held.shape[1] // BLOCKS
    ordered(order, where, blocks, held)
    split_rows(block_of(held, width), mid, rows, width)
    for r in range(GROUPS):
        grad = spectrum(mid, forward, r, width)
        grad_spec[r] = grad.astype(grad_spec.dtype)
        taps = taps_spec[r].astype(jnp.float32)
        gr, gi, hr, hi = grad[:, :width], grad[:, width:], taps[:, :width], taps[:, width:]
        product = jnp.concatenate([hr * gr + hi * gi, hr * gi - hi * gr], axis=1)
        invert_group(product.astype(jnp.bfloat16), backward, r, width, wide)
    merge_rows(wide, block_into(held, width), rows, width)
    span = outs[0].shape[1]
    for k, out in zip(back_order, outs):
        start = pl.multiple_of(lax.bitwise_xor(where[0], k) * span, span)
        out[...] = held[:, pl.ds(start, span)]


def cross_kernel(where, blocks, grad_spec, forward, backward, *refs):
    *outs, held, mid, wide = refs
    rows, width = held.shape[0], held.shape[1] // BLOCKS
    span = blocks.shape[2]
    for p in range(blocks.shape[0]):
        held[:, p * span : (p + 1) * span] = blocks[p]
    split_rows(block_of(held, width), mid, rows, width)
    for r in range(GROUPS):
        signal = spectrum(mid, forward, r, width)
        grad = grad_spec[r].astype(jnp.float32)
        gr, gi, xr, xi = grad[:, :width], grad[:, width:], signal[:, :width], signal[:, width:]
        product = jnp.concatenate([gr * xr + gi * xi, gi * xr - gr * xi], axis=1)
        invert_group(product.astype(jnp.bfloat16), backward, r, width, wide)
    merge_rows(wide, block_into(held, width), rows, width)
    part = held.shape[1] // len(outs)
    for k, out in zip(far_first(len(outs)), outs):
        start = pl.multiple_of(lax.bitwise_xor(where[1], k) * part, part)
        out[...] = held[:, pl.ds(start, part)]


def call(kernel, operands, outs, scratch=(), flops=0, streams=()):
    size = sum(math.prod(o.shape) * o.dtype.itemsize for o in list(operands) + list(outs))
    specs = [pl.BlockSpec(memory_space=pl.ANY if i in streams else pltpu.VMEM) for i in range(len(operands))]
    if operands[0].dtype == jnp.int32:
        specs[0] = pl.BlockSpec(memory_space=pltpu.SMEM)
    outputs = pl.pallas_call(
        kernel,
        out_shape=list(outs),
        in_specs=specs,
        out_specs=[pl.BlockSpec(memory_space=pltpu.VMEM)] * len(outs),
        scratch_shapes=list(scratch),
        compiler_params=pltpu.CompilerParams(vmem_limit_bytes=LIMIT),
        cost_estimate=pl.CostEstimate(flops=flops, bytes_accessed=size, transcendentals=0),
    )(*operands)
    return list(outputs)


def far_first(size):
    return [*range(size // 2, size), *range(1, size // 2), 0]


def mixed(size):
    far = far_first(size)
    return [k for pair in zip(far[: size // 2], far[size // 2 :]) for k in pair]


def back_mixed(size):
    half = size // 2
    pairs = [k for pair in zip(range(1, half), range(half, size)) for k in pair]
    return [*pairs[:-2], size - 2, size - 1, half - 1, 0]


def exchange(pieces, order, axis, size):
    moved = []
    for k, piece in zip(order, pieces):
        moved.append(lax.ppermute(piece, axis, [(i, i ^ k) for i in range(size)]) if k else piece)
    return moved


def on_device(saved_input, out_gate, grad_out, long_filter):
    count, shares = lax.axis_size("ctx"), lax.axis_size("dp")
    channels, span = saved_input.shape[1:]
    rows, length = long_filter.shape
    width = length // BLOCKS
    order, back_order = mixed(count), back_mixed(count)
    every = range(count + 8)
    where = jnp.stack([lax.axis_index("ctx"), lax.axis_index("dp")]).astype(jnp.int32)
    forward, backward = (jnp.asarray(t) for t in transform_tables(width))
    half, full = jnp.bfloat16, jnp.float32
    piece = jax.ShapeDtypeStruct((rows, span), half)
    spec = jax.ShapeDtypeStruct((GROUPS, rows, 2 * width), half)
    held = pltpu.VMEM((rows, length), half)
    mid = pltpu.VMEM((GROUPS, rows, 2 * width), half)
    wide = pltpu.VMEM((GROUPS, rows, 2 * width), full)
    slots = pltpu.VMEM((count, rows, span), half)
    sems = pltpu.SemaphoreType.DMA
    work = 2 * GROUPS * rows * 4 * width * width

    grad_pieces = call(
        functools.partial(gate_kernel, order),
        [where, *(pltpu.with_memory_space_constraint(x[0], pltpu.HBM) for x in (out_gate, grad_out))],
        [piece] * count,
        [slots, slots, sems((2, count))],
        streams=(1, 2),
    )
    grad_blocks = exchange(grad_pieces, order, "ctx", count)
    whole_input = saved_input.reshape(count, rows, span)
    input_blocks = lax.all_to_all(whole_input, "ctx", split_axis=0, concat_axis=0, tiled=True)
    (taps_spec,) = call(taps_kernel, [long_filter, forward], [spec], [mid], flops=work)
    *back, grad_spec = call(
        functools.partial(back_kernel, order, back_order),
        [where, *grad_blocks, taps_spec, forward, backward],
        [piece] * count + [spec],
        [held, mid, wide],
        flops=2 * work,
    )
    back_blocks = exchange(back, back_order, "ctx", count)
    share = jax.ShapeDtypeStruct((rows, length // shares), half)
    cross = call(
        cross_kernel,
        [where, input_blocks, grad_spec, forward, backward],
        [share] * shares,
        [held, mid, wide],
        flops=2 * work,
    )
    cross_blocks = exchange(cross, far_first(shares), "dp", shares)
    scale = 1.0 / math.sqrt(shares * length)
    grad_filter = sum(x.astype(full) for x in cross_blocks) * scale
    (whole,) = call(
        functools.partial(place_kernel, back_order),
        [where, *back_blocks],
        [jax.ShapeDtypeStruct((count, rows, span), half)],
    )
    return (whole.reshape(1, channels, span), grad_filter)


def solution(mesh):
    in_specs = (P("dp", None, "ctx"), P("dp", None, "ctx"), P("dp", None, "ctx"), P("ctx", None))
    out_specs = (P("dp", None, "ctx"), P("ctx", "dp"))
    return jax.shard_map(
        on_device, mesh=mesh, in_specs=in_specs, out_specs=out_specs, check_vma=False
    )
```

```python
import functools
import math

import jax
import jax.numpy as jnp
import ml_dtypes
import numpy as np
from jax import lax
from jax.experimental import pallas as pl
from jax.experimental.pallas import tpu as pltpu
from jax.sharding import PartitionSpec as P

BLOCKS = 8
GROUPS = 9
TILE = 16
C1 = math.cos(math.pi / 8)
C2 = math.cos(math.pi / 4)
C3 = math.cos(3 * math.pi / 8)
LIMIT = 32 * 1024 * 1024


def transform_tables(width):
    points = 2 * BLOCKS * width
    row = np.arange(width)
    forward = np.zeros((GROUPS, 2 * width, 2 * width), np.float64)
    for r in range(GROUPS):
        angle = 2.0 * np.pi * (np.outer(row, 16 * row + r) % points) / points
        cos, sin = np.cos(angle), np.sin(angle)
        forward[r] = np.block([[cos, -sin], [sin, cos]])
    scale = np.full((GROUPS, 1, 1), 2.0 / points)
    scale[0] = scale[-1] = 1.0 / points
    backward = np.swapaxes(forward, 1, 2) * scale
    return forward.astype(ml_dtypes.bfloat16), backward.astype(ml_dtypes.bfloat16)


def first_stage(b):
    e = [b[p] + b[p + 4] for p in range(4)]
    f = [b[p] - b[p + 4] for p in range(4)]
    e02, e13 = e[0] + e[2], e[1] + e[3]
    fd, fs = C2 * (f[1] - f[3]), C2 * (f[1] + f[3])
    d = [None] + [b[p] - b[8 - p] for p in (1, 2, 3)]
    g = [None] + [b[p] + b[8 - p] for p in (1, 2, 3)]
    d2, g2 = C2 * d[2], C2 * g[2]
    re1, re3 = C1 * d[1] + C3 * d[3], C3 * d[1] - C1 * d[3]
    im1, im3 = C3 * g[1] + C1 * g[3], C1 * g[1] - C3 * g[3]
    up, down = b[0] + d2, b[0] - d2
    bp, bm = b[4] + g2, b[4] - g2
    return [
        (e02 + e13, None),
        (up + re1, -(bp + im1)),
        (f[0] + fd, -(f[2] + fs)),
        (down + re3, bm - im3),
        (e[0] - e[2], e[3] - e[1]),
        (down - re3, -(bm + im3)),
        (f[0] - fd, f[2] - fs),
        (up - re1, bp - im1),
        (e02 - e13, None),
    ]


def last_stage(u):
    re = [pair[0] for pair in u]
    im = [pair[1] for pair in u]
    sum08, dif08 = re[0] + re[8], re[0] - re[8]
    r26, i26 = re[2] + re[6], im[2] - im[6]
    rd, sd = C2 * (re[2] - re[6]), C2 * (im[2] + im[6])
    top, low = sum08 + re[4], sum08 - re[4]
    dp, dm = dif08 + rd, dif08 - rd
    ip, im4 = sd + im[4], sd - im[4]
    even = [
        top + r26,
        dp - ip,
        low - i26,
        dm - im4,
        top - r26,
        dm + im4,
        low + i26,
        dp + ip,
    ]
    a1p, a1m = re[1] + re[7], re[1] - re[7]
    a3p, a3m = re[3] + re[5], re[3] - re[5]
    j1p, j1m = im[1] + im[7], im[1] - im[7]
    j3p, j3m = im[3] + im[5], im[3] - im[5]
    c1, c3 = C1 * a1m + C3 * a3m, C3 * a1m - C1 * a3m
    c2 = C2 * (a1p - a3p)
    s1, s3 = C3 * j1p + C1 * j3p, C1 * j1p - C3 * j3p
    s2 = C2 * (j1m + j3m)
    odd = [
        a1p + a3p,
        c1 - s1,
        c2 - s2,
        c3 - s3,
        j3m - j1m,
        -(c3 + s3),
        -(c2 + s2),
        -(c1 + s1),
    ]
    return [x + y for x, y in zip(even, odd)]


def rows_loop(rows, body):
    @pl.loop(0, rows // TILE)
    def _(step):
        body(pl.ds(pl.multiple_of(step * TILE, TILE), TILE))


def split_rows(load, mid, rows, width):
    def body(at):
        for r, pair in enumerate(first_stage([load(p, at) for p in range(BLOCKS)])):
            mid[r, at, :width] = pair[0].astype(jnp.bfloat16)
            if pair[1] is not None:
                mid[r, at, width:] = pair[1].astype(jnp.bfloat16)

    rows_loop(rows, body)


def spectrum(mid, table, r, width):
    if r in (0, GROUPS - 1):
        return jnp.dot(mid[r, :, :width], table[r, :width, :], preferred_element_type=jnp.float32)
    return jnp.dot(mid[r], table[r], preferred_element_type=jnp.float32)


def invert_group(product, table, r, width, wide):
    if r in (0, GROUPS - 1):
        wide[r, :, :width] = jnp.dot(product, table[r, :, :width], preferred_element_type=jnp.float32)
    else:
        wide[r] = jnp.dot(product, table[r], preferred_element_type=jnp.float32)


def merge_rows(wide, store, rows, width):
    def body(at):
        parts = []
        for r in range(GROUPS):
            im = None if r in (0, GROUPS - 1) else wide[r, at, width:]
            parts.append((wide[r, at, :width], im))
        for p, value in enumerate(last_stage(parts)):
            store(p, at, value)

    rows_loop(rows, body)


def piece_at(ref, where, k, rows):
    start = pl.multiple_of(lax.bitwise_xor(where[0], k) * rows, rows)
    return ref.at[pl.ds(start, rows), :]


def gate_kernel(order, where, gate, upper, *refs):
    outs, (left, right, sems) = refs[: len(order)], refs[len(order) :]
    rows = outs[0].shape[0]
    loads = []
    for i, k in enumerate(order):
        pair = (
            pltpu.make_async_copy(piece_at(gate, where, k, rows), left.at[i], sems.at[0, i]),
            pltpu.make_async_copy(piece_at(upper, where, k, rows), right.at[i], sems.at[1, i]),
        )
        for copy in pair:
            copy.start()
        loads.append(pair)
    for i, out in enumerate(outs):
        for copy in loads[i]:
            copy.wait()
        out[...] = (left[i].astype(jnp.float32) * right[i].astype(jnp.float32)).astype(jnp.bfloat16)


def place_kernel(order, where, *refs):
    pieces, whole = refs[:-1], refs[-1]
    for k, piece in zip(order, pieces):
        whole[lax.bitwise_xor(where[0], k)] = piece[...]


def taps_kernel(taps, forward, taps_spec, mid):
    rows, width = (taps.shape[0], taps.shape[1] // BLOCKS)
    split_rows(lambda p, at: taps[at, p * width : (p + 1) * width], mid, rows, width)
    for r in range(GROUPS):
        taps_spec[r] = spectrum(mid, forward, r, width).astype(taps_spec.dtype)


def ordered(order, where, refs, held):
    span = refs[0].shape[1]
    for k, ref in zip(order, refs):
        start = pl.multiple_of(lax.bitwise_xor(where[0], k) * span, span)
        held[:, pl.ds(start, span)] = ref[...]


def block_of(held, width):
    return lambda p, at: held[at, p * width : (p + 1) * width].astype(jnp.float32)


def block_into(held, width):
    def store(p, at, value):
        held[at, p * width : (p + 1) * width] = value.astype(jnp.bfloat16)

    return store


def back_kernel(order, back_order, where, *refs):
    blocks, refs = refs[: len(order)], refs[len(order) :]
    taps_spec, forward, backward, *outs, grad_spec, held, mid, wide = refs
    rows, width = held.shape[0], held.shape[1] // BLOCKS
    ordered(order, where, blocks, held)
    split_rows(block_of(held, width), mid, rows, width)
    for r in range(GROUPS):
        grad = spectrum(mid, forward, r, width)
        grad_spec[r] = grad.astype(grad_spec.dtype)
        taps = taps_spec[r].astype(jnp.float32)
        gr, gi, hr, hi = grad[:, :width], grad[:, width:], taps[:, :width], taps[:, width:]
        product = jnp.concatenate([hr * gr + hi * gi, hr * gi - hi * gr], axis=1)
        invert_group(product.astype(jnp.bfloat16), backward, r, width, wide)
    merge_rows(wide, block_into(held, width), rows, width)
    span = outs[0].shape[1]
    for k, out in zip(back_order, outs):
        start = pl.multiple_of(lax.bitwise_xor(where[0], k) * span, span)
        out[...] = held[:, pl.ds(start, span)]


def cross_kernel(where, upper, lower, grad_spec, forward, backward, *refs):
    *outs, held, mid, wide = refs
    rows, width = held.shape[0], held.shape[1] // BLOCKS
    span = upper.shape[2]
    for p in range(upper.shape[0]):
        held[: rows // 2, p * span : (p + 1) * span] = upper[p]
        held[rows // 2 :, p * span : (p + 1) * span] = lower[p]
    split_rows(block_of(held, width), mid, rows, width)
    for r in range(GROUPS):
        signal = spectrum(mid, forward, r, width)
        grad = grad_spec[r].astype(jnp.float32)
        gr, gi, xr, xi = grad[:, :width], grad[:, width:], signal[:, :width], signal[:, width:]
        product = jnp.concatenate([gr * xr + gi * xi, gi * xr - gr * xi], axis=1)
        invert_group(product.astype(jnp.bfloat16), backward, r, width, wide)
    merge_rows(wide, block_into(held, width), rows, width)
    part = held.shape[1] // len(outs)
    for k, out in zip(far_first(len(outs)), outs):
        start = pl.multiple_of(lax.bitwise_xor(where[1], k) * part, part)
        out[...] = held[:, pl.ds(start, part)]


def call(kernel, operands, outs, scratch=(), flops=0, streams=()):
    size = sum(math.prod(o.shape) * o.dtype.itemsize for o in list(operands) + list(outs))
    specs = [pl.BlockSpec(memory_space=pl.ANY if i in streams else pltpu.VMEM) for i in range(len(operands))]
    if operands[0].dtype == jnp.int32:
        specs[0] = pl.BlockSpec(memory_space=pltpu.SMEM)
    outputs = pl.pallas_call(
        kernel,
        out_shape=list(outs),
        in_specs=specs,
        out_specs=[pl.BlockSpec(memory_space=pltpu.VMEM)] * len(outs),
        scratch_shapes=list(scratch),
        compiler_params=pltpu.CompilerParams(vmem_limit_bytes=LIMIT),
        cost_estimate=pl.CostEstimate(flops=flops, bytes_accessed=size, transcendentals=0),
    )(*operands)
    return list(outputs)


def far_first(size):
    return [*range(size // 2, size), *range(1, size // 2), 0]


def exchange(pieces, order, axis, size):
    moved = []
    for k, piece in zip(order, pieces):
        moved.append(lax.ppermute(piece, axis, [(i, i ^ k) for i in range(size)]) if k else piece)
    return moved


def on_device(saved_input, out_gate, grad_out, long_filter):
    count, shares = lax.axis_size("ctx"), lax.axis_size("dp")
    channels, span = saved_input.shape[1:]
    rows, length = long_filter.shape
    width = length // BLOCKS
    order, back_order = far_first(count), far_first(count)
    every = range(count + 8)
    where = jnp.stack([lax.axis_index("ctx"), lax.axis_index("dp")]).astype(jnp.int32)
    forward, backward = (jnp.asarray(t) for t in transform_tables(width))
    half, full = jnp.bfloat16, jnp.float32
    piece = jax.ShapeDtypeStruct((rows, span), half)
    spec = jax.ShapeDtypeStruct((GROUPS, rows, 2 * width), half)
    held = pltpu.VMEM((rows, length), half)
    mid = pltpu.VMEM((GROUPS, rows, 2 * width), half)
    wide = pltpu.VMEM((GROUPS, rows, 2 * width), full)
    slots = pltpu.VMEM((count, rows, span), half)
    sems = pltpu.SemaphoreType.DMA
    work = 2 * GROUPS * rows * 4 * width * width

    grad_pieces = call(
        functools.partial(gate_kernel, order),
        [where, *(pltpu.with_memory_space_constraint(x[0], pltpu.HBM) for x in (out_gate, grad_out))],
        [piece] * count,
        [slots, slots, sems((2, count))],
        streams=(1, 2),
    )
    grad_blocks = exchange(grad_pieces, order, "ctx", count)
    whole_input = saved_input.reshape(count, rows, span)
    input_parts = [
        lax.all_to_all(part, "ctx", split_axis=0, concat_axis=0, tiled=True)
        for part in (whole_input[:, : rows // 2], whole_input[:, rows // 2 :])
    ]
    (taps_spec,) = call(taps_kernel, [long_filter, forward], [spec], [mid], flops=work)
    *back, grad_spec = call(
        functools.partial(back_kernel, order, back_order),
        [where, *grad_blocks, taps_spec, forward, backward],
        [piece] * count + [spec],
        [held, mid, wide],
        flops=2 * work,
    )
    back_blocks = exchange(back, back_order, "ctx", count)
    share = jax.ShapeDtypeStruct((rows, length // shares), half)
    cross = call(
        cross_kernel,
        [where, *input_parts, grad_spec, forward, backward],
        [share] * shares,
        [held, mid, wide],
        flops=2 * work,
    )
    cross_blocks = exchange(cross, far_first(shares), "dp", shares)
    scale = 1.0 / math.sqrt(shares * length)
    grad_filter = sum(x.astype(full) for x in cross_blocks) * scale
    (whole,) = call(
        functools.partial(place_kernel, back_order),
        [where, *back_blocks],
        [jax.ShapeDtypeStruct((count, rows, span), half)],
    )
    return (whole.reshape(1, channels, span), grad_filter)


def solution(mesh):
    in_specs = (P("dp", None, "ctx"), P("dp", None, "ctx"), P("dp", None, "ctx"), P("ctx", None))
    out_specs = (P("dp", None, "ctx"), P("ctx", "dp"))
    return jax.shard_map(
        on_device, mesh=mesh, in_specs=in_specs, out_specs=out_specs, check_vma=False
    )
```

```python
import functools
import math

import jax
import jax.numpy as jnp
import ml_dtypes
import numpy as np
from jax import lax
from jax.experimental import pallas as pl
from jax.experimental.pallas import tpu as pltpu
from jax.sharding import PartitionSpec as P

BLOCKS = 8
GROUPS = 9
TILE = 16
C1 = math.cos(math.pi / 8)
C2 = math.cos(math.pi / 4)
C3 = math.cos(3 * math.pi / 8)
LIMIT = 32 * 1024 * 1024


def transform_tables(width):
    points = 2 * BLOCKS * width
    row = np.arange(width)
    forward = np.zeros((GROUPS, 2 * width, 2 * width), np.float64)
    for r in range(GROUPS):
        angle = 2.0 * np.pi * (np.outer(row, 16 * row + r) % points) / points
        cos, sin = np.cos(angle), np.sin(angle)
        forward[r] = np.block([[cos, -sin], [sin, cos]])
    scale = np.full((GROUPS, 1, 1), 2.0 / points)
    scale[0] = scale[-1] = 1.0 / points
    backward = np.swapaxes(forward, 1, 2) * scale
    return forward.astype(ml_dtypes.bfloat16), backward.astype(ml_dtypes.bfloat16)


def first_stage(b):
    e = [b[p] + b[p + 4] for p in range(4)]
    f = [b[p] - b[p + 4] for p in range(4)]
    e02, e13 = e[0] + e[2], e[1] + e[3]
    fd, fs = C2 * (f[1] - f[3]), C2 * (f[1] + f[3])
    d = [None] + [b[p] - b[8 - p] for p in (1, 2, 3)]
    g = [None] + [b[p] + b[8 - p] for p in (1, 2, 3)]
    d2, g2 = C2 * d[2], C2 * g[2]
    re1, re3 = C1 * d[1] + C3 * d[3], C3 * d[1] - C1 * d[3]
    im1, im3 = C3 * g[1] + C1 * g[3], C1 * g[1] - C3 * g[3]
    up, down = b[0] + d2, b[0] - d2
    bp, bm = b[4] + g2, b[4] - g2
    return [
        (e02 + e13, None),
        (up + re1, -(bp + im1)),
        (f[0] + fd, -(f[2] + fs)),
        (down + re3, bm - im3),
        (e[0] - e[2], e[3] - e[1]),
        (down - re3, -(bm + im3)),
        (f[0] - fd, f[2] - fs),
        (up - re1, bp - im1),
        (e02 - e13, None),
    ]


def last_stage(u):
    re = [pair[0] for pair in u]
    im = [pair[1] for pair in u]
    sum08, dif08 = re[0] + re[8], re[0] - re[8]
    r26, i26 = re[2] + re[6], im[2] - im[6]
    rd, sd = C2 * (re[2] - re[6]), C2 * (im[2] + im[6])
    top, low = sum08 + re[4], sum08 - re[4]
    dp, dm = dif08 + rd, dif08 - rd
    ip, im4 = sd + im[4], sd - im[4]
    even = [
        top + r26,
        dp - ip,
        low - i26,
        dm - im4,
        top - r26,
        dm + im4,
        low + i26,
        dp + ip,
    ]
    a1p, a1m = re[1] + re[7], re[1] - re[7]
    a3p, a3m = re[3] + re[5], re[3] - re[5]
    j1p, j1m = im[1] + im[7], im[1] - im[7]
    j3p, j3m = im[3] + im[5], im[3] - im[5]
    c1, c3 = C1 * a1m + C3 * a3m, C3 * a1m - C1 * a3m
    c2 = C2 * (a1p - a3p)
    s1, s3 = C3 * j1p + C1 * j3p, C1 * j1p - C3 * j3p
    s2 = C2 * (j1m + j3m)
    odd = [
        a1p + a3p,
        c1 - s1,
        c2 - s2,
        c3 - s3,
        j3m - j1m,
        -(c3 + s3),
        -(c2 + s2),
        -(c1 + s1),
    ]
    return [x + y for x, y in zip(even, odd)]


def rows_loop(rows, body):
    @pl.loop(0, rows // TILE)
    def _(step):
        body(pl.ds(pl.multiple_of(step * TILE, TILE), TILE))


def split_rows(load, mid, rows, width):
    def body(at):
        for r, pair in enumerate(first_stage([load(p, at) for p in range(BLOCKS)])):
            mid[r, at, :width] = pair[0].astype(jnp.bfloat16)
            if pair[1] is not None:
                mid[r, at, width:] = pair[1].astype(jnp.bfloat16)

    rows_loop(rows, body)


def spectrum(mid, table, r, width):
    if r in (0, GROUPS - 1):
        return jnp.dot(mid[r, :, :width], table[r, :width, :], preferred_element_type=jnp.float32)
    return jnp.dot(mid[r], table[r], preferred_element_type=jnp.float32)


def invert_group(product, table, r, width, wide):
    if r in (0, GROUPS - 1):
        wide[r, :, :width] = jnp.dot(product, table[r, :, :width], preferred_element_type=jnp.float32)
    else:
        wide[r] = jnp.dot(product, table[r], preferred_element_type=jnp.float32)


def merge_rows(wide, store, rows, width):
    def body(at):
        parts = []
        for r in range(GROUPS):
            im = None if r in (0, GROUPS - 1) else wide[r, at, width:]
            parts.append((wide[r, at, :width], im))
        for p, value in enumerate(last_stage(parts)):
            store(p, at, value)

    rows_loop(rows, body)


def piece_at(ref, where, k, rows):
    start = pl.multiple_of(lax.bitwise_xor(where[0], k) * rows, rows)
    return ref.at[pl.ds(start, rows), :]


def gate_kernel(order, input_order, where, gate, upper, whole, *refs):
    outs, picks, refs = refs[: len(order)], refs[len(order) : 2 * len(order)], refs[2 * len(order) :]
    left, right, sems, pick_sems = refs
    rows = outs[0].shape[0]
    loads, moves = [], []
    for i, k in enumerate(order):
        pair = (
            pltpu.make_async_copy(piece_at(gate, where, k, rows), left.at[i], sems.at[0, i]),
            pltpu.make_async_copy(piece_at(upper, where, k, rows), right.at[i], sems.at[1, i]),
        )
        for copy in pair:
            copy.start()
        loads.append(pair)
    for i, k in enumerate(input_order):
        moves.append(pltpu.make_async_copy(piece_at(whole, where, k, rows), picks[i], pick_sems.at[i]))
        moves[-1].start()
    for i, out in enumerate(outs):
        for copy in loads[i]:
            copy.wait()
        out[...] = (left[i].astype(jnp.float32) * right[i].astype(jnp.float32)).astype(jnp.bfloat16)
    for copy in moves:
        copy.wait()


def place_kernel(order, where, *refs):
    pieces, whole = refs[:-1], refs[-1]
    for k, piece in zip(order, pieces):
        whole[lax.bitwise_xor(where[0], k)] = piece[...]


def taps_kernel(taps, forward, taps_spec, mid):
    rows, width = (taps.shape[0], taps.shape[1] // BLOCKS)
    split_rows(lambda p, at: taps[at, p * width : (p + 1) * width], mid, rows, width)
    for r in range(GROUPS):
        taps_spec[r] = spectrum(mid, forward, r, width).astype(taps_spec.dtype)


def ordered(order, where, refs, held):
    span = refs[0].shape[1]
    for k, ref in zip(order, refs):
        start = pl.multiple_of(lax.bitwise_xor(where[0], k) * span, span)
        held[:, pl.ds(start, span)] = ref[...]


def block_of(held, width):
    return lambda p, at: held[at, p * width : (p + 1) * width].astype(jnp.float32)


def block_into(held, width):
    def store(p, at, value):
        held[at, p * width : (p + 1) * width] = value.astype(jnp.bfloat16)

    return store


def back_kernel(order, back_order, late, where, *refs):
    blocks, refs = refs[: len(order)], refs[len(order) + late :]
    taps_spec, forward, backward, *outs, grad_spec, held, mid, wide = refs
    outs = outs[late:]
    rows, width = held.shape[0], held.shape[1] // BLOCKS
    ordered(order, where, blocks, held)
    split_rows(block_of(held, width), mid, rows, width)
    for r in range(GROUPS):
        grad = spectrum(mid, forward, r, width)
        grad_spec[r] = grad.astype(grad_spec.dtype)
        taps = taps_spec[r].astype(jnp.float32)
        gr, gi, hr, hi = grad[:, :width], grad[:, width:], taps[:, :width], taps[:, width:]
        product = jnp.concatenate([hr * gr + hi * gi, hr * gi - hi * gr], axis=1)
        invert_group(product.astype(jnp.bfloat16), backward, r, width, wide)
    merge_rows(wide, block_into(held, width), rows, width)
    span = outs[0].shape[1]
    for k, out in zip(back_order, outs):
        start = pl.multiple_of(lax.bitwise_xor(where[0], k) * span, span)
        out[...] = held[:, pl.ds(start, span)]


def cross_kernel(order, where, *refs):
    blocks, refs = refs[: len(order)], refs[len(order) :]
    grad_spec, forward, backward, *outs, held, mid, wide = refs
    rows, width = held.shape[0], held.shape[1] // BLOCKS
    ordered(order, where, blocks, held)
    split_rows(block_of(held, width), mid, rows, width)
    for r in range(GROUPS):
        signal = spectrum(mid, forward, r, width)
        grad = grad_spec[r].astype(jnp.float32)
        gr, gi, xr, xi = grad[:, :width], grad[:, width:], signal[:, :width], signal[:, width:]
        product = jnp.concatenate([gr * xr + gi * xi, gi * xr - gr * xi], axis=1)
        invert_group(product.astype(jnp.bfloat16), backward, r, width, wide)
    merge_rows(wide, block_into(held, width), rows, width)
    part = held.shape[1] // len(outs)
    for k, out in zip(far_first(len(outs)), outs):
        start = pl.multiple_of(lax.bitwise_xor(where[1], k) * part, part)
        out[...] = held[:, pl.ds(start, part)]


def call(kernel, operands, outs, scratch=(), flops=0, streams=(), out_streams=(), aliases=None, hbm=()):
    def spec(stream):
        return pl.BlockSpec(memory_space=pl.ANY if stream else pltpu.VMEM)

    size = sum(math.prod(o.shape) * o.dtype.itemsize for o in list(operands) + list(outs))
    specs = [spec(i in streams) for i in range(len(operands))]
    for i in hbm:
        specs[i] = pl.BlockSpec(memory_space=pltpu.HBM)
    if operands[0].dtype == jnp.int32:
        specs[0] = pl.BlockSpec(memory_space=pltpu.SMEM)
    outputs = pl.pallas_call(
        kernel,
        out_shape=list(outs),
        in_specs=specs,
        out_specs=[spec(i in out_streams) for i in range(len(outs))],
        scratch_shapes=list(scratch),
        input_output_aliases=aliases or {},
        compiler_params=pltpu.CompilerParams(vmem_limit_bytes=LIMIT),
        cost_estimate=pl.CostEstimate(flops=flops, bytes_accessed=size, transcendentals=0),
    )(*operands)
    return list(outputs)


def far_first(size):
    return [*range(size // 2, size), *range(1, size // 2), 0]


def spread(size, order):
    part = size // 8
    return [k * part + i for k in order for i in range(part)] + [*range(1, part), 0]


def exchange(pieces, order, axis, size):
    moved = []
    for k, piece in zip(order, pieces):
        moved.append(lax.ppermute(piece, axis, [(i, i ^ k) for i in range(size)]) if k else piece)
    return moved


def on_device(saved_input, out_gate, grad_out, long_filter):
    count, shares = lax.axis_size("ctx"), lax.axis_size("dp")
    channels, span = saved_input.shape[1:]
    rows, length = long_filter.shape
    width = length // BLOCKS
    grad_order, input_order, back_order = (spread(count, o) for o in ((1, 2, 4, 5, 6, 7, 3), (4, 5, 1, 6, 2, 7, 3), (1, 2, 3, 4, 5, 6, 7)))
    late = 2
    at = count - 1 - late
    every = range(count + 8)
    where = jnp.stack([lax.axis_index("ctx"), lax.axis_index("dp")]).astype(jnp.int32)
    forward, backward = (jnp.asarray(t) for t in transform_tables(width))
    half, full = jnp.bfloat16, jnp.float32
    piece = jax.ShapeDtypeStruct((rows, span), half)
    spec = jax.ShapeDtypeStruct((GROUPS, rows, 2 * width), half)
    held = pltpu.VMEM((rows, length), half)
    mid = pltpu.VMEM((GROUPS, rows, 2 * width), half)
    wide = pltpu.VMEM((GROUPS, rows, 2 * width), full)
    slots = pltpu.VMEM((count, rows, span), half)
    sems = pltpu.SemaphoreType.DMA
    work = 2 * GROUPS * rows * 4 * width * width

    pieces = call(
        functools.partial(gate_kernel, grad_order, input_order),
        [where, *(pltpu.with_memory_space_constraint(x[0], pltpu.HBM) for x in (out_gate, grad_out, saved_input))],
        [piece] * (2 * count),
        [slots, slots, sems((2, count)), sems((count,))],
        hbm=(1, 2, 3),
    )
    grad_pieces, input_pieces = pieces[:count], pieces[count:]
    grad_blocks = exchange(grad_pieces, grad_order, "ctx", count)
    (taps_spec,) = call(taps_kernel, [long_filter, forward], [spec], [mid], flops=work)
    passed = [*input_pieces[at : at + late]]
    *back, grad_spec = call(
        functools.partial(back_kernel, grad_order, back_order, late),
        [where, *grad_blocks, *passed, taps_spec, forward, backward],
        [piece] * (late + count) + [spec],
        [held, mid, wide],
        flops=2 * work,
        streams=range(1 + count, 1 + count + late),
        out_streams=range(late),
        aliases={1 + count + i: i for i in range(late)},
    )
    input_pieces[at : at + late], back = back[:late], back[late:]
    input_blocks = exchange(input_pieces, input_order, "ctx", count)
    back_blocks = exchange(back, back_order, "ctx", count)
    share = jax.ShapeDtypeStruct((rows, length // shares), half)
    cross = call(
        functools.partial(cross_kernel, input_order),
        [where, *input_blocks, grad_spec, forward, backward],
        [share] * shares,
        [held, mid, wide],
        flops=2 * work,
    )
    cross_blocks = exchange(cross, far_first(shares), "dp", shares)
    scale = 1.0 / math.sqrt(shares * length)
    grad_filter = sum(x.astype(full) for x in cross_blocks) * scale
    (whole,) = call(
        functools.partial(place_kernel, back_order),
        [where, *back_blocks],
        [jax.ShapeDtypeStruct((count, rows, span), half)],
    )
    return (whole.reshape(1, channels, span), grad_filter)


def solution(mesh):
    in_specs = (P("dp", None, "ctx"), P("dp", None, "ctx"), P("dp", None, "ctx"), P("ctx", None))
    out_specs = (P("dp", None, "ctx"), P("ctx", "dp"))
    return jax.shard_map(
        on_device, mesh=mesh, in_specs=in_specs, out_specs=out_specs, check_vma=False
    )
```

```python
import functools
import math

import jax
import jax.numpy as jnp
import ml_dtypes
import numpy as np
from jax import lax
from jax.experimental import pallas as pl
from jax.experimental.pallas import tpu as pltpu
from jax.sharding import PartitionSpec as P

BLOCKS = 8
GROUPS = 9
TILE = 16
C1 = math.cos(math.pi / 8)
C2 = math.cos(math.pi / 4)
C3 = math.cos(3 * math.pi / 8)
LIMIT = 32 * 1024 * 1024


def transform_tables(width):
    points = 2 * BLOCKS * width
    row = np.arange(width)
    forward = np.zeros((GROUPS, 2 * width, 2 * width), np.float64)
    for r in range(GROUPS):
        angle = 2.0 * np.pi * (np.outer(row, 16 * row + r) % points) / points
        cos, sin = np.cos(angle), np.sin(angle)
        forward[r] = np.block([[cos, -sin], [sin, cos]])
    scale = np.full((GROUPS, 1, 1), 2.0 / points)
    scale[0] = scale[-1] = 1.0 / points
    backward = np.swapaxes(forward, 1, 2) * scale
    return forward.astype(ml_dtypes.bfloat16), backward.astype(ml_dtypes.bfloat16)


def first_stage(b):
    e = [b[p] + b[p + 4] for p in range(4)]
    f = [b[p] - b[p + 4] for p in range(4)]
    e02, e13 = e[0] + e[2], e[1] + e[3]
    fd, fs = C2 * (f[1] - f[3]), C2 * (f[1] + f[3])
    d = [None] + [b[p] - b[8 - p] for p in (1, 2, 3)]
    g = [None] + [b[p] + b[8 - p] for p in (1, 2, 3)]
    d2, g2 = C2 * d[2], C2 * g[2]
    re1, re3 = C1 * d[1] + C3 * d[3], C3 * d[1] - C1 * d[3]
    im1, im3 = C3 * g[1] + C1 * g[3], C1 * g[1] - C3 * g[3]
    up, down = b[0] + d2, b[0] - d2
    bp, bm = b[4] + g2, b[4] - g2
    return [
        (e02 + e13, None),
        (up + re1, -(bp + im1)),
        (f[0] + fd, -(f[2] + fs)),
        (down + re3, bm - im3),
        (e[0] - e[2], e[3] - e[1]),
        (down - re3, -(bm + im3)),
        (f[0] - fd, f[2] - fs),
        (up - re1, bp - im1),
        (e02 - e13, None),
    ]


def last_stage(u):
    re = [pair[0] for pair in u]
    im = [pair[1] for pair in u]
    sum08, dif08 = re[0] + re[8], re[0] - re[8]
    r26, i26 = re[2] + re[6], im[2] - im[6]
    rd, sd = C2 * (re[2] - re[6]), C2 * (im[2] + im[6])
    top, low = sum08 + re[4], sum08 - re[4]
    dp, dm = dif08 + rd, dif08 - rd
    ip, im4 = sd + im[4], sd - im[4]
    even = [
        top + r26,
        dp - ip,
        low - i26,
        dm - im4,
        top - r26,
        dm + im4,
        low + i26,
        dp + ip,
    ]
    a1p, a1m = re[1] + re[7], re[1] - re[7]
    a3p, a3m = re[3] + re[5], re[3] - re[5]
    j1p, j1m = im[1] + im[7], im[1] - im[7]
    j3p, j3m = im[3] + im[5], im[3] - im[5]
    c1, c3 = C1 * a1m + C3 * a3m, C3 * a1m - C1 * a3m
    c2 = C2 * (a1p - a3p)
    s1, s3 = C3 * j1p + C1 * j3p, C1 * j1p - C3 * j3p
    s2 = C2 * (j1m + j3m)
    odd = [
        a1p + a3p,
        c1 - s1,
        c2 - s2,
        c3 - s3,
        j3m - j1m,
        -(c3 + s3),
        -(c2 + s2),
        -(c1 + s1),
    ]
    return [x + y for x, y in zip(even, odd)]


def rows_loop(rows, body):
    @pl.loop(0, rows // TILE)
    def _(step):
        body(pl.ds(pl.multiple_of(step * TILE, TILE), TILE))


def split_rows(load, mid, rows, width):
    def body(at):
        for r, pair in enumerate(first_stage([load(p, at) for p in range(BLOCKS)])):
            mid[r, at, :width] = pair[0].astype(jnp.bfloat16)
            if pair[1] is not None:
                mid[r, at, width:] = pair[1].astype(jnp.bfloat16)

    rows_loop(rows, body)


def spectrum(mid, table, r, width):
    if r in (0, GROUPS - 1):
        return jnp.dot(mid[r, :, :width], table[r, :width, :], preferred_element_type=jnp.float32)
    return jnp.dot(mid[r], table[r], preferred_element_type=jnp.float32)


def invert_group(product, table, r, width, wide):
    if r in (0, GROUPS - 1):
        wide[r, :, :width] = jnp.dot(product, table[r, :, :width], preferred_element_type=jnp.float32)
    else:
        wide[r] = jnp.dot(product, table[r], preferred_element_type=jnp.float32)


def merge_rows(wide, store, rows, width):
    def body(at):
        parts = []
        for r in range(GROUPS):
            im = None if r in (0, GROUPS - 1) else wide[r, at, width:]
            parts.append((wide[r, at, :width], im))
        for p, value in enumerate(last_stage(parts)):
            store(p, at, value)

    rows_loop(rows, body)


def piece_at(ref, where, k, rows):
    start = pl.multiple_of(lax.bitwise_xor(where[0], k) * rows, rows)
    return ref.at[pl.ds(start, rows), :]


def gate_kernel(order, input_order, where, gate, upper, whole, *refs):
    outs, picks, refs = refs[: len(order)], refs[len(order) : 2 * len(order)], refs[2 * len(order) :]
    left, right, sems, pick_sems = refs
    rows = outs[0].shape[0]
    loads, moves = [], []
    for i, k in enumerate(order):
        pair = (
            pltpu.make_async_copy(piece_at(gate, where, k, rows), left.at[i], sems.at[0, i]),
            pltpu.make_async_copy(piece_at(upper, where, k, rows), right.at[i], sems.at[1, i]),
        )
        for copy in pair:
            copy.start()
        loads.append(pair)
    for i, k in enumerate(input_order):
        moves.append(pltpu.make_async_copy(piece_at(whole, where, k, rows), picks[i], pick_sems.at[i]))
        moves[-1].start()
    for i, out in enumerate(outs):
        for copy in loads[i]:
            copy.wait()
        out[...] = (left[i].astype(jnp.float32) * right[i].astype(jnp.float32)).astype(jnp.bfloat16)
    for copy in moves:
        copy.wait()


def place_kernel(order, where, *refs):
    pieces, whole = refs[:-1], refs[-1]
    for k, piece in zip(order, pieces):
        whole[lax.bitwise_xor(where[0], k)] = piece[...]


def taps_kernel(taps, forward, taps_spec, mid):
    rows, width = (taps.shape[0], taps.shape[1] // BLOCKS)
    split_rows(lambda p, at: taps[at, p * width : (p + 1) * width], mid, rows, width)
    for r in range(GROUPS):
        taps_spec[r] = spectrum(mid, forward, r, width).astype(taps_spec.dtype)


def ordered(order, where, refs, held):
    span = refs[0].shape[-1]
    for k, ref in zip(order, refs):
        other = lax.bitwise_xor(where[0], k)
        block = ref[...] if len(ref.shape) == 2 else ref[(other > where[0]).astype(jnp.int32)]
        held[:, pl.ds(pl.multiple_of(other * span, span), span)] = block


def block_of(held, width):
    return lambda p, at: held[at, p * width : (p + 1) * width].astype(jnp.float32)


def block_into(held, width):
    def store(p, at, value):
        held[at, p * width : (p + 1) * width] = value.astype(jnp.bfloat16)

    return store


def back_kernel(order, back_order, where, *refs):
    blocks, refs = refs[: len(order)], refs[len(order) :]
    taps_spec, forward, backward, *outs, grad_spec, held, mid, wide = refs
    rows, width = held.shape[0], held.shape[1] // BLOCKS
    ordered(order, where, blocks, held)
    split_rows(block_of(held, width), mid, rows, width)
    for r in range(GROUPS):
        grad = spectrum(mid, forward, r, width)
        grad_spec[r] = grad.astype(grad_spec.dtype)
        taps = taps_spec[r].astype(jnp.float32)
        gr, gi, hr, hi = grad[:, :width], grad[:, width:], taps[:, :width], taps[:, width:]
        product = jnp.concatenate([hr * gr + hi * gi, hr * gi - hi * gr], axis=1)
        invert_group(product.astype(jnp.bfloat16), backward, r, width, wide)
    merge_rows(wide, block_into(held, width), rows, width)
    span = outs[0].shape[1]
    for k, out in zip(back_order, outs):
        start = pl.multiple_of(lax.bitwise_xor(where[0], k) * span, span)
        out[...] = held[:, pl.ds(start, span)]


def cross_kernel(order, where, *refs):
    blocks, refs = refs[: len(order)], refs[len(order) :]
    grad_spec, forward, backward, *outs, held, mid, wide = refs
    rows, width = held.shape[0], held.shape[1] // BLOCKS
    ordered(order, where, blocks, held)
    split_rows(block_of(held, width), mid, rows, width)
    for r in range(GROUPS):
        signal = spectrum(mid, forward, r, width)
        grad = grad_spec[r].astype(jnp.float32)
        gr, gi, xr, xi = grad[:, :width], grad[:, width:], signal[:, :width], signal[:, width:]
        product = jnp.concatenate([gr * xr + gi * xi, gi * xr - gr * xi], axis=1)
        invert_group(product.astype(jnp.bfloat16), backward, r, width, wide)
    merge_rows(wide, block_into(held, width), rows, width)
    part = held.shape[1] // len(outs)
    for k, out in zip(far_first(len(outs)), outs):
        start = pl.multiple_of(lax.bitwise_xor(where[1], k) * part, part)
        out[...] = held[:, pl.ds(start, part)]


def call(kernel, operands, outs, scratch=(), flops=0, streams=(), out_streams=(), aliases=None, hbm=()):
    def spec(stream):
        return pl.BlockSpec(memory_space=pl.ANY if stream else pltpu.VMEM)

    size = sum(math.prod(o.shape) * o.dtype.itemsize for o in list(operands) + list(outs))
    specs = [spec(i in streams) for i in range(len(operands))]
    for i in hbm:
        specs[i] = pl.BlockSpec(memory_space=pltpu.HBM)
    if operands[0].dtype == jnp.int32:
        specs[0] = pl.BlockSpec(memory_space=pltpu.SMEM)
    outputs = pl.pallas_call(
        kernel,
        out_shape=list(outs),
        in_specs=specs,
        out_specs=[spec(i in out_streams) for i in range(len(outs))],
        scratch_shapes=list(scratch),
        input_output_aliases=aliases or {},
        compiler_params=pltpu.CompilerParams(vmem_limit_bytes=LIMIT),
        cost_estimate=pl.CostEstimate(flops=flops, bytes_accessed=size, transcendentals=0),
    )(*operands)
    return list(outputs)


def far_first(size):
    return [*range(size // 2, size), *range(1, size // 2), 0]


def spread(size, order):
    part = size // 8
    return [k * part + i for k in order for i in range(part)] + [*range(1, part), 0]


def exchange(pieces, order, axis, size):
    moved = []
    for k, piece in zip(order, pieces):
        moved.append(lax.ppermute(piece, axis, [(i, i ^ k) for i in range(size)]) if k else piece)
    return moved


def gather_pairs(pieces, order, axis, size):
    moved = []
    for k, piece in zip(order, pieces):
        pairs = [(i, i ^ k) for i in range(size) if i < i ^ k]
        moved.append(lax.all_gather(piece, axis, axis_index_groups=pairs, axis=0, tiled=False) if k else piece)
    return moved


def on_device(saved_input, out_gate, grad_out, long_filter):
    count, shares = lax.axis_size("ctx"), lax.axis_size("dp")
    channels, span = saved_input.shape[1:]
    rows, length = long_filter.shape
    width = length // BLOCKS
    grad_order, input_order, back_order = (spread(count, o) for o in ((4, 5, 6, 7, 1, 2, 3), (4, 5, 6, 7, 1, 2, 3), (6, 7, 3, 1, 2, 4, 5)))
    every = range(count + 8)
    where = jnp.stack([lax.axis_index("ctx"), lax.axis_index("dp")]).astype(jnp.int32)
    forward, backward = (jnp.asarray(t) for t in transform_tables(width))
    half, full = jnp.bfloat16, jnp.float32
    piece = jax.ShapeDtypeStruct((rows, span), half)
    spec = jax.ShapeDtypeStruct((GROUPS, rows, 2 * width), half)
    held = pltpu.VMEM((rows, length), half)
    mid = pltpu.VMEM((GROUPS, rows, 2 * width), half)
    wide = pltpu.VMEM((GROUPS, rows, 2 * width), full)
    slots = pltpu.VMEM((count, rows, span), half)
    sems = pltpu.SemaphoreType.DMA
    work = 2 * GROUPS * rows * 4 * width * width

    pieces = call(
        functools.partial(gate_kernel, grad_order, input_order),
        [where, *(pltpu.with_memory_space_constraint(x[0], pltpu.HBM) for x in (out_gate, grad_out, saved_input))],
        [piece] * (2 * count),
        [slots, slots, sems((2, count)), sems((count,))],
        hbm=(1, 2, 3),
    )
    grad_pieces, input_pieces = pieces[:count], pieces[count:]
    grad_blocks = exchange(grad_pieces, grad_order, "ctx", count)
    (taps_spec,) = call(taps_kernel, [long_filter, forward], [spec], [mid], flops=work)
    *back, grad_spec = call(
        functools.partial(back_kernel, grad_order, back_order),
        [where, *grad_blocks, taps_spec, forward, backward],
        [piece] * count + [spec],
        [held, mid, wide],
        flops=2 * work,
    )
    input_blocks = gather_pairs(input_pieces, input_order, "ctx", count)
    back_blocks = exchange(back, back_order, "ctx", count)
    share = jax.ShapeDtypeStruct((rows, length // shares), half)
    cross = call(
        functools.partial(cross_kernel, input_order),
        [where, *input_blocks, grad_spec, forward, backward],
        [share] * shares,
        [held, mid, wide],
        flops=2 * work,
    )
    cross_blocks = exchange(cross, far_first(shares), "dp", shares)
    scale = 1.0 / math.sqrt(shares * length)
    grad_filter = sum(x.astype(full) for x in cross_blocks) * scale
    (whole,) = call(
        functools.partial(place_kernel, back_order),
        [where, *back_blocks],
        [jax.ShapeDtypeStruct((count, rows, span), half)],
    )
    return (whole.reshape(1, channels, span), grad_filter)


def solution(mesh):
    in_specs = (P("dp", None, "ctx"), P("dp", None, "ctx"), P("dp", None, "ctx"), P("ctx", None))
    out_specs = (P("dp", None, "ctx"), P("ctx", "dp"))
    return jax.shard_map(
        on_device, mesh=mesh, in_specs=in_specs, out_specs=out_specs, check_vma=False
    )
```

```python
import functools
import math

import jax
import jax.numpy as jnp
import ml_dtypes
import numpy as np
from jax import lax
from jax.experimental import pallas as pl
from jax.experimental.pallas import tpu as pltpu
from jax.sharding import PartitionSpec as P

BLOCKS = 8
GROUPS = 9
TILE = 16
C1 = math.cos(math.pi / 8)
C2 = math.cos(math.pi / 4)
C3 = math.cos(3 * math.pi / 8)
LIMIT = 32 * 1024 * 1024


def transform_tables(width):
    points = 2 * BLOCKS * width
    row = np.arange(width)
    forward = np.zeros((GROUPS, 2 * width, 2 * width), np.float64)
    for r in range(GROUPS):
        angle = 2.0 * np.pi * (np.outer(row, 16 * row + r) % points) / points
        cos, sin = np.cos(angle), np.sin(angle)
        forward[r] = np.block([[cos, -sin], [sin, cos]])
    scale = np.full((GROUPS, 1, 1), 2.0 / points)
    scale[0] = scale[-1] = 1.0 / points
    backward = np.swapaxes(forward, 1, 2) * scale
    return forward.astype(ml_dtypes.bfloat16), backward.astype(ml_dtypes.bfloat16)


def first_stage(b):
    e = [b[p] + b[p + 4] for p in range(4)]
    f = [b[p] - b[p + 4] for p in range(4)]
    e02, e13 = e[0] + e[2], e[1] + e[3]
    fd, fs = C2 * (f[1] - f[3]), C2 * (f[1] + f[3])
    d = [None] + [b[p] - b[8 - p] for p in (1, 2, 3)]
    g = [None] + [b[p] + b[8 - p] for p in (1, 2, 3)]
    d2, g2 = C2 * d[2], C2 * g[2]
    re1, re3 = C1 * d[1] + C3 * d[3], C3 * d[1] - C1 * d[3]
    im1, im3 = C3 * g[1] + C1 * g[3], C1 * g[1] - C3 * g[3]
    up, down = b[0] + d2, b[0] - d2
    bp, bm = b[4] + g2, b[4] - g2
    return [
        (e02 + e13, None),
        (up + re1, -(bp + im1)),
        (f[0] + fd, -(f[2] + fs)),
        (down + re3, bm - im3),
        (e[0] - e[2], e[3] - e[1]),
        (down - re3, -(bm + im3)),
        (f[0] - fd, f[2] - fs),
        (up - re1, bp - im1),
        (e02 - e13, None),
    ]


def last_stage(u):
    re = [pair[0] for pair in u]
    im = [pair[1] for pair in u]
    sum08, dif08 = re[0] + re[8], re[0] - re[8]
    r26, i26 = re[2] + re[6], im[2] - im[6]
    rd, sd = C2 * (re[2] - re[6]), C2 * (im[2] + im[6])
    top, low = sum08 + re[4], sum08 - re[4]
    dp, dm = dif08 + rd, dif08 - rd
    ip, im4 = sd + im[4], sd - im[4]
    even = [
        top + r26,
        dp - ip,
        low - i26,
        dm - im4,
        top - r26,
        dm + im4,
        low + i26,
        dp + ip,
    ]
    a1p, a1m = re[1] + re[7], re[1] - re[7]
    a3p, a3m = re[3] + re[5], re[3] - re[5]
    j1p, j1m = im[1] + im[7], im[1] - im[7]
    j3p, j3m = im[3] + im[5], im[3] - im[5]
    c1, c3 = C1 * a1m + C3 * a3m, C3 * a1m - C1 * a3m
    c2 = C2 * (a1p - a3p)
    s1, s3 = C3 * j1p + C1 * j3p, C1 * j1p - C3 * j3p
    s2 = C2 * (j1m + j3m)
    odd = [
        a1p + a3p,
        c1 - s1,
        c2 - s2,
        c3 - s3,
        j3m - j1m,
        -(c3 + s3),
        -(c2 + s2),
        -(c1 + s1),
    ]
    return [x + y for x, y in zip(even, odd)]


def rows_loop(rows, body):
    @pl.loop(0, rows // TILE)
    def _(step):
        body(pl.ds(pl.multiple_of(step * TILE, TILE), TILE))


def split_rows(load, mid, rows, width):
    def body(at):
        for r, pair in enumerate(first_stage([load(p, at) for p in range(BLOCKS)])):
            mid[r, at, :width] = pair[0].astype(jnp.bfloat16)
            if pair[1] is not None:
                mid[r, at, width:] = pair[1].astype(jnp.bfloat16)

    rows_loop(rows, body)


def spectrum(mid, table, r, width):
    if r in (0, GROUPS - 1):
        return jnp.dot(mid[r, :, :width], table[r, :width, :], preferred_element_type=jnp.float32)
    return jnp.dot(mid[r], table[r], preferred_element_type=jnp.float32)


def invert_group(product, table, r, width, wide):
    if r in (0, GROUPS - 1):
        wide[r, :, :width] = jnp.dot(product, table[r, :, :width], preferred_element_type=jnp.float32)
    else:
        wide[r] = jnp.dot(product, table[r], preferred_element_type=jnp.float32)


def merge_rows(wide, store, rows, width):
    def body(at):
        parts = []
        for r in range(GROUPS):
            im = None if r in (0, GROUPS - 1) else wide[r, at, width:]
            parts.append((wide[r, at, :width], im))
        for p, value in enumerate(last_stage(parts)):
            store(p, at, value)

    rows_loop(rows, body)


def piece_at(ref, where, k, rows):
    start = pl.multiple_of(lax.bitwise_xor(where[0], k) * rows, rows)
    return ref.at[pl.ds(start, rows), :]


def gate_kernel(order, alone, where, gate, upper, whole, *refs):
    outs, picks, refs = refs[: len(order)], refs[len(order) : -4], refs[-4:]
    left, right, sems, pick_sems = refs
    rows = left.shape[1]
    loads, moves = [], []
    for i, k in enumerate(order):
        pair = (
            pltpu.make_async_copy(piece_at(gate, where, k, rows), left.at[i], sems.at[0, i]),
            pltpu.make_async_copy(piece_at(upper, where, k, rows), right.at[i], sems.at[1, i]),
        )
        for copy in pair:
            copy.start()
        loads.append(pair)
    for i, k in enumerate(order):
        target = picks[alone.index(k)] if k in alone else outs[i].at[1]
        moves.append(pltpu.make_async_copy(piece_at(whole, where, k, rows), target, pick_sems.at[i]))
        moves[-1].start()
    for i, k in enumerate(order):
        for copy in loads[i]:
            copy.wait()
        product = (left[i].astype(jnp.float32) * right[i].astype(jnp.float32)).astype(jnp.bfloat16)
        if k in alone:
            outs[i][...] = product
        else:
            outs[i][0] = product
    for copy in moves:
        copy.wait()


def place_kernel(order, where, *refs):
    pieces, whole = refs[:-1], refs[-1]
    for k, piece in zip(order, pieces):
        whole[lax.bitwise_xor(where[0], k)] = piece[...]


def taps_kernel(taps, forward, taps_spec, mid):
    rows, width = (taps.shape[0], taps.shape[1] // BLOCKS)
    split_rows(lambda p, at: taps[at, p * width : (p + 1) * width], mid, rows, width)
    for r in range(GROUPS):
        taps_spec[r] = spectrum(mid, forward, r, width).astype(taps_spec.dtype)


def ordered(order, part, where, refs, held):
    span = refs[0].shape[-1]
    for k, ref in zip(order, refs):
        start = pl.multiple_of(lax.bitwise_xor(where[0], k) * span, span)
        held[:, pl.ds(start, span)] = ref[...] if len(ref.shape) == 2 else ref[part]


def block_of(held, width):
    return lambda p, at: held[at, p * width : (p + 1) * width].astype(jnp.float32)


def block_into(held, width):
    def store(p, at, value):
        held[at, p * width : (p + 1) * width] = value.astype(jnp.bfloat16)

    return store


def back_kernel(order, back_order, where, *refs):
    blocks, refs = refs[: len(order)], refs[len(order) :]
    taps_spec, forward, backward, *outs, grad_spec, held, mid, wide = refs
    rows, width = held.shape[0], held.shape[1] // BLOCKS
    ordered(order, 0, where, blocks, held)
    split_rows(block_of(held, width), mid, rows, width)
    for r in range(GROUPS):
        grad = spectrum(mid, forward, r, width)
        grad_spec[r] = grad.astype(grad_spec.dtype)
        taps = taps_spec[r].astype(jnp.float32)
        gr, gi, hr, hi = grad[:, :width], grad[:, width:], taps[:, :width], taps[:, width:]
        product = jnp.concatenate([hr * gr + hi * gi, hr * gi - hi * gr], axis=1)
        invert_group(product.astype(jnp.bfloat16), backward, r, width, wide)
    merge_rows(wide, block_into(held, width), rows, width)
    span = outs[0].shape[1]
    for k, out in zip(back_order, outs):
        start = pl.multiple_of(lax.bitwise_xor(where[0], k) * span, span)
        out[...] = held[:, pl.ds(start, span)]


def cross_kernel(order, where, *refs):
    blocks, refs = refs[: len(order)], refs[len(order) :]
    grad_spec, forward, backward, *outs, held, mid, wide = refs
    rows, width = held.shape[0], held.shape[1] // BLOCKS
    ordered(order, 1, where, blocks, held)
    split_rows(block_of(held, width), mid, rows, width)
    for r in range(GROUPS):
        signal = spectrum(mid, forward, r, width)
        grad = grad_spec[r].astype(jnp.float32)
        gr, gi, xr, xi = grad[:, :width], grad[:, width:], signal[:, :width], signal[:, width:]
        product = jnp.concatenate([gr * xr + gi * xi, gi * xr - gr * xi], axis=1)
        invert_group(product.astype(jnp.bfloat16), backward, r, width, wide)
    merge_rows(wide, block_into(held, width), rows, width)
    part = held.shape[1] // len(outs)
    for k, out in zip(far_first(len(outs)), outs):
        start = pl.multiple_of(lax.bitwise_xor(where[1], k) * part, part)
        out[...] = held[:, pl.ds(start, part)]


def call(kernel, operands, outs, scratch=(), flops=0, streams=()):
    size = sum(math.prod(o.shape) * o.dtype.itemsize for o in list(operands) + list(outs))
    specs = [pl.BlockSpec(memory_space=pl.ANY if i in streams else pltpu.VMEM) for i in range(len(operands))]
    if operands[0].dtype == jnp.int32:
        specs[0] = pl.BlockSpec(memory_space=pltpu.SMEM)
    outputs = pl.pallas_call(
        kernel,
        out_shape=list(outs),
        in_specs=specs,
        out_specs=[pl.BlockSpec(memory_space=pltpu.VMEM)] * len(outs),
        scratch_shapes=list(scratch),
        compiler_params=pltpu.CompilerParams(vmem_limit_bytes=LIMIT),
        cost_estimate=pl.CostEstimate(flops=flops, bytes_accessed=size, transcendentals=0),
    )(*operands)
    return list(outputs)


def far_first(size):
    return [*range(size // 2, size), *range(1, size // 2), 0]


def spread(size, order):
    part = size // 8
    return [k * part + i for k in order for i in range(part)] + [*range(1, part), 0]


def exchange(pieces, order, axis, size):
    moved = []
    for k, piece in zip(order, pieces):
        moved.append(lax.ppermute(piece, axis, [(i, i ^ k) for i in range(size)]) if k else piece)
    return moved


def on_device(saved_input, out_gate, grad_out, long_filter):
    count, shares = lax.axis_size("ctx"), lax.axis_size("dp")
    channels, span = saved_input.shape[1:]
    rows, length = long_filter.shape
    width = length // BLOCKS
    order, back_order = (spread(count, o) for o in ((1, 6, 7, 4, 5, 2, 3), (1, 4, 5, 6, 7, 2, 3)))
    alone = spread(count, (6, 7))[: count // 4]
    where = jnp.stack([lax.axis_index("ctx"), lax.axis_index("dp")]).astype(jnp.int32)
    forward, backward = (jnp.asarray(t) for t in transform_tables(width))
    half, full = jnp.bfloat16, jnp.float32
    piece = jax.ShapeDtypeStruct((rows, span), half)
    spec = jax.ShapeDtypeStruct((GROUPS, rows, 2 * width), half)
    held = pltpu.VMEM((rows, length), half)
    mid = pltpu.VMEM((GROUPS, rows, 2 * width), half)
    wide = pltpu.VMEM((GROUPS, rows, 2 * width), full)
    slots = pltpu.VMEM((count, rows, span), half)
    sems = pltpu.SemaphoreType.DMA
    work = 2 * GROUPS * rows * 4 * width * width

    both = jax.ShapeDtypeStruct((2, rows, span), half)
    pieces = call(
        functools.partial(gate_kernel, order, alone),
        [where, *(pltpu.with_memory_space_constraint(x[0], pltpu.HBM) for x in (out_gate, grad_out, saved_input))],
        [piece if k in alone else both for k in order] + [piece] * len(alone),
        [slots, slots, sems((2, count)), sems((count,))],
        streams=(1, 2, 3),
    )
    grad_blocks = exchange(pieces[:count], order, "ctx", count)
    late_blocks = exchange(pieces[count:], alone, "ctx", count)
    (taps_spec,) = call(taps_kernel, [long_filter, forward], [spec], [mid], flops=work)
    *back, grad_spec = call(
        functools.partial(back_kernel, order, back_order),
        [where, *grad_blocks, taps_spec, forward, backward],
        [piece] * count + [spec],
        [held, mid, wide],
        flops=2 * work,
    )
    input_blocks = [late_blocks[alone.index(k)] if k in alone else both for k, both in zip(order, grad_blocks)]
    back_blocks = exchange(back, back_order, "ctx", count)
    share = jax.ShapeDtypeStruct((rows, length // shares), half)
    cross = call(
        functools.partial(cross_kernel, order),
        [where, *input_blocks, grad_spec, forward, backward],
        [share] * shares,
        [held, mid, wide],
        flops=2 * work,
    )
    cross_blocks = exchange(cross, far_first(shares), "dp", shares)
    scale = 1.0 / math.sqrt(shares * length)
    grad_filter = sum(x.astype(full) for x in cross_blocks) * scale
    (whole,) = call(
        functools.partial(place_kernel, back_order),
        [where, *back_blocks],
        [jax.ShapeDtypeStruct((count, rows, span), half)],
    )
    return (whole.reshape(1, channels, span), grad_filter)


def solution(mesh):
    in_specs = (P("dp", None, "ctx"), P("dp", None, "ctx"), P("dp", None, "ctx"), P("ctx", None))
    out_specs = (P("dp", None, "ctx"), P("ctx", "dp"))
    return jax.shard_map(
        on_device, mesh=mesh, in_specs=in_specs, out_specs=out_specs, check_vma=False
    )
```

```python
import functools
import math

import jax
import jax.numpy as jnp
import ml_dtypes
import numpy as np
from jax import lax
from jax.experimental import pallas as pl
from jax.experimental.pallas import tpu as pltpu
from jax.sharding import PartitionSpec as P

BLOCKS = 8
GROUPS = 9
TILE = 16
C1 = math.cos(math.pi / 8)
C2 = math.cos(math.pi / 4)
C3 = math.cos(3 * math.pi / 8)
LIMIT = 32 * 1024 * 1024


def transform_tables(width):
    points = 2 * BLOCKS * width
    row = np.arange(width)
    forward = np.zeros((GROUPS, 2 * width, 2 * width), np.float64)
    for r in range(GROUPS):
        angle = 2.0 * np.pi * (np.outer(row, 16 * row + r) % points) / points
        cos, sin = np.cos(angle), np.sin(angle)
        forward[r] = np.block([[cos, -sin], [sin, cos]])
    scale = np.full((GROUPS, 1, 1), 2.0 / points)
    scale[0] = scale[-1] = 1.0 / points
    backward = np.swapaxes(forward, 1, 2) * scale
    return forward.astype(ml_dtypes.bfloat16), backward.astype(ml_dtypes.bfloat16)


def first_stage(b):
    e = [b[p] + b[p + 4] for p in range(4)]
    f = [b[p] - b[p + 4] for p in range(4)]
    e02, e13 = e[0] + e[2], e[1] + e[3]
    fd, fs = C2 * (f[1] - f[3]), C2 * (f[1] + f[3])
    d = [None] + [b[p] - b[8 - p] for p in (1, 2, 3)]
    g = [None] + [b[p] + b[8 - p] for p in (1, 2, 3)]
    d2, g2 = C2 * d[2], C2 * g[2]
    re1, re3 = C1 * d[1] + C3 * d[3], C3 * d[1] - C1 * d[3]
    im1, im3 = C3 * g[1] + C1 * g[3], C1 * g[1] - C3 * g[3]
    up, down = b[0] + d2, b[0] - d2
    bp, bm = b[4] + g2, b[4] - g2
    return [
        (e02 + e13, None),
        (up + re1, -(bp + im1)),
        (f[0] + fd, -(f[2] + fs)),
        (down + re3, bm - im3),
        (e[0] - e[2], e[3] - e[1]),
        (down - re3, -(bm + im3)),
        (f[0] - fd, f[2] - fs),
        (up - re1, bp - im1),
        (e02 - e13, None),
    ]


def last_stage(u):
    re = [pair[0] for pair in u]
    im = [pair[1] for pair in u]
    sum08, dif08 = re[0] + re[8], re[0] - re[8]
    r26, i26 = re[2] + re[6], im[2] - im[6]
    rd, sd = C2 * (re[2] - re[6]), C2 * (im[2] + im[6])
    top, low = sum08 + re[4], sum08 - re[4]
    dp, dm = dif08 + rd, dif08 - rd
    ip, im4 = sd + im[4], sd - im[4]
    even = [
        top + r26,
        dp - ip,
        low - i26,
        dm - im4,
        top - r26,
        dm + im4,
        low + i26,
        dp + ip,
    ]
    a1p, a1m = re[1] + re[7], re[1] - re[7]
    a3p, a3m = re[3] + re[5], re[3] - re[5]
    j1p, j1m = im[1] + im[7], im[1] - im[7]
    j3p, j3m = im[3] + im[5], im[3] - im[5]
    c1, c3 = C1 * a1m + C3 * a3m, C3 * a1m - C1 * a3m
    c2 = C2 * (a1p - a3p)
    s1, s3 = C3 * j1p + C1 * j3p, C1 * j1p - C3 * j3p
    s2 = C2 * (j1m + j3m)
    odd = [
        a1p + a3p,
        c1 - s1,
        c2 - s2,
        c3 - s3,
        j3m - j1m,
        -(c3 + s3),
        -(c2 + s2),
        -(c1 + s1),
    ]
    return [x + y for x, y in zip(even, odd)]


def rows_loop(rows, body):
    @pl.loop(0, rows // TILE)
    def _(step):
        body(pl.ds(pl.multiple_of(step * TILE, TILE), TILE))


def split_rows(load, mid, rows, width):
    def body(at):
        for r, pair in enumerate(first_stage([load(p, at) for p in range(BLOCKS)])):
            mid[r, at, :width] = pair[0].astype(jnp.bfloat16)
            if pair[1] is not None:
                mid[r, at, width:] = pair[1].astype(jnp.bfloat16)

    rows_loop(rows, body)


def spectrum(mid, table, r, width):
    if r in (0, GROUPS - 1):
        return jnp.dot(mid[r, :, :width], table[r, :width, :], preferred_element_type=jnp.float32)
    return jnp.dot(mid[r], table[r], preferred_element_type=jnp.float32)


def invert_group(product, table, r, width, wide):
    if r in (0, GROUPS - 1):
        wide[r, :, :width] = jnp.dot(product, table[r, :, :width], preferred_element_type=jnp.float32)
    else:
        wide[r] = jnp.dot(product, table[r], preferred_element_type=jnp.float32)


def merge_rows(wide, store, rows, width):
    def body(at):
        parts = []
        for r in range(GROUPS):
            im = None if r in (0, GROUPS - 1) else wide[r, at, width:]
            parts.append((wide[r, at, :width], im))
        for p, value in enumerate(last_stage(parts)):
            store(p, at, value)

    rows_loop(rows, body)


def piece_at(ref, where, k, rows):
    start = pl.multiple_of(lax.bitwise_xor(where[0], k) * rows, rows)
    return ref.at[pl.ds(start, rows), :]


def gate_kernel(order, alone, where, gate, upper, whole, *refs):
    outs, picks, refs = refs[: len(order)], refs[len(order) : -4], refs[-4:]
    left, right, sems, pick_sems = refs
    rows = left.shape[1]
    loads, moves = [], []
    for i, k in enumerate(order):
        pair = (
            pltpu.make_async_copy(piece_at(gate, where, k, rows), left.at[i], sems.at[0, i]),
            pltpu.make_async_copy(piece_at(upper, where, k, rows), right.at[i], sems.at[1, i]),
        )
        for copy in pair:
            copy.start()
        loads.append(pair)
    for i, k in enumerate(order):
        target = picks[alone.index(k)] if k in alone else outs[i].at[1]
        moves.append(pltpu.make_async_copy(piece_at(whole, where, k, rows), target, pick_sems.at[i]))
        moves[-1].start()
    for i, k in enumerate(order):
        for copy in loads[i]:
            copy.wait()
        product = (left[i].astype(jnp.float32) * right[i].astype(jnp.float32)).astype(jnp.bfloat16)
        if k in alone:
            outs[i][...] = product
        else:
            outs[i][0] = product
    for copy in moves:
        copy.wait()


def place_kernel(order, where, *refs):
    pieces, whole = refs[:-1], refs[-1]
    for k, piece in zip(order, pieces):
        whole[lax.bitwise_xor(where[0], k)] = piece[...]


def taps_kernel(taps, forward, taps_spec, mid):
    rows, width = (taps.shape[0], taps.shape[1] // BLOCKS)
    split_rows(lambda p, at: taps[at, p * width : (p + 1) * width], mid, rows, width)
    for r in range(GROUPS):
        taps_spec[r] = spectrum(mid, forward, r, width).astype(taps_spec.dtype)


def ordered(order, part, where, refs, held):
    span = refs[0].shape[-1]
    for k, ref in zip(order, refs):
        start = pl.multiple_of(lax.bitwise_xor(where[0], k) * span, span)
        held[:, pl.ds(start, span)] = ref[...] if len(ref.shape) == 2 else ref[part]


def block_of(held, width):
    return lambda p, at: held[at, p * width : (p + 1) * width].astype(jnp.float32)


def block_into(held, width):
    def store(p, at, value):
        held[at, p * width : (p + 1) * width] = value.astype(jnp.bfloat16)

    return store


def back_kernel(order, back_order, where, *refs):
    blocks, refs = refs[: len(order)], refs[len(order) :]
    taps_spec, forward, backward, *outs, grad_spec, held, mid, wide = refs
    rows, width = held.shape[0], held.shape[1] // BLOCKS
    ordered(order, 0, where, blocks, held)
    split_rows(block_of(held, width), mid, rows, width)
    for r in range(GROUPS):
        grad = spectrum(mid, forward, r, width)
        grad_spec[r] = grad.astype(grad_spec.dtype)
        taps = taps_spec[r].astype(jnp.float32)
        gr, gi, hr, hi = grad[:, :width], grad[:, width:], taps[:, :width], taps[:, width:]
        product = jnp.concatenate([hr * gr + hi * gi, hr * gi - hi * gr], axis=1)
        invert_group(product.astype(jnp.bfloat16), backward, r, width, wide)
    merge_rows(wide, block_into(held, width), rows, width)
    span = outs[0].shape[1]
    for k, out in zip(back_order, outs):
        start = pl.multiple_of(lax.bitwise_xor(where[0], k) * span, span)
        out[...] = held[:, pl.ds(start, span)]


def cross_kernel(order, where, *refs):
    blocks, refs = refs[: len(order)], refs[len(order) :]
    grad_spec, forward, backward, *outs, held, mid, wide = refs
    rows, width = held.shape[0], held.shape[1] // BLOCKS
    ordered(order, 1, where, blocks, held)
    split_rows(block_of(held, width), mid, rows, width)
    for r in range(GROUPS):
        signal = spectrum(mid, forward, r, width)
        grad = grad_spec[r].astype(jnp.float32)
        gr, gi, xr, xi = grad[:, :width], grad[:, width:], signal[:, :width], signal[:, width:]
        product = jnp.concatenate([gr * xr + gi * xi, gi * xr - gr * xi], axis=1)
        invert_group(product.astype(jnp.bfloat16), backward, r, width, wide)
    merge_rows(wide, block_into(held, width), rows, width)
    part = held.shape[1] // len(outs)
    for k, out in zip(far_first(len(outs)), outs):
        start = pl.multiple_of(lax.bitwise_xor(where[1], k) * part, part)
        out[...] = held[:, pl.ds(start, part)]


def call(kernel, operands, outs, scratch=(), flops=0, streams=()):
    size = sum(math.prod(o.shape) * o.dtype.itemsize for o in list(operands) + list(outs))
    specs = [pl.BlockSpec(memory_space=pl.ANY if i in streams else pltpu.VMEM) for i in range(len(operands))]
    if operands[0].dtype == jnp.int32:
        specs[0] = pl.BlockSpec(memory_space=pltpu.SMEM)
    outputs = pl.pallas_call(
        kernel,
        out_shape=list(outs),
        in_specs=specs,
        out_specs=[pl.BlockSpec(memory_space=pltpu.VMEM)] * len(outs),
        scratch_shapes=list(scratch),
        compiler_params=pltpu.CompilerParams(vmem_limit_bytes=LIMIT),
        cost_estimate=pl.CostEstimate(flops=flops, bytes_accessed=size, transcendentals=0),
    )(*operands)
    return list(outputs)


def far_first(size):
    return [*range(size // 2, size), *range(1, size // 2), 0]


def spread(size, order):
    part = size // 8
    return [k * part + i for k in order for i in range(part)] + [*range(1, part), 0]


def exchange(pieces, order, axis, size):
    moved = []
    for k, piece in zip(order, pieces):
        moved.append(lax.ppermute(piece, axis, [(i, i ^ k) for i in range(size)]) if k else piece)
    return moved


def on_device(saved_input, out_gate, grad_out, long_filter):
    count, shares = lax.axis_size("ctx"), lax.axis_size("dp")
    channels, span = saved_input.shape[1:]
    rows, length = long_filter.shape
    width = length // BLOCKS
    order, back_order = (spread(count, o) for o in ((4, 1, 5, 2, 6, 7, 3), (1, 4, 2, 5, 6, 7, 3)))
    alone = spread(count, (4, 5, 6, 7))[: count // 2]
    where = jnp.stack([lax.axis_index("ctx"), lax.axis_index("dp")]).astype(jnp.int32)
    forward, backward = (jnp.asarray(t) for t in transform_tables(width))
    half, full = jnp.bfloat16, jnp.float32
    piece = jax.ShapeDtypeStruct((rows, span), half)
    spec = jax.ShapeDtypeStruct((GROUPS, rows, 2 * width), half)
    held = pltpu.VMEM((rows, length), half)
    mid = pltpu.VMEM((GROUPS, rows, 2 * width), half)
    wide = pltpu.VMEM((GROUPS, rows, 2 * width), full)
    slots = pltpu.VMEM((count, rows, span), half)
    sems = pltpu.SemaphoreType.DMA
    work = 2 * GROUPS * rows * 4 * width * width

    both = jax.ShapeDtypeStruct((2, rows, span), half)
    pieces = call(
        functools.partial(gate_kernel, order, alone),
        [where, *(pltpu.with_memory_space_constraint(x[0], pltpu.HBM) for x in (out_gate, grad_out, saved_input))],
        [piece if k in alone else both for k in order] + [piece] * len(alone),
        [slots, slots, sems((2, count)), sems((count,))],
        streams=(1, 2, 3),
    )
    grad_blocks = exchange(pieces[:count], order, "ctx", count)
    late_blocks = exchange(pieces[count:], alone, "ctx", count)
    (taps_spec,) = call(taps_kernel, [long_filter, forward], [spec], [mid], flops=work)
    *back, grad_spec = call(
        functools.partial(back_kernel, order, back_order),
        [where, *grad_blocks, taps_spec, forward, backward],
        [piece] * count + [spec],
        [held, mid, wide],
        flops=2 * work,
    )
    input_blocks = [late_blocks[alone.index(k)] if k in alone else both for k, both in zip(order, grad_blocks)]
    back_blocks = exchange(back, back_order, "ctx", count)
    share = jax.ShapeDtypeStruct((rows, length // shares), half)
    cross = call(
        functools.partial(cross_kernel, order),
        [where, *input_blocks, grad_spec, forward, backward],
        [share] * shares,
        [held, mid, wide],
        flops=2 * work,
    )
    cross_blocks = exchange(cross, far_first(shares), "dp", shares)
    scale = 1.0 / math.sqrt(shares * length)
    grad_filter = sum(x.astype(full) for x in cross_blocks) * scale
    (whole,) = call(
        functools.partial(place_kernel, back_order),
        [where, *back_blocks],
        [jax.ShapeDtypeStruct((count, rows, span), half)],
    )
    return (whole.reshape(1, channels, span), grad_filter)


def solution(mesh):
    in_specs = (P("dp", None, "ctx"), P("dp", None, "ctx"), P("dp", None, "ctx"), P("ctx", None))
    out_specs = (P("dp", None, "ctx"), P("ctx", "dp"))
    return jax.shard_map(
        on_device, mesh=mesh, in_specs=in_specs, out_specs=out_specs, check_vma=False
    )
```

```python
import functools
import math

import jax
import jax.numpy as jnp
import ml_dtypes
import numpy as np
from jax import lax
from jax.experimental import pallas as pl
from jax.experimental.pallas import tpu as pltpu
from jax.sharding import PartitionSpec as P

BLOCKS = 8
GROUPS = 9
TILE = 16
C1 = math.cos(math.pi / 8)
C2 = math.cos(math.pi / 4)
C3 = math.cos(3 * math.pi / 8)
LIMIT = 32 * 1024 * 1024


def transform_tables(width):
    points = 2 * BLOCKS * width
    row = np.arange(width)
    forward = np.zeros((GROUPS, 2 * width, 2 * width), np.float64)
    for r in range(GROUPS):
        angle = 2.0 * np.pi * (np.outer(row, 16 * row + r) % points) / points
        cos, sin = np.cos(angle), np.sin(angle)
        forward[r] = np.block([[cos, -sin], [sin, cos]])
    scale = np.full((GROUPS, 1, 1), 2.0 / points)
    scale[0] = scale[-1] = 1.0 / points
    backward = np.swapaxes(forward, 1, 2) * scale
    return forward.astype(ml_dtypes.bfloat16), backward.astype(ml_dtypes.bfloat16)


def first_stage(b):
    e = [b[p] + b[p + 4] for p in range(4)]
    f = [b[p] - b[p + 4] for p in range(4)]
    e02, e13 = e[0] + e[2], e[1] + e[3]
    fd, fs = C2 * (f[1] - f[3]), C2 * (f[1] + f[3])
    d = [None] + [b[p] - b[8 - p] for p in (1, 2, 3)]
    g = [None] + [b[p] + b[8 - p] for p in (1, 2, 3)]
    d2, g2 = C2 * d[2], C2 * g[2]
    re1, re3 = C1 * d[1] + C3 * d[3], C3 * d[1] - C1 * d[3]
    im1, im3 = C3 * g[1] + C1 * g[3], C1 * g[1] - C3 * g[3]
    up, down = b[0] + d2, b[0] - d2
    bp, bm = b[4] + g2, b[4] - g2
    return [
        (e02 + e13, None),
        (up + re1, -(bp + im1)),
        (f[0] + fd, -(f[2] + fs)),
        (down + re3, bm - im3),
        (e[0] - e[2], e[3] - e[1]),
        (down - re3, -(bm + im3)),
        (f[0] - fd, f[2] - fs),
        (up - re1, bp - im1),
        (e02 - e13, None),
    ]


def last_stage(u):
    re = [pair[0] for pair in u]
    im = [pair[1] for pair in u]
    sum08, dif08 = re[0] + re[8], re[0] - re[8]
    r26, i26 = re[2] + re[6], im[2] - im[6]
    rd, sd = C2 * (re[2] - re[6]), C2 * (im[2] + im[6])
    top, low = sum08 + re[4], sum08 - re[4]
    dp, dm = dif08 + rd, dif08 - rd
    ip, im4 = sd + im[4], sd - im[4]
    even = [
        top + r26,
        dp - ip,
        low - i26,
        dm - im4,
        top - r26,
        dm + im4,
        low + i26,
        dp + ip,
    ]
    a1p, a1m = re[1] + re[7], re[1] - re[7]
    a3p, a3m = re[3] + re[5], re[3] - re[5]
    j1p, j1m = im[1] + im[7], im[1] - im[7]
    j3p, j3m = im[3] + im[5], im[3] - im[5]
    c1, c3 = C1 * a1m + C3 * a3m, C3 * a1m - C1 * a3m
    c2 = C2 * (a1p - a3p)
    s1, s3 = C3 * j1p + C1 * j3p, C1 * j1p - C3 * j3p
    s2 = C2 * (j1m + j3m)
    odd = [
        a1p + a3p,
        c1 - s1,
        c2 - s2,
        c3 - s3,
        j3m - j1m,
        -(c3 + s3),
        -(c2 + s2),
        -(c1 + s1),
    ]
    return [x + y for x, y in zip(even, odd)]


def rows_loop(rows, body):
    @pl.loop(0, rows // TILE)
    def _(step):
        body(pl.ds(pl.multiple_of(step * TILE, TILE), TILE))


def split_rows(load, mid, rows, width):
    def body(at):
        for r, pair in enumerate(first_stage([load(p, at) for p in range(BLOCKS)])):
            mid[r, at, :width] = pair[0].astype(jnp.bfloat16)
            if pair[1] is not None:
                mid[r, at, width:] = pair[1].astype(jnp.bfloat16)

    rows_loop(rows, body)


def spectrum(mid, table, r, width):
    if r in (0, GROUPS - 1):
        return jnp.dot(mid[r, :, :width], table[r, :width, :], preferred_element_type=jnp.float32)
    return jnp.dot(mid[r], table[r], preferred_element_type=jnp.float32)


def invert_group(product, table, r, width, wide):
    if r in (0, GROUPS - 1):
        wide[r, :, :width] = jnp.dot(product, table[r, :, :width], preferred_element_type=jnp.float32)
    else:
        wide[r] = jnp.dot(product, table[r], preferred_element_type=jnp.float32)


def merge_rows(wide, store, rows, width):
    def body(at):
        parts = []
        for r in range(GROUPS):
            im = None if r in (0, GROUPS - 1) else wide[r, at, width:]
            parts.append((wide[r, at, :width], im))
        for p, value in enumerate(last_stage(parts)):
            store(p, at, value)

    rows_loop(rows, body)


def piece_at(ref, where, k, rows):
    start = pl.multiple_of(lax.bitwise_xor(where[0], k) * rows, rows)
    return ref.at[pl.ds(start, rows), :]


def gate_kernel(order, input_order, where, gate, upper, whole, *refs):
    outs, picks, refs = refs[: len(order)], refs[len(order) : 2 * len(order)], refs[2 * len(order) :]
    left, right, sems, pick_sems = refs
    rows = outs[0].shape[0]
    loads, moves = [], []
    for i, k in enumerate(order):
        pair = (
            pltpu.make_async_copy(piece_at(gate, where, k, rows), left.at[i], sems.at[0, i]),
            pltpu.make_async_copy(piece_at(upper, where, k, rows), right.at[i], sems.at[1, i]),
        )
        for copy in pair:
            copy.start()
        loads.append(pair)
    for i, k in enumerate(input_order):
        moves.append(pltpu.make_async_copy(piece_at(whole, where, k, rows), picks[i], pick_sems.at[i]))
        moves[-1].start()
    for i, out in enumerate(outs):
        for copy in loads[i]:
            copy.wait()
        out[...] = (left[i].astype(jnp.float32) * right[i].astype(jnp.float32)).astype(jnp.bfloat16)
    for copy in moves:
        copy.wait()


def finish_kernel(order, scale, where, *refs):
    pieces, shares, (whole, total, sems) = refs[: len(order)], refs[len(order) : -3], refs[-3:]
    copies = []
    for i, k in enumerate(order):
        copies.append(pltpu.make_async_copy(pieces[i], whole.at[lax.bitwise_xor(where[0], k)], sems.at[i]))
        copies[-1].start()
    added = shares[0][...].astype(jnp.float32)
    for share in shares[1:]:
        added = added + share[...].astype(jnp.float32)
    total[...] = added * scale
    for copy in copies:
        copy.wait()


def taps_kernel(taps, forward, taps_spec, mid):
    rows, width = (taps.shape[0], taps.shape[1] // BLOCKS)
    split_rows(lambda p, at: taps[at, p * width : (p + 1) * width], mid, rows, width)
    for r in range(GROUPS):
        taps_spec[r] = spectrum(mid, forward, r, width).astype(taps_spec.dtype)


def ordered(order, where, refs, held):
    span = refs[0].shape[1]
    for k, ref in zip(order, refs):
        start = pl.multiple_of(lax.bitwise_xor(where[0], k) * span, span)
        held[:, pl.ds(start, span)] = ref[...]


def block_of(held, width):
    return lambda p, at: held[at, p * width : (p + 1) * width].astype(jnp.float32)


def block_into(held, width):
    def store(p, at, value):
        held[at, p * width : (p + 1) * width] = value.astype(jnp.bfloat16)

    return store


def back_kernel(order, back_order, late, where, *refs):
    blocks, refs = refs[: len(order)], refs[len(order) + late :]
    taps_spec, forward, backward, *outs, grad_spec, held, mid, wide = refs
    outs = outs[late:]
    rows, width = held.shape[0], held.shape[1] // BLOCKS
    ordered(order, where, blocks, held)
    split_rows(block_of(held, width), mid, rows, width)
    for r in range(GROUPS):
        grad = spectrum(mid, forward, r, width)
        grad_spec[r] = grad.astype(grad_spec.dtype)
        taps = taps_spec[r].astype(jnp.float32)
        gr, gi, hr, hi = grad[:, :width], grad[:, width:], taps[:, :width], taps[:, width:]
        product = jnp.concatenate([hr * gr + hi * gi, hr * gi - hi * gr], axis=1)
        invert_group(product.astype(jnp.bfloat16), backward, r, width, wide)
    merge_rows(wide, block_into(held, width), rows, width)
    span = outs[0].shape[1]
    for k, out in zip(back_order, outs):
        start = pl.multiple_of(lax.bitwise_xor(where[0], k) * span, span)
        out[...] = held[:, pl.ds(start, span)]


def cross_kernel(order, where, *refs):
    blocks, refs = refs[: len(order)], refs[len(order) :]
    grad_spec, forward, backward, *outs, held, mid, wide = refs
    rows, width = held.shape[0], held.shape[1] // BLOCKS
    ordered(order, where, blocks, held)
    split_rows(block_of(held, width), mid, rows, width)
    for r in range(GROUPS):
        signal = spectrum(mid, forward, r, width)
        grad = grad_spec[r].astype(jnp.float32)
        gr, gi, xr, xi = grad[:, :width], grad[:, width:], signal[:, :width], signal[:, width:]
        product = jnp.concatenate([gr * xr + gi * xi, gi * xr - gr * xi], axis=1)
        invert_group(product.astype(jnp.bfloat16), backward, r, width, wide)
    merge_rows(wide, block_into(held, width), rows, width)
    part = held.shape[1] // len(outs)
    for k, out in zip(far_first(len(outs)), outs):
        start = pl.multiple_of(lax.bitwise_xor(where[1], k) * part, part)
        out[...] = held[:, pl.ds(start, part)]


def call(kernel, operands, outs, scratch=(), flops=0, streams=(), out_streams=(), aliases=None, hbm=()):
    def spec(stream):
        return pl.BlockSpec(memory_space=pl.ANY if stream else pltpu.VMEM)

    size = sum(math.prod(o.shape) * o.dtype.itemsize for o in list(operands) + list(outs))
    specs = [spec(i in streams) for i in range(len(operands))]
    for i in hbm:
        specs[i] = pl.BlockSpec(memory_space=pltpu.HBM)
    if operands[0].dtype == jnp.int32:
        specs[0] = pl.BlockSpec(memory_space=pltpu.SMEM)
    outputs = pl.pallas_call(
        kernel,
        out_shape=list(outs),
        in_specs=specs,
        out_specs=[spec(i in out_streams) for i in range(len(outs))],
        scratch_shapes=list(scratch),
        input_output_aliases=aliases or {},
        compiler_params=pltpu.CompilerParams(vmem_limit_bytes=LIMIT),
        cost_estimate=pl.CostEstimate(flops=flops, bytes_accessed=size, transcendentals=0),
    )(*operands)
    return list(outputs)


def far_first(size):
    return [*range(size // 2, size), *range(1, size // 2), 0]


def spread(size, order):
    part = size // 8
    return [k * part + i for k in order for i in range(part)] + [*range(1, part), 0]


def exchange(pieces, order, axis, size):
    moved = []
    for k, piece in zip(order, pieces):
        moved.append(lax.ppermute(piece, axis, [(i, i ^ k) for i in range(size)]) if k else piece)
    return moved


def on_device(saved_input, out_gate, grad_out, long_filter):
    count, shares = lax.axis_size("ctx"), lax.axis_size("dp")
    channels, span = saved_input.shape[1:]
    rows, length = long_filter.shape
    width = length // BLOCKS
    grad_order, input_order, back_order = (spread(count, o) for o in ((4, 1, 5, 2, 6, 3, 7), (4, 1, 5, 2, 6, 3, 7), (1, 4, 5, 6, 7, 2, 3)))
    late = 2
    at = count - 1 - late
    every = range(count + 8)
    where = jnp.stack([lax.axis_index("ctx"), lax.axis_index("dp")]).astype(jnp.int32)
    forward, backward = (jnp.asarray(t) for t in transform_tables(width))
    half, full = jnp.bfloat16, jnp.float32
    piece = jax.ShapeDtypeStruct((rows, span), half)
    spec = jax.ShapeDtypeStruct((GROUPS, rows, 2 * width), half)
    held = pltpu.VMEM((rows, length), half)
    mid = pltpu.VMEM((GROUPS, rows, 2 * width), half)
    wide = pltpu.VMEM((GROUPS, rows, 2 * width), full)
    slots = pltpu.VMEM((count, rows, span), half)
    sems = pltpu.SemaphoreType.DMA
    work = 2 * GROUPS * rows * 4 * width * width

    pieces = call(
        functools.partial(gate_kernel, grad_order, input_order),
        [where, *(pltpu.with_memory_space_constraint(x[0], pltpu.HBM) for x in (out_gate, grad_out, saved_input))],
        [piece] * (2 * count),
        [slots, slots, sems((2, count)), sems((count,))],
        hbm=(1, 2, 3),
    )
    grad_pieces, input_pieces = pieces[:count], pieces[count:]
    grad_blocks = exchange(grad_pieces, grad_order, "ctx", count)
    (taps_spec,) = call(taps_kernel, [long_filter, forward], [spec], [mid], flops=work)
    passed = [*input_pieces[at : at + late]]
    *back, grad_spec = call(
        functools.partial(back_kernel, grad_order, back_order, late),
        [where, *grad_blocks, *passed, taps_spec, forward, backward],
        [piece] * (late + count) + [spec],
        [held, mid, wide],
        flops=2 * work,
        streams=range(1 + count, 1 + count + late),
        out_streams=range(late),
        aliases={1 + count + i: i for i in range(late)},
    )
    input_pieces[at : at + late], back = back[:late], back[late:]
    input_blocks = exchange(input_pieces, input_order, "ctx", count)
    back_blocks = exchange(back, back_order, "ctx", count)
    share = jax.ShapeDtypeStruct((rows, length // shares), half)
    cross = call(
        functools.partial(cross_kernel, input_order),
        [where, *input_blocks, grad_spec, forward, backward],
        [share] * shares,
        [held, mid, wide],
        flops=2 * work,
    )
    cross_blocks = exchange(cross, far_first(shares), "dp", shares)
    scale = 1.0 / math.sqrt(shares * length)
    whole, grad_filter = call(
        functools.partial(finish_kernel, back_order, scale),
        [where, *back_blocks, *cross_blocks],
        [jax.ShapeDtypeStruct((count, rows, span), half), jax.ShapeDtypeStruct((rows, length // shares), full)],
        [sems((count,))],
        out_streams=(0,),
    )
    return (whole.reshape(1, channels, span), grad_filter)


def solution(mesh):
    in_specs = (P("dp", None, "ctx"), P("dp", None, "ctx"), P("dp", None, "ctx"), P("ctx", None))
    out_specs = (P("dp", None, "ctx"), P("ctx", "dp"))
    return jax.shard_map(
        on_device, mesh=mesh, in_specs=in_specs, out_specs=out_specs, check_vma=False
    )
```

```python
import functools
import math

import jax
import jax.numpy as jnp
import ml_dtypes
import numpy as np
from jax import lax
from jax.experimental import pallas as pl
from jax.experimental.pallas import tpu as pltpu
from jax.sharding import PartitionSpec as P

BLOCKS = 8
GROUPS = 9
TILE = 16
C1 = math.cos(math.pi / 8)
C2 = math.cos(math.pi / 4)
C3 = math.cos(3 * math.pi / 8)
LIMIT = 32 * 1024 * 1024


def transform_tables(width):
    points = 2 * BLOCKS * width
    row = np.arange(width)
    forward = np.zeros((GROUPS, 2 * width, 2 * width), np.float64)
    for r in range(GROUPS):
        angle = 2.0 * np.pi * (np.outer(row, 16 * row + r) % points) / points
        cos, sin = np.cos(angle), np.sin(angle)
        forward[r] = np.block([[cos, -sin], [sin, cos]])
    scale = np.full((GROUPS, 1, 1), 2.0 / points)
    scale[0] = scale[-1] = 1.0 / points
    backward = np.swapaxes(forward, 1, 2) * scale
    return forward.astype(ml_dtypes.bfloat16), backward.astype(ml_dtypes.bfloat16)


def first_stage(b):
    e = [b[p] + b[p + 4] for p in range(4)]
    f = [b[p] - b[p + 4] for p in range(4)]
    e02, e13 = e[0] + e[2], e[1] + e[3]
    fd, fs = C2 * (f[1] - f[3]), C2 * (f[1] + f[3])
    d = [None] + [b[p] - b[8 - p] for p in (1, 2, 3)]
    g = [None] + [b[p] + b[8 - p] for p in (1, 2, 3)]
    d2, g2 = C2 * d[2], C2 * g[2]
    re1, re3 = C1 * d[1] + C3 * d[3], C3 * d[1] - C1 * d[3]
    im1, im3 = C3 * g[1] + C1 * g[3], C1 * g[1] - C3 * g[3]
    up, down = b[0] + d2, b[0] - d2
    bp, bm = b[4] + g2, b[4] - g2
    return [
        (e02 + e13, None),
        (up + re1, -(bp + im1)),
        (f[0] + fd, -(f[2] + fs)),
        (down + re3, bm - im3),
        (e[0] - e[2], e[3] - e[1]),
        (down - re3, -(bm + im3)),
        (f[0] - fd, f[2] - fs),
        (up - re1, bp - im1),
        (e02 - e13, None),
    ]


def last_stage(u):
    re = [pair[0] for pair in u]
    im = [pair[1] for pair in u]
    sum08, dif08 = re[0] + re[8], re[0] - re[8]
    r26, i26 = re[2] + re[6], im[2] - im[6]
    rd, sd = C2 * (re[2] - re[6]), C2 * (im[2] + im[6])
    top, low = sum08 + re[4], sum08 - re[4]
    dp, dm = dif08 + rd, dif08 - rd
    ip, im4 = sd + im[4], sd - im[4]
    even = [
        top + r26,
        dp - ip,
        low - i26,
        dm - im4,
        top - r26,
        dm + im4,
        low + i26,
        dp + ip,
    ]
    a1p, a1m = re[1] + re[7], re[1] - re[7]
    a3p, a3m = re[3] + re[5], re[3] - re[5]
    j1p, j1m = im[1] + im[7], im[1] - im[7]
    j3p, j3m = im[3] + im[5], im[3] - im[5]
    c1, c3 = C1 * a1m + C3 * a3m, C3 * a1m - C1 * a3m
    c2 = C2 * (a1p - a3p)
    s1, s3 = C3 * j1p + C1 * j3p, C1 * j1p - C3 * j3p
    s2 = C2 * (j1m + j3m)
    odd = [
        a1p + a3p,
        c1 - s1,
        c2 - s2,
        c3 - s3,
        j3m - j1m,
        -(c3 + s3),
        -(c2 + s2),
        -(c1 + s1),
    ]
    return [x + y for x, y in zip(even, odd)]


def rows_loop(rows, body):
    @pl.loop(0, rows // TILE)
    def _(step):
        body(pl.ds(pl.multiple_of(step * TILE, TILE), TILE))


def split_rows(load, mid, rows, width):
    def body(at):
        for r, pair in enumerate(first_stage([load(p, at) for p in range(BLOCKS)])):
            mid[r, at, :width] = pair[0].astype(jnp.bfloat16)
            if pair[1] is not None:
                mid[r, at, width:] = pair[1].astype(jnp.bfloat16)

    rows_loop(rows, body)


def spectrum(mid, table, r, width):
    if r in (0, GROUPS - 1):
        return jnp.dot(mid[r, :, :width], table[r, :width, :], preferred_element_type=jnp.float32)
    return jnp.dot(mid[r], table[r], preferred_element_type=jnp.float32)


def invert_group(product, table, r, width, wide):
    if r in (0, GROUPS - 1):
        wide[r, :, :width] = jnp.dot(product, table[r, :, :width], preferred_element_type=jnp.float32)
    else:
        wide[r] = jnp.dot(product, table[r], preferred_element_type=jnp.float32)


def merge_rows(wide, store, rows, width):
    def body(at):
        parts = []
        for r in range(GROUPS):
            im = None if r in (0, GROUPS - 1) else wide[r, at, width:]
            parts.append((wide[r, at, :width], im))
        for p, value in enumerate(last_stage(parts)):
            store(p, at, value)

    rows_loop(rows, body)


def piece_at(ref, where, k, rows):
    start = pl.multiple_of(lax.bitwise_xor(where[0], k) * rows, rows)
    return ref.at[pl.ds(start, rows), :]


def gate_kernel(order, where, gate, upper, *refs):
    outs, (left, right, sems) = refs[: len(order)], refs[len(order) :]
    rows = outs[0].shape[0]
    loads = []
    for i, k in enumerate(order):
        pair = (
            pltpu.make_async_copy(piece_at(gate, where, k, rows), left.at[i], sems.at[0, i]),
            pltpu.make_async_copy(piece_at(upper, where, k, rows), right.at[i], sems.at[1, i]),
        )
        for copy in pair:
            copy.start()
        loads.append(pair)
    for i, out in enumerate(outs):
        for copy in loads[i]:
            copy.wait()
        out[...] = (left[i].astype(jnp.float32) * right[i].astype(jnp.float32)).astype(jnp.bfloat16)


def place_kernel(order, where, *refs):
    pieces, whole = refs[:-1], refs[-1]
    for k, piece in zip(order, pieces):
        whole[lax.bitwise_xor(where[0], k)] = piece[...]


def taps_kernel(whole, taps, forward, *refs):
    taps_spec, copied, mid, sem = refs[-4:]
    rows, width = (taps.shape[0], taps.shape[1] // BLOCKS)
    copy = pltpu.make_async_copy(whole, copied, sem.at[0])
    copy.start()
    split_rows(lambda p, at: taps[at, p * width : (p + 1) * width], mid, rows, width)
    for r in range(GROUPS):
        taps_spec[r] = spectrum(mid, forward, r, width).astype(taps_spec.dtype)
    copy.wait()


def ordered(order, where, refs, held):
    span = refs[0].shape[1]
    for k, ref in zip(order, refs):
        start = pl.multiple_of(lax.bitwise_xor(where[0], k) * span, span)
        held[:, pl.ds(start, span)] = ref[...]


def block_of(held, width):
    return lambda p, at: held[at, p * width : (p + 1) * width].astype(jnp.float32)


def block_into(held, width):
    def store(p, at, value):
        held[at, p * width : (p + 1) * width] = value.astype(jnp.bfloat16)

    return store


def back_kernel(order, back_order, where, *refs):
    blocks, refs = refs[: len(order)], refs[len(order) :]
    taps_spec, forward, backward, *outs, grad_spec, held, mid, wide = refs
    rows, width = held.shape[0], held.shape[1] // BLOCKS
    ordered(order, where, blocks, held)
    split_rows(block_of(held, width), mid, rows, width)
    for r in range(GROUPS):
        grad = spectrum(mid, forward, r, width)
        grad_spec[r] = grad.astype(grad_spec.dtype)
        taps = taps_spec[r].astype(jnp.float32)
        gr, gi, hr, hi = grad[:, :width], grad[:, width:], taps[:, :width], taps[:, width:]
        product = jnp.concatenate([hr * gr + hi * gi, hr * gi - hi * gr], axis=1)
        invert_group(product.astype(jnp.bfloat16), backward, r, width, wide)
    merge_rows(wide, block_into(held, width), rows, width)
    span = outs[0].shape[1]
    for k, out in zip(back_order, outs):
        start = pl.multiple_of(lax.bitwise_xor(where[0], k) * span, span)
        out[...] = held[:, pl.ds(start, span)]


def cross_kernel(where, blocks, grad_spec, forward, backward, *refs):
    *outs, held, mid, wide = refs
    rows, width = held.shape[0], held.shape[1] // BLOCKS
    span = blocks.shape[2]
    for p in range(blocks.shape[0]):
        held[:, p * span : (p + 1) * span] = blocks[p]
    split_rows(block_of(held, width), mid, rows, width)
    for r in range(GROUPS):
        signal = spectrum(mid, forward, r, width)
        grad = grad_spec[r].astype(jnp.float32)
        gr, gi, xr, xi = grad[:, :width], grad[:, width:], signal[:, :width], signal[:, width:]
        product = jnp.concatenate([gr * xr + gi * xi, gi * xr - gr * xi], axis=1)
        invert_group(product.astype(jnp.bfloat16), backward, r, width, wide)
    merge_rows(wide, block_into(held, width), rows, width)
    part = held.shape[1] // len(outs)
    for k, out in zip(far_first(len(outs)), outs):
        start = pl.multiple_of(lax.bitwise_xor(where[1], k) * part, part)
        out[...] = held[:, pl.ds(start, part)]


def call(kernel, operands, outs, scratch=(), flops=0, streams=()):
    size = sum(math.prod(o.shape) * o.dtype.itemsize for o in list(operands) + list(outs))
    specs = [pl.BlockSpec(memory_space=pl.ANY if i in streams else pltpu.VMEM) for i in range(len(operands))]
    if operands[0].dtype == jnp.int32:
        specs[0] = pl.BlockSpec(memory_space=pltpu.SMEM)
    outputs = pl.pallas_call(
        kernel,
        out_shape=list(outs),
        in_specs=specs,
        out_specs=[pl.BlockSpec(memory_space=pltpu.VMEM)] * len(outs),
        scratch_shapes=list(scratch),
        compiler_params=pltpu.CompilerParams(vmem_limit_bytes=LIMIT),
        cost_estimate=pl.CostEstimate(flops=flops, bytes_accessed=size, transcendentals=0),
    )(*operands)
    return list(outputs)


def far_first(size):
    return [*range(size // 2, size), *range(1, size // 2), 0]


def spread(size, order):
    part = size // 8
    return [k * part + i for k in order for i in range(part)] + [*range(1, part), 0]


def exchange(pieces, order, axis, size):
    moved = []
    for k, piece in zip(order, pieces):
        moved.append(lax.ppermute(piece, axis, [(i, i ^ k) for i in range(size)]) if k else piece)
    return moved


def on_device(saved_input, out_gate, grad_out, long_filter):
    count, shares = lax.axis_size("ctx"), lax.axis_size("dp")
    channels, span = saved_input.shape[1:]
    rows, length = long_filter.shape
    width = length // BLOCKS
    order, back_order, tied = (spread(count, o) for o in ((4, 1, 5, 2, 6, 7, 3), (4, 1, 5, 2, 6, 7, 3), (4, 5, 6)))
    tied = tied[: 3 * count // 8]
    every = range(count + 8)
    where = jnp.stack([lax.axis_index("ctx"), lax.axis_index("dp")]).astype(jnp.int32)
    forward, backward = (jnp.asarray(t) for t in transform_tables(width))
    half, full = jnp.bfloat16, jnp.float32
    piece = jax.ShapeDtypeStruct((rows, span), half)
    spec = jax.ShapeDtypeStruct((GROUPS, rows, 2 * width), half)
    held = pltpu.VMEM((rows, length), half)
    mid = pltpu.VMEM((GROUPS, rows, 2 * width), half)
    wide = pltpu.VMEM((GROUPS, rows, 2 * width), full)
    slots = pltpu.VMEM((count, rows, span), half)
    sems = pltpu.SemaphoreType.DMA
    work = 2 * GROUPS * rows * 4 * width * width

    grad_pieces = call(
        functools.partial(gate_kernel, order),
        [where, *(pltpu.with_memory_space_constraint(x[0], pltpu.HBM) for x in (out_gate, grad_out))],
        [piece] * count,
        [slots, slots, sems((2, count))],
        streams=(1, 2),
    )
    grad_blocks = exchange(grad_pieces, order, "ctx", count)
    whole_input = pltpu.with_memory_space_constraint(saved_input.reshape(count, rows, span), pltpu.HBM)
    waited = [block for k, block in zip(order, grad_blocks) if k in tied]
    taps_spec, copied = call(
        taps_kernel,
        [whole_input, long_filter, forward, *waited],
        [spec, jax.ShapeDtypeStruct((count, rows, span), half)],
        [mid, sems((1,))],
        flops=work,
        streams=(0, *range(3, 3 + len(waited))),
    )
    input_blocks = lax.all_to_all(copied, "ctx", split_axis=0, concat_axis=0, tiled=True)
    *back, grad_spec = call(
        functools.partial(back_kernel, order, back_order),
        [where, *grad_blocks, taps_spec, forward, backward],
        [piece] * count + [spec],
        [held, mid, wide],
        flops=2 * work,
    )
    back_blocks = exchange(back, back_order, "ctx", count)
    share = jax.ShapeDtypeStruct((rows, length // shares), half)
    cross = call(
        cross_kernel,
        [where, input_blocks, grad_spec, forward, backward],
        [share] * shares,
        [held, mid, wide],
        flops=2 * work,
    )
    cross_blocks = exchange(cross, far_first(shares), "dp", shares)
    scale = 1.0 / math.sqrt(shares * length)
    grad_filter = sum(x.astype(full) for x in cross_blocks) * scale
    (whole,) = call(
        functools.partial(place_kernel, back_order),
        [where, *back_blocks],
        [jax.ShapeDtypeStruct((count, rows, span), half)],
    )
    return (whole.reshape(1, channels, span), grad_filter)


def solution(mesh):
    in_specs = (P("dp", None, "ctx"), P("dp", None, "ctx"), P("dp", None, "ctx"), P("ctx", None))
    out_specs = (P("dp", None, "ctx"), P("ctx", "dp"))
    return jax.shard_map(
        on_device, mesh=mesh, in_specs=in_specs, out_specs=out_specs, check_vma=False
    )
```

```python
import functools
import math

import jax
import jax.numpy as jnp
import ml_dtypes
import numpy as np
from jax import lax
from jax.experimental import pallas as pl
from jax.experimental.pallas import tpu as pltpu
from jax.sharding import PartitionSpec as P

BLOCKS = 8
GROUPS = 9
TILE = 16
C1 = math.cos(math.pi / 8)
C2 = math.cos(math.pi / 4)
C3 = math.cos(3 * math.pi / 8)
LIMIT = 32 * 1024 * 1024


def transform_tables(width):
    points = 2 * BLOCKS * width
    row = np.arange(width)
    forward = np.zeros((GROUPS, 2 * width, 2 * width), np.float64)
    for r in range(GROUPS):
        angle = 2.0 * np.pi * (np.outer(row, 16 * row + r) % points) / points
        cos, sin = np.cos(angle), np.sin(angle)
        forward[r] = np.block([[cos, -sin], [sin, cos]])
    scale = np.full((GROUPS, 1, 1), 2.0 / points)
    scale[0] = scale[-1] = 1.0 / points
    backward = np.swapaxes(forward, 1, 2) * scale
    return forward.astype(ml_dtypes.bfloat16), backward.astype(ml_dtypes.bfloat16)


def first_stage(b):
    e = [b[p] + b[p + 4] for p in range(4)]
    f = [b[p] - b[p + 4] for p in range(4)]
    e02, e13 = e[0] + e[2], e[1] + e[3]
    fd, fs = C2 * (f[1] - f[3]), C2 * (f[1] + f[3])
    d = [None] + [b[p] - b[8 - p] for p in (1, 2, 3)]
    g = [None] + [b[p] + b[8 - p] for p in (1, 2, 3)]
    d2, g2 = C2 * d[2], C2 * g[2]
    re1, re3 = C1 * d[1] + C3 * d[3], C3 * d[1] - C1 * d[3]
    im1, im3 = C3 * g[1] + C1 * g[3], C1 * g[1] - C3 * g[3]
    up, down = b[0] + d2, b[0] - d2
    bp, bm = b[4] + g2, b[4] - g2
    return [
        (e02 + e13, None),
        (up + re1, -(bp + im1)),
        (f[0] + fd, -(f[2] + fs)),
        (down + re3, bm - im3),
        (e[0] - e[2], e[3] - e[1]),
        (down - re3, -(bm + im3)),
        (f[0] - fd, f[2] - fs),
        (up - re1, bp - im1),
        (e02 - e13, None),
    ]


def last_stage(u):
    re = [pair[0] for pair in u]
    im = [pair[1] for pair in u]
    sum08, dif08 = re[0] + re[8], re[0] - re[8]
    r26, i26 = re[2] + re[6], im[2] - im[6]
    rd, sd = C2 * (re[2] - re[6]), C2 * (im[2] + im[6])
    top, low = sum08 + re[4], sum08 - re[4]
    dp, dm = dif08 + rd, dif08 - rd
    ip, im4 = sd + im[4], sd - im[4]
    even = [
        top + r26,
        dp - ip,
        low - i26,
        dm - im4,
        top - r26,
        dm + im4,
        low + i26,
        dp + ip,
    ]
    a1p, a1m = re[1] + re[7], re[1] - re[7]
    a3p, a3m = re[3] + re[5], re[3] - re[5]
    j1p, j1m = im[1] + im[7], im[1] - im[7]
    j3p, j3m = im[3] + im[5], im[3] - im[5]
    c1, c3 = C1 * a1m + C3 * a3m, C3 * a1m - C1 * a3m
    c2 = C2 * (a1p - a3p)
    s1, s3 = C3 * j1p + C1 * j3p, C1 * j1p - C3 * j3p
    s2 = C2 * (j1m + j3m)
    odd = [
        a1p + a3p,
        c1 - s1,
        c2 - s2,
        c3 - s3,
        j3m - j1m,
        -(c3 + s3),
        -(c2 + s2),
        -(c1 + s1),
    ]
    return [x + y for x, y in zip(even, odd)]


def rows_loop(rows, body):
    @pl.loop(0, rows // TILE)
    def _(step):
        body(pl.ds(pl.multiple_of(step * TILE, TILE), TILE))


def split_rows(load, mid, rows, width):
    def body(at):
        for r, pair in enumerate(first_stage([load(p, at) for p in range(BLOCKS)])):
            mid[r, at, :width] = pair[0].astype(jnp.bfloat16)
            if pair[1] is not None:
                mid[r, at, width:] = pair[1].astype(jnp.bfloat16)

    rows_loop(rows, body)


def spectrum(mid, table, r, width):
    if r in (0, GROUPS - 1):
        return jnp.dot(mid[r, :, :width], table[r, :width, :], preferred_element_type=jnp.float32)
    return jnp.dot(mid[r], table[r], preferred_element_type=jnp.float32)


def invert_group(product, table, r, width, wide):
    if r in (0, GROUPS - 1):
        wide[r, :, :width] = jnp.dot(product, table[r, :, :width], preferred_element_type=jnp.float32)
    else:
        wide[r] = jnp.dot(product, table[r], preferred_element_type=jnp.float32)


def merge_rows(wide, store, rows, width):
    def body(at):
        parts = []
        for r in range(GROUPS):
            im = None if r in (0, GROUPS - 1) else wide[r, at, width:]
            parts.append((wide[r, at, :width], im))
        for p, value in enumerate(last_stage(parts)):
            store(p, at, value)

    rows_loop(rows, body)


def piece_at(ref, where, k, rows):
    start = pl.multiple_of(where[k] * rows, rows)
    return ref.at[pl.ds(start, rows), :]


def gate_kernel(order, input_order, where, gate, upper, whole, *refs):
    outs, picks, refs = refs[: len(order)], refs[len(order) : 2 * len(order)], refs[2 * len(order) :]
    left, right, sems, pick_sems = refs
    rows = outs[0].shape[0]
    loads, moves = [], []
    for i, k in enumerate(order):
        pair = (
            pltpu.make_async_copy(piece_at(gate, where, k, rows), left.at[i], sems.at[0, i]),
            pltpu.make_async_copy(piece_at(upper, where, k, rows), right.at[i], sems.at[1, i]),
        )
        for copy in pair:
            copy.start()
        loads.append(pair)
    for i, k in enumerate(input_order):
        moves.append(pltpu.make_async_copy(piece_at(whole, where, k, rows), picks[i], pick_sems.at[i]))
        moves[-1].start()
    for i, out in enumerate(outs):
        for copy in loads[i]:
            copy.wait()
        out[...] = (left[i].astype(jnp.float32) * right[i].astype(jnp.float32)).astype(jnp.bfloat16)
    for copy in moves:
        copy.wait()


def place_kernel(order, where, *refs):
    pieces, whole = refs[:-1], refs[-1]
    for k, piece in zip(order, pieces):
        whole[where[k]] = piece[...]


def taps_kernel(taps, forward, taps_spec, mid):
    rows, width = (taps.shape[0], taps.shape[1] // BLOCKS)
    split_rows(lambda p, at: taps[at, p * width : (p + 1) * width], mid, rows, width)
    for r in range(GROUPS):
        taps_spec[r] = spectrum(mid, forward, r, width).astype(taps_spec.dtype)


def ordered(order, where, refs, held):
    span = refs[0].shape[1]
    for k, ref in zip(order, refs):
        start = pl.multiple_of(where[k] * span, span)
        held[:, pl.ds(start, span)] = ref[...]


def block_of(held, width):
    return lambda p, at: held[at, p * width : (p + 1) * width].astype(jnp.float32)


def block_into(held, width):
    def store(p, at, value):
        held[at, p * width : (p + 1) * width] = value.astype(jnp.bfloat16)

    return store


def back_kernel(order, back_order, late, where, *refs):
    blocks, refs = refs[: len(order)], refs[len(order) + late :]
    taps_spec, forward, backward, *outs, grad_spec, held, mid, wide = refs
    outs = outs[late:]
    rows, width = held.shape[0], held.shape[1] // BLOCKS
    ordered(order, where, blocks, held)
    split_rows(block_of(held, width), mid, rows, width)
    for r in range(GROUPS):
        grad = spectrum(mid, forward, r, width)
        grad_spec[r] = grad.astype(grad_spec.dtype)
        taps = taps_spec[r].astype(jnp.float32)
        gr, gi, hr, hi = grad[:, :width], grad[:, width:], taps[:, :width], taps[:, width:]
        product = jnp.concatenate([hr * gr + hi * gi, hr * gi - hi * gr], axis=1)
        invert_group(product.astype(jnp.bfloat16), backward, r, width, wide)
    merge_rows(wide, block_into(held, width), rows, width)
    span = outs[0].shape[1]
    for k, out in zip(back_order, outs):
        start = pl.multiple_of(where[k] * span, span)
        out[...] = held[:, pl.ds(start, span)]


def cross_kernel(order, where, *refs):
    blocks, refs = refs[: len(order)], refs[len(order) :]
    grad_spec, forward, backward, *outs, held, mid, wide = refs
    rows, width = held.shape[0], held.shape[1] // BLOCKS
    ordered(order, where, blocks, held)
    split_rows(block_of(held, width), mid, rows, width)
    for r in range(GROUPS):
        signal = spectrum(mid, forward, r, width)
        grad = grad_spec[r].astype(jnp.float32)
        gr, gi, xr, xi = grad[:, :width], grad[:, width:], signal[:, :width], signal[:, width:]
        product = jnp.concatenate([gr * xr + gi * xi, gi * xr - gr * xi], axis=1)
        invert_group(product.astype(jnp.bfloat16), backward, r, width, wide)
    merge_rows(wide, block_into(held, width), rows, width)
    part = held.shape[1] // len(outs)
    for k, out in zip(far_first(len(outs)), outs):
        start = pl.multiple_of(lax.bitwise_xor(where[where.shape[0] - 1], k) * part, part)
        out[...] = held[:, pl.ds(start, part)]


def call(kernel, operands, outs, scratch=(), flops=0, streams=(), out_streams=(), aliases=None, hbm=()):
    def spec(stream):
        return pl.BlockSpec(memory_space=pl.ANY if stream else pltpu.VMEM)

    size = sum(math.prod(o.shape) * o.dtype.itemsize for o in list(operands) + list(outs))
    specs = [spec(i in streams) for i in range(len(operands))]
    for i in hbm:
        specs[i] = pl.BlockSpec(memory_space=pltpu.HBM)
    if operands[0].dtype == jnp.int32:
        specs[0] = pl.BlockSpec(memory_space=pltpu.SMEM)
    outputs = pl.pallas_call(
        kernel,
        out_shape=list(outs),
        in_specs=specs,
        out_specs=[spec(i in out_streams) for i in range(len(outs))],
        scratch_shapes=list(scratch),
        input_output_aliases=aliases or {},
        compiler_params=pltpu.CompilerParams(vmem_limit_bytes=LIMIT),
        cost_estimate=pl.CostEstimate(flops=flops, bytes_accessed=size, transcendentals=0),
    )(*operands)
    return list(outputs)


def far_first(size):
    return [*range(size // 2, size), *range(1, size // 2), 0]


def pairings(size):
    if size != 8:
        return [[i ^ k for i in range(size)] for k in [*range(1, size), 0]]
    rounds = [[i ^ 4 for i in range(8)]]
    for k, l in ((0, 1), (2, 3), (0, 2), (1, 3), (0, 3), (1, 2)):
        i, j = (n for n in range(4) if n not in (k, l))
        partner = [0] * 8
        for one, two in ((k, 4 + l), (l, 4 + k), (i, j), (4 + i, 4 + j)):
            partner[one], partner[two] = two, one
        rounds.append(partner)
    return rounds + [list(range(8))]


def spread(size, order):
    part = size // 8
    return [k * part + i for k in (*order, 7) for i in range(part)]


def exchange(pieces, order, rounds, axis):
    moved = []
    for k, piece in zip(order, pieces):
        pairs = list(enumerate(rounds[k]))
        moved.append(piece if pairs[0][1] == 0 else lax.ppermute(piece, axis, pairs))
    return moved


def on_device(saved_input, out_gate, grad_out, long_filter):
    count, shares = lax.axis_size("ctx"), lax.axis_size("dp")
    channels, span = saved_input.shape[1:]
    rows, length = long_filter.shape
    width = length // BLOCKS
    rounds = pairings(count)
    grad_order, input_order, back_order = (spread(count, o) for o in ((0, 1, 2, 3, 4, 5, 6), (0, 1, 2, 3, 4, 5, 6), (0, 1, 2, 3, 4, 5, 6)))
    late = 2
    at = count - 1 - late
    every = range(count + 8)
    me = lax.axis_index("ctx")
    partners = lax.dynamic_index_in_dim(jnp.asarray(np.array(rounds, np.int32).T), me, 0, keepdims=False)
    where = jnp.concatenate([partners, jnp.stack([me, lax.axis_index("dp")]).astype(jnp.int32)])
    forward, backward = (jnp.asarray(t) for t in transform_tables(width))
    half, full = jnp.bfloat16, jnp.float32
    piece = jax.ShapeDtypeStruct((rows, span), half)
    spec = jax.ShapeDtypeStruct((GROUPS, rows, 2 * width), half)
    held = pltpu.VMEM((rows, length), half)
    mid = pltpu.VMEM((GROUPS, rows, 2 * width), half)
    wide = pltpu.VMEM((GROUPS, rows, 2 * width), full)
    slots = pltpu.VMEM((count, rows, span), half)
    sems = pltpu.SemaphoreType.DMA
    work = 2 * GROUPS * rows * 4 * width * width

    pieces = call(
        functools.partial(gate_kernel, grad_order, input_order),
        [where, *(pltpu.with_memory_space_constraint(x[0], pltpu.HBM) for x in (out_gate, grad_out, saved_input))],
        [piece] * (2 * count),
        [slots, slots, sems((2, count)), sems((count,))],
        hbm=(1, 2, 3),
    )
    grad_pieces, input_pieces = pieces[:count], pieces[count:]
    grad_blocks = exchange(grad_pieces, grad_order, rounds, "ctx")
    (taps_spec,) = call(taps_kernel, [long_filter, forward], [spec], [mid], flops=work)
    passed = [*input_pieces[at : at + late]]
    *back, grad_spec = call(
        functools.partial(back_kernel, grad_order, back_order, late),
        [where, *grad_blocks, *passed, taps_spec, forward, backward],
        [piece] * (late + count) + [spec],
        [held, mid, wide],
        flops=2 * work,
        streams=range(1 + count, 1 + count + late),
        out_streams=range(late),
        aliases={1 + count + i: i for i in range(late)},
    )
    input_pieces[at : at + late], back = back[:late], back[late:]
    input_blocks = exchange(input_pieces, input_order, rounds, "ctx")
    back_blocks = exchange(back, back_order, rounds, "ctx")
    share = jax.ShapeDtypeStruct((rows, length // shares), half)
    cross = call(
        functools.partial(cross_kernel, input_order),
        [where, *input_blocks, grad_spec, forward, backward],
        [share] * shares,
        [held, mid, wide],
        flops=2 * work,
    )
    swaps = [[i ^ k for i in range(shares)] for k in far_first(shares)]
    cross_blocks = exchange(cross, range(shares), swaps, "dp")
    scale = 1.0 / math.sqrt(shares * length)
    grad_filter = sum(x.astype(full) for x in cross_blocks) * scale
    (whole,) = call(
        functools.partial(place_kernel, back_order),
        [where, *back_blocks],
        [jax.ShapeDtypeStruct((count, rows, span), half)],
    )
    return (whole.reshape(1, channels, span), grad_filter)


def solution(mesh):
    in_specs = (P("dp", None, "ctx"), P("dp", None, "ctx"), P("dp", None, "ctx"), P("ctx", None))
    out_specs = (P("dp", None, "ctx"), P("ctx", "dp"))
    return jax.shard_map(
        on_device, mesh=mesh, in_specs=in_specs, out_specs=out_specs, check_vma=False
    )
```

```python
import functools
import math

import jax
import jax.numpy as jnp
import ml_dtypes
import numpy as np
from jax import lax
from jax.experimental import pallas as pl
from jax.experimental.pallas import tpu as pltpu
from jax.sharding import PartitionSpec as P

BLOCKS = 8
GROUPS = 9
TILE = 16
C1 = math.cos(math.pi / 8)
C2 = math.cos(math.pi / 4)
C3 = math.cos(3 * math.pi / 8)
LIMIT = 32 * 1024 * 1024


def transform_tables(width):
    points = 2 * BLOCKS * width
    row = np.arange(width)
    forward = np.zeros((GROUPS, 2 * width, 2 * width), np.float64)
    for r in range(GROUPS):
        angle = 2.0 * np.pi * (np.outer(row, 16 * row + r) % points) / points
        cos, sin = np.cos(angle), np.sin(angle)
        forward[r] = np.block([[cos, -sin], [sin, cos]])
    scale = np.full((GROUPS, 1, 1), 2.0 / points)
    scale[0] = scale[-1] = 1.0 / points
    backward = np.swapaxes(forward, 1, 2) * scale
    return forward.astype(ml_dtypes.bfloat16), backward.astype(ml_dtypes.bfloat16)


def first_stage(b):
    e = [b[p] + b[p + 4] for p in range(4)]
    f = [b[p] - b[p + 4] for p in range(4)]
    e02, e13 = e[0] + e[2], e[1] + e[3]
    fd, fs = C2 * (f[1] - f[3]), C2 * (f[1] + f[3])
    d = [None] + [b[p] - b[8 - p] for p in (1, 2, 3)]
    g = [None] + [b[p] + b[8 - p] for p in (1, 2, 3)]
    d2, g2 = C2 * d[2], C2 * g[2]
    re1, re3 = C1 * d[1] + C3 * d[3], C3 * d[1] - C1 * d[3]
    im1, im3 = C3 * g[1] + C1 * g[3], C1 * g[1] - C3 * g[3]
    up, down = b[0] + d2, b[0] - d2
    bp, bm = b[4] + g2, b[4] - g2
    return [
        (e02 + e13, None),
        (up + re1, -(bp + im1)),
        (f[0] + fd, -(f[2] + fs)),
        (down + re3, bm - im3),
        (e[0] - e[2], e[3] - e[1]),
        (down - re3, -(bm + im3)),
        (f[0] - fd, f[2] - fs),
        (up - re1, bp - im1),
        (e02 - e13, None),
    ]


def last_stage(u):
    re = [pair[0] for pair in u]
    im = [pair[1] for pair in u]
    sum08, dif08 = re[0] + re[8], re[0] - re[8]
    r26, i26 = re[2] + re[6], im[2] - im[6]
    rd, sd = C2 * (re[2] - re[6]), C2 * (im[2] + im[6])
    top, low = sum08 + re[4], sum08 - re[4]
    dp, dm = dif08 + rd, dif08 - rd
    ip, im4 = sd + im[4], sd - im[4]
    even = [
        top + r26,
        dp - ip,
        low - i26,
        dm - im4,
        top - r26,
        dm + im4,
        low + i26,
        dp + ip,
    ]
    a1p, a1m = re[1] + re[7], re[1] - re[7]
    a3p, a3m = re[3] + re[5], re[3] - re[5]
    j1p, j1m = im[1] + im[7], im[1] - im[7]
    j3p, j3m = im[3] + im[5], im[3] - im[5]
    c1, c3 = C1 * a1m + C3 * a3m, C3 * a1m - C1 * a3m
    c2 = C2 * (a1p - a3p)
    s1, s3 = C3 * j1p + C1 * j3p, C1 * j1p - C3 * j3p
    s2 = C2 * (j1m + j3m)
    odd = [
        a1p + a3p,
        c1 - s1,
        c2 - s2,
        c3 - s3,
        j3m - j1m,
        -(c3 + s3),
        -(c2 + s2),
        -(c1 + s1),
    ]
    return [x + y for x, y in zip(even, odd)]


def rows_loop(rows, body):
    @pl.loop(0, rows // TILE)
    def _(step):
        body(pl.ds(pl.multiple_of(step * TILE, TILE), TILE))


def split_rows(load, mid, rows, width):
    def body(at):
        for r, pair in enumerate(first_stage([load(p, at) for p in range(BLOCKS)])):
            mid[r, at, :width] = pair[0].astype(jnp.bfloat16)
            if pair[1] is not None:
                mid[r, at, width:] = pair[1].astype(jnp.bfloat16)

    rows_loop(rows, body)


def spectrum(mid, table, r, width):
    if r in (0, GROUPS - 1):
        return jnp.dot(mid[r, :, :width], table[r, :width, :], preferred_element_type=jnp.float32)
    return jnp.dot(mid[r], table[r], preferred_element_type=jnp.float32)


def invert_group(product, table, r, width, wide):
    if r in (0, GROUPS - 1):
        wide[r, :, :width] = jnp.dot(product, table[r, :, :width], preferred_element_type=jnp.float32)
    else:
        wide[r] = jnp.dot(product, table[r], preferred_element_type=jnp.float32)


def merge_rows(wide, store, rows, width):
    def body(at):
        parts = []
        for r in range(GROUPS):
            im = None if r in (0, GROUPS - 1) else wide[r, at, width:]
            parts.append((wide[r, at, :width], im))
        for p, value in enumerate(last_stage(parts)):
            store(p, at, value)

    rows_loop(rows, body)


def piece_at(ref, where, k, rows):
    start = pl.multiple_of(lax.bitwise_xor(where[0], k) * rows, rows)
    return ref.at[pl.ds(start, rows), :]


def gate_kernel(order, input_order, where, gate, upper, whole, *refs):
    outs, picks, refs = refs[: len(order)], refs[len(order) : 2 * len(order)], refs[2 * len(order) :]
    left, right, sems, pick_sems = refs
    rows = outs[0].shape[0]
    loads, moves = [], []
    for i, k in enumerate(order):
        pair = (
            pltpu.make_async_copy(piece_at(gate, where, k, rows), left.at[i], sems.at[0, i]),
            pltpu.make_async_copy(piece_at(upper, where, k, rows), right.at[i], sems.at[1, i]),
        )
        for copy in pair:
            copy.start()
        loads.append(pair)
    for i, k in enumerate(input_order):
        moves.append(pltpu.make_async_copy(piece_at(whole, where, k, rows), picks[i], pick_sems.at[i]))
        moves[-1].start()
    for i, out in enumerate(outs):
        for copy in loads[i]:
            copy.wait()
        out[...] = (left[i].astype(jnp.float32) * right[i].astype(jnp.float32)).astype(jnp.bfloat16)
    for copy in moves:
        copy.wait()


def place_kernel(order, where, *refs):
    pieces, whole = refs[:-1], refs[-1]
    for k, piece in zip(order, pieces):
        whole[lax.bitwise_xor(where[0], k)] = piece[...]


def taps_kernel(taps, forward, *refs):
    taps_spec, mid = refs[-2:]
    rows, width = (taps.shape[0], taps.shape[1] // BLOCKS)
    split_rows(lambda p, at: taps[at, p * width : (p + 1) * width], mid, rows, width)
    for r in range(GROUPS):
        taps_spec[r] = spectrum(mid, forward, r, width).astype(taps_spec.dtype)


def ordered(order, where, refs, held):
    span = refs[0].shape[1]
    for k, ref in zip(order, refs):
        start = pl.multiple_of(lax.bitwise_xor(where[0], k) * span, span)
        held[:, pl.ds(start, span)] = ref[...]


def block_of(held, width):
    return lambda p, at: held[at, p * width : (p + 1) * width].astype(jnp.float32)


def block_into(held, width):
    def store(p, at, value):
        held[at, p * width : (p + 1) * width] = value.astype(jnp.bfloat16)

    return store


def back_kernel(order, back_order, late, where, *refs):
    blocks, refs = refs[: len(order)], refs[len(order) + late :]
    taps_spec, forward, backward, *outs, grad_spec, held, mid, wide = refs
    outs = outs[late:]
    rows, width = held.shape[0], held.shape[1] // BLOCKS
    ordered(order, where, blocks, held)
    split_rows(block_of(held, width), mid, rows, width)
    for r in range(GROUPS):
        grad = spectrum(mid, forward, r, width)
        grad_spec[r] = grad.astype(grad_spec.dtype)
        taps = taps_spec[r].astype(jnp.float32)
        gr, gi, hr, hi = grad[:, :width], grad[:, width:], taps[:, :width], taps[:, width:]
        product = jnp.concatenate([hr * gr + hi * gi, hr * gi - hi * gr], axis=1)
        invert_group(product.astype(jnp.bfloat16), backward, r, width, wide)
    merge_rows(wide, block_into(held, width), rows, width)
    span = outs[0].shape[1]
    for k, out in zip(back_order, outs):
        start = pl.multiple_of(lax.bitwise_xor(where[0], k) * span, span)
        out[...] = held[:, pl.ds(start, span)]


def cross_kernel(order, where, *refs):
    blocks, refs = refs[: len(order)], refs[len(order) :]
    grad_spec, forward, backward, *outs, held, mid, wide = refs
    rows, width = held.shape[0], held.shape[1] // BLOCKS
    ordered(order, where, blocks, held)
    split_rows(block_of(held, width), mid, rows, width)
    for r in range(GROUPS):
        signal = spectrum(mid, forward, r, width)
        grad = grad_spec[r].astype(jnp.float32)
        gr, gi, xr, xi = grad[:, :width], grad[:, width:], signal[:, :width], signal[:, width:]
        product = jnp.concatenate([gr * xr + gi * xi, gi * xr - gr * xi], axis=1)
        invert_group(product.astype(jnp.bfloat16), backward, r, width, wide)
    merge_rows(wide, block_into(held, width), rows, width)
    part = held.shape[1] // len(outs)
    for k, out in zip(far_first(len(outs)), outs):
        start = pl.multiple_of(lax.bitwise_xor(where[1], k) * part, part)
        out[...] = held[:, pl.ds(start, part)]


def call(kernel, operands, outs, scratch=(), flops=0, streams=(), out_streams=(), aliases=None, hbm=()):
    def spec(stream):
        return pl.BlockSpec(memory_space=pl.ANY if stream else pltpu.VMEM)

    size = sum(math.prod(o.shape) * o.dtype.itemsize for o in list(operands) + list(outs))
    specs = [spec(i in streams) for i in range(len(operands))]
    for i in hbm:
        specs[i] = pl.BlockSpec(memory_space=pltpu.HBM)
    if operands[0].dtype == jnp.int32:
        specs[0] = pl.BlockSpec(memory_space=pltpu.SMEM)
    outputs = pl.pallas_call(
        kernel,
        out_shape=list(outs),
        in_specs=specs,
        out_specs=[spec(i in out_streams) for i in range(len(outs))],
        scratch_shapes=list(scratch),
        input_output_aliases=aliases or {},
        compiler_params=pltpu.CompilerParams(vmem_limit_bytes=LIMIT),
        cost_estimate=pl.CostEstimate(flops=flops, bytes_accessed=size, transcendentals=0),
    )(*operands)
    return list(outputs)


def far_first(size):
    return [*range(size // 2, size), *range(1, size // 2), 0]


def spread(size, order):
    part = size // 8
    return [k * part + i for k in order for i in range(part)] + [*range(1, part), 0]


def exchange(pieces, order, axis, size):
    moved = []
    for k, piece in zip(order, pieces):
        moved.append(lax.ppermute(piece, axis, [(i, i ^ k) for i in range(size)]) if k else piece)
    return moved


def on_device(saved_input, out_gate, grad_out, long_filter):
    count, shares = lax.axis_size("ctx"), lax.axis_size("dp")
    channels, span = saved_input.shape[1:]
    rows, length = long_filter.shape
    width = length // BLOCKS
    grad_order, input_order, back_order = (spread(count, o) for o in ((4, 1, 5, 2, 6, 7, 3), (4, 1, 5, 2, 6, 3, 7), (1, 4, 2, 5, 6, 7, 3)))
    late = 2
    at = count - 1 - late
    every = range(count + 8)
    where = jnp.stack([lax.axis_index("ctx"), lax.axis_index("dp")]).astype(jnp.int32)
    forward, backward = (jnp.asarray(t) for t in transform_tables(width))
    half, full = jnp.bfloat16, jnp.float32
    piece = jax.ShapeDtypeStruct((rows, span), half)
    spec = jax.ShapeDtypeStruct((GROUPS, rows, 2 * width), half)
    held = pltpu.VMEM((rows, length), half)
    mid = pltpu.VMEM((GROUPS, rows, 2 * width), half)
    wide = pltpu.VMEM((GROUPS, rows, 2 * width), full)
    slots = pltpu.VMEM((count, rows, span), half)
    sems = pltpu.SemaphoreType.DMA
    work = 2 * GROUPS * rows * 4 * width * width

    pieces = call(
        functools.partial(gate_kernel, grad_order, input_order),
        [where, *(pltpu.with_memory_space_constraint(x[0], pltpu.HBM) for x in (out_gate, grad_out, saved_input))],
        [piece] * (2 * count),
        [slots, slots, sems((2, count)), sems((count,))],
        hbm=(1, 2, 3),
    )
    grad_pieces, input_pieces = pieces[:count], pieces[count:]
    grad_blocks = exchange(grad_pieces, grad_order, "ctx", count)
    ahead = 5
    *input_pieces[:ahead], taps_spec = call(
        taps_kernel,
        [long_filter, forward, *input_pieces[:ahead]],
        [piece] * ahead + [spec],
        [mid],
        flops=work,
        streams=range(2, 2 + ahead),
        out_streams=range(ahead),
        aliases={2 + i: i for i in range(ahead)},
    )
    passed = [*input_pieces[at : at + late]]
    *back, grad_spec = call(
        functools.partial(back_kernel, grad_order, back_order, late),
        [where, *grad_blocks, *passed, taps_spec, forward, backward],
        [piece] * (late + count) + [spec],
        [held, mid, wide],
        flops=2 * work,
        streams=range(1 + count, 1 + count + late),
        out_streams=range(late),
        aliases={1 + count + i: i for i in range(late)},
    )
    input_pieces[at : at + late], back = back[:late], back[late:]
    input_blocks = exchange(input_pieces, input_order, "ctx", count)
    back_blocks = exchange(back, back_order, "ctx", count)
    share = jax.ShapeDtypeStruct((rows, length // shares), half)
    cross = call(
        functools.partial(cross_kernel, input_order),
        [where, *input_blocks, grad_spec, forward, backward],
        [share] * shares,
        [held, mid, wide],
        flops=2 * work,
    )
    cross_blocks = exchange(cross, far_first(shares), "dp", shares)
    scale = 1.0 / math.sqrt(shares * length)
    grad_filter = sum(x.astype(full) for x in cross_blocks) * scale
    (whole,) = call(
        functools.partial(place_kernel, back_order),
        [where, *back_blocks],
        [jax.ShapeDtypeStruct((count, rows, span), half)],
    )
    return (whole.reshape(1, channels, span), grad_filter)


def solution(mesh):
    in_specs = (P("dp", None, "ctx"), P("dp", None, "ctx"), P("dp", None, "ctx"), P("ctx", None))
    out_specs = (P("dp", None, "ctx"), P("ctx", "dp"))
    return jax.shard_map(
        on_device, mesh=mesh, in_specs=in_specs, out_specs=out_specs, check_vma=False
    )
```

```python
import functools
import math

import jax
import jax.numpy as jnp
import ml_dtypes
import numpy as np
from jax import lax
from jax.experimental import pallas as pl
from jax.experimental.pallas import tpu as pltpu
from jax.sharding import PartitionSpec as P

BLOCKS = 8
GROUPS = 9
TILE = 16
C1 = math.cos(math.pi / 8)
C2 = math.cos(math.pi / 4)
C3 = math.cos(3 * math.pi / 8)
LIMIT = 32 * 1024 * 1024


def transform_tables(width):
    points = 2 * BLOCKS * width
    row = np.arange(width)
    forward = np.zeros((GROUPS, 2 * width, 2 * width), np.float64)
    for r in range(GROUPS):
        angle = 2.0 * np.pi * (np.outer(row, 16 * row + r) % points) / points
        cos, sin = np.cos(angle), np.sin(angle)
        forward[r] = np.block([[cos, -sin], [sin, cos]])
    scale = np.full((GROUPS, 1, 1), 2.0 / points)
    scale[0] = scale[-1] = 1.0 / points
    backward = np.swapaxes(forward, 1, 2) * scale
    return forward.astype(ml_dtypes.bfloat16), backward.astype(ml_dtypes.bfloat16)


def first_stage(b):
    e = [b[p] + b[p + 4] for p in range(4)]
    f = [b[p] - b[p + 4] for p in range(4)]
    e02, e13 = e[0] + e[2], e[1] + e[3]
    fd, fs = C2 * (f[1] - f[3]), C2 * (f[1] + f[3])
    d = [None] + [b[p] - b[8 - p] for p in (1, 2, 3)]
    g = [None] + [b[p] + b[8 - p] for p in (1, 2, 3)]
    d2, g2 = C2 * d[2], C2 * g[2]
    re1, re3 = C1 * d[1] + C3 * d[3], C3 * d[1] - C1 * d[3]
    im1, im3 = C3 * g[1] + C1 * g[3], C1 * g[1] - C3 * g[3]
    up, down = b[0] + d2, b[0] - d2
    bp, bm = b[4] + g2, b[4] - g2
    return [
        (e02 + e13, None),
        (up + re1, -(bp + im1)),
        (f[0] + fd, -(f[2] + fs)),
        (down + re3, bm - im3),
        (e[0] - e[2], e[3] - e[1]),
        (down - re3, -(bm + im3)),
        (f[0] - fd, f[2] - fs),
        (up - re1, bp - im1),
        (e02 - e13, None),
    ]


def last_stage(u):
    re = [pair[0] for pair in u]
    im = [pair[1] for pair in u]
    sum08, dif08 = re[0] + re[8], re[0] - re[8]
    r26, i26 = re[2] + re[6], im[2] - im[6]
    rd, sd = C2 * (re[2] - re[6]), C2 * (im[2] + im[6])
    top, low = sum08 + re[4], sum08 - re[4]
    dp, dm = dif08 + rd, dif08 - rd
    ip, im4 = sd + im[4], sd - im[4]
    even = [
        top + r26,
        dp - ip,
        low - i26,
        dm - im4,
        top - r26,
        dm + im4,
        low + i26,
        dp + ip,
    ]
    a1p, a1m = re[1] + re[7], re[1] - re[7]
    a3p, a3m = re[3] + re[5], re[3] - re[5]
    j1p, j1m = im[1] + im[7], im[1] - im[7]
    j3p, j3m = im[3] + im[5], im[3] - im[5]
    c1, c3 = C1 * a1m + C3 * a3m, C3 * a1m - C1 * a3m
    c2 = C2 * (a1p - a3p)
    s1, s3 = C3 * j1p + C1 * j3p, C1 * j1p - C3 * j3p
    s2 = C2 * (j1m + j3m)
    odd = [
        a1p + a3p,
        c1 - s1,
        c2 - s2,
        c3 - s3,
        j3m - j1m,
        -(c3 + s3),
        -(c2 + s2),
        -(c1 + s1),
    ]
    return [x + y for x, y in zip(even, odd)]


def rows_loop(rows, body):
    @pl.loop(0, rows // TILE)
    def _(step):
        body(pl.ds(pl.multiple_of(step * TILE, TILE), TILE))


def split_rows(load, mid, rows, width):
    def body(at):
        for r, pair in enumerate(first_stage([load(p, at) for p in range(BLOCKS)])):
            mid[r, at, :width] = pair[0].astype(jnp.bfloat16)
            if pair[1] is not None:
                mid[r, at, width:] = pair[1].astype(jnp.bfloat16)

    rows_loop(rows, body)


def spectrum(mid, table, r, width):
    if r in (0, GROUPS - 1):
        return jnp.dot(mid[r, :, :width], table[r, :width, :], preferred_element_type=jnp.float32)
    return jnp.dot(mid[r], table[r], preferred_element_type=jnp.float32)


def invert_group(product, table, r, width, wide):
    if r in (0, GROUPS - 1):
        wide[r, :, :width] = jnp.dot(product, table[r, :, :width], preferred_element_type=jnp.float32)
    else:
        wide[r] = jnp.dot(product, table[r], preferred_element_type=jnp.float32)


def merge_rows(wide, store, rows, width):
    def body(at):
        parts = []
        for r in range(GROUPS):
            im = None if r in (0, GROUPS - 1) else wide[r, at, width:]
            parts.append((wide[r, at, :width], im))
        for p, value in enumerate(last_stage(parts)):
            store(p, at, value)

    rows_loop(rows, body)


def piece_at(ref, where, k, rows):
    start = pl.multiple_of(lax.bitwise_xor(where[0], k) * rows, rows)
    return ref.at[pl.ds(start, rows), :]


def gate_kernel(order, where, gate, upper, *refs):
    outs, (left, right, sems) = refs[: len(order)], refs[len(order) :]
    rows = outs[0].shape[0]
    loads = []
    for i, k in enumerate(order):
        pair = (
            pltpu.make_async_copy(piece_at(gate, where, k, rows), left.at[i], sems.at[0, i]),
            pltpu.make_async_copy(piece_at(upper, where, k, rows), right.at[i], sems.at[1, i]),
        )
        for copy in pair:
            copy.start()
        loads.append(pair)
    for i, out in enumerate(outs):
        for copy in loads[i]:
            copy.wait()
        out[...] = (left[i].astype(jnp.float32) * right[i].astype(jnp.float32)).astype(jnp.bfloat16)


def place_kernel(order, where, *refs):
    pieces, whole = refs[:-1], refs[-1]
    for k, piece in zip(order, pieces):
        whole[lax.bitwise_xor(where[0], k)] = piece[...]


def taps_kernel(order, where, whole, taps, forward, *refs):
    picks, (taps_spec, mid, sems) = refs[: len(order)], refs[len(order) :]
    rows, width = (taps.shape[0], taps.shape[1] // BLOCKS)
    moves = []
    for i, k in enumerate(order):
        moves.append(pltpu.make_async_copy(piece_at(whole, where, k, rows), picks[i], sems.at[i]))
        moves[-1].start()
    split_rows(lambda p, at: taps[at, p * width : (p + 1) * width], mid, rows, width)
    for r in range(GROUPS):
        taps_spec[r] = spectrum(mid, forward, r, width).astype(taps_spec.dtype)
    for copy in moves:
        copy.wait()


def ordered(order, where, refs, held):
    span = refs[0].shape[1]
    for k, ref in zip(order, refs):
        start = pl.multiple_of(lax.bitwise_xor(where[0], k) * span, span)
        held[:, pl.ds(start, span)] = ref[...]


def block_of(held, width):
    return lambda p, at: held[at, p * width : (p + 1) * width].astype(jnp.float32)


def block_into(held, width):
    def store(p, at, value):
        held[at, p * width : (p + 1) * width] = value.astype(jnp.bfloat16)

    return store


def back_kernel(order, back_order, late, where, *refs):
    blocks, refs = refs[: len(order)], refs[len(order) + late :]
    taps_spec, forward, backward, *outs, grad_spec, held, mid, wide = refs
    outs = outs[late:]
    rows, width = held.shape[0], held.shape[1] // BLOCKS
    ordered(order, where, blocks, held)
    split_rows(block_of(held, width), mid, rows, width)
    for r in range(GROUPS):
        grad = spectrum(mid, forward, r, width)
        grad_spec[r] = grad.astype(grad_spec.dtype)
        taps = taps_spec[r].astype(jnp.float32)
        gr, gi, hr, hi = grad[:, :width], grad[:, width:], taps[:, :width], taps[:, width:]
        product = jnp.concatenate([hr * gr + hi * gi, hr * gi - hi * gr], axis=1)
        invert_group(product.astype(jnp.bfloat16), backward, r, width, wide)
    merge_rows(wide, block_into(held, width), rows, width)
    span = outs[0].shape[1]
    for k, out in zip(back_order, outs):
        start = pl.multiple_of(lax.bitwise_xor(where[0], k) * span, span)
        out[...] = held[:, pl.ds(start, span)]


def cross_kernel(order, where, *refs):
    blocks, refs = refs[: len(order)], refs[len(order) :]
    grad_spec, forward, backward, *outs, held, mid, wide = refs
    rows, width = held.shape[0], held.shape[1] // BLOCKS
    ordered(order, where, blocks, held)
    split_rows(block_of(held, width), mid, rows, width)
    for r in range(GROUPS):
        signal = spectrum(mid, forward, r, width)
        grad = grad_spec[r].astype(jnp.float32)
        gr, gi, xr, xi = grad[:, :width], grad[:, width:], signal[:, :width], signal[:, width:]
        product = jnp.concatenate([gr * xr + gi * xi, gi * xr - gr * xi], axis=1)
        invert_group(product.astype(jnp.bfloat16), backward, r, width, wide)
    merge_rows(wide, block_into(held, width), rows, width)
    part = held.shape[1] // len(outs)
    for k, out in zip(far_first(len(outs)), outs):
        start = pl.multiple_of(lax.bitwise_xor(where[1], k) * part, part)
        out[...] = held[:, pl.ds(start, part)]


def call(kernel, operands, outs, scratch=(), flops=0, streams=(), out_streams=(), aliases=None, hbm=()):
    def spec(stream):
        return pl.BlockSpec(memory_space=pl.ANY if stream else pltpu.VMEM)

    size = sum(math.prod(o.shape) * o.dtype.itemsize for o in list(operands) + list(outs))
    specs = [spec(i in streams) for i in range(len(operands))]
    for i in hbm:
        specs[i] = pl.BlockSpec(memory_space=pltpu.HBM)
    if operands[0].dtype == jnp.int32:
        specs[0] = pl.BlockSpec(memory_space=pltpu.SMEM)
    outputs = pl.pallas_call(
        kernel,
        out_shape=list(outs),
        in_specs=specs,
        out_specs=[spec(i in out_streams) for i in range(len(outs))],
        scratch_shapes=list(scratch),
        input_output_aliases=aliases or {},
        compiler_params=pltpu.CompilerParams(vmem_limit_bytes=LIMIT),
        cost_estimate=pl.CostEstimate(flops=flops, bytes_accessed=size, transcendentals=0),
    )(*operands)
    return list(outputs)


def far_first(size):
    return [*range(size // 2, size), *range(1, size // 2), 0]


def spread(size, order):
    part = size // 8
    return [k * part + i for k in order for i in range(part)] + [*range(1, part), 0]


def exchange(pieces, order, axis, size):
    moved = []
    for k, piece in zip(order, pieces):
        moved.append(lax.ppermute(piece, axis, [(i, i ^ k) for i in range(size)]) if k else piece)
    return moved


def on_device(saved_input, out_gate, grad_out, long_filter):
    count, shares = lax.axis_size("ctx"), lax.axis_size("dp")
    channels, span = saved_input.shape[1:]
    rows, length = long_filter.shape
    width = length // BLOCKS
    grad_order, input_order, back_order = (spread(count, o) for o in ((4, 1, 5, 2, 6, 7, 3), (4, 5, 6, 1, 2, 7, 3), (1, 4, 2, 5, 6, 7, 3)))
    late = 2
    at = count - 1 - late
    every = range(count + 8)
    where = jnp.stack([lax.axis_index("ctx"), lax.axis_index("dp")]).astype(jnp.int32)
    forward, backward = (jnp.asarray(t) for t in transform_tables(width))
    half, full = jnp.bfloat16, jnp.float32
    piece = jax.ShapeDtypeStruct((rows, span), half)
    spec = jax.ShapeDtypeStruct((GROUPS, rows, 2 * width), half)
    held = pltpu.VMEM((rows, length), half)
    mid = pltpu.VMEM((GROUPS, rows, 2 * width), half)
    wide = pltpu.VMEM((GROUPS, rows, 2 * width), full)
    slots = pltpu.VMEM((count, rows, span), half)
    sems = pltpu.SemaphoreType.DMA
    work = 2 * GROUPS * rows * 4 * width * width

    stay = [pltpu.with_memory_space_constraint(x[0], pltpu.HBM) for x in (out_gate, grad_out, saved_input)]
    grad_pieces = call(
        functools.partial(gate_kernel, grad_order),
        [where, *stay[:2]],
        [piece] * count,
        [slots, slots, sems((2, count))],
        hbm=(1, 2),
    )
    grad_blocks = exchange(grad_pieces, grad_order, "ctx", count)
    *input_pieces, taps_spec = call(
        functools.partial(taps_kernel, input_order),
        [where, stay[2], long_filter, forward],
        [piece] * count + [spec],
        [mid, sems((count,))],
        flops=work,
        hbm=(1,),
    )
    passed = [*input_pieces[at : at + late]]
    *back, grad_spec = call(
        functools.partial(back_kernel, grad_order, back_order, late),
        [where, *grad_blocks, *passed, taps_spec, forward, backward],
        [piece] * (late + count) + [spec],
        [held, mid, wide],
        flops=2 * work,
        streams=range(1 + count, 1 + count + late),
        out_streams=range(late),
        aliases={1 + count + i: i for i in range(late)},
    )
    input_pieces[at : at + late], back = back[:late], back[late:]
    input_blocks = exchange(input_pieces, input_order, "ctx", count)
    back_blocks = exchange(back, back_order, "ctx", count)
    share = jax.ShapeDtypeStruct((rows, length // shares), half)
    cross = call(
        functools.partial(cross_kernel, input_order),
        [where, *input_blocks, grad_spec, forward, backward],
        [share] * shares,
        [held, mid, wide],
        flops=2 * work,
    )
    cross_blocks = exchange(cross, far_first(shares), "dp", shares)
    scale = 1.0 / math.sqrt(shares * length)
    grad_filter = sum(x.astype(full) for x in cross_blocks) * scale
    (whole,) = call(
        functools.partial(place_kernel, back_order),
        [where, *back_blocks],
        [jax.ShapeDtypeStruct((count, rows, span), half)],
    )
    return (whole.reshape(1, channels, span), grad_filter)


def solution(mesh):
    in_specs = (P("dp", None, "ctx"), P("dp", None, "ctx"), P("dp", None, "ctx"), P("ctx", None))
    out_specs = (P("dp", None, "ctx"), P("ctx", "dp"))
    return jax.shard_map(
        on_device, mesh=mesh, in_specs=in_specs, out_specs=out_specs, check_vma=False
    )
```

```python
import functools
import math

import jax
import jax.numpy as jnp
import ml_dtypes
import numpy as np
from jax import lax
from jax.experimental import pallas as pl
from jax.experimental.pallas import tpu as pltpu
from jax.sharding import PartitionSpec as P

BLOCKS = 8
GROUPS = 9
TILE = 16
C1 = math.cos(math.pi / 8)
C2 = math.cos(math.pi / 4)
C3 = math.cos(3 * math.pi / 8)
LIMIT = 32 * 1024 * 1024


def transform_tables(width):
    points = 2 * BLOCKS * width
    row = np.arange(width)
    forward = np.zeros((GROUPS, 2 * width, 2 * width), np.float64)
    for r in range(GROUPS):
        angle = 2.0 * np.pi * (np.outer(row, 16 * row + r) % points) / points
        cos, sin = np.cos(angle), np.sin(angle)
        forward[r] = np.block([[cos, -sin], [sin, cos]])
    scale = np.full((GROUPS, 1, 1), 2.0 / points)
    scale[0] = scale[-1] = 1.0 / points
    backward = np.swapaxes(forward, 1, 2) * scale
    return forward.astype(ml_dtypes.bfloat16), backward.astype(ml_dtypes.bfloat16)


def first_stage(b):
    e = [b[p] + b[p + 4] for p in range(4)]
    f = [b[p] - b[p + 4] for p in range(4)]
    e02, e13 = e[0] + e[2], e[1] + e[3]
    fd, fs = C2 * (f[1] - f[3]), C2 * (f[1] + f[3])
    d = [None] + [b[p] - b[8 - p] for p in (1, 2, 3)]
    g = [None] + [b[p] + b[8 - p] for p in (1, 2, 3)]
    d2, g2 = C2 * d[2], C2 * g[2]
    re1, re3 = C1 * d[1] + C3 * d[3], C3 * d[1] - C1 * d[3]
    im1, im3 = C3 * g[1] + C1 * g[3], C1 * g[1] - C3 * g[3]
    up, down = b[0] + d2, b[0] - d2
    bp, bm = b[4] + g2, b[4] - g2
    return [
        (e02 + e13, None),
        (up + re1, -(bp + im1)),
        (f[0] + fd, -(f[2] + fs)),
        (down + re3, bm - im3),
        (e[0] - e[2], e[3] - e[1]),
        (down - re3, -(bm + im3)),
        (f[0] - fd, f[2] - fs),
        (up - re1, bp - im1),
        (e02 - e13, None),
    ]


def last_stage(u):
    re = [pair[0] for pair in u]
    im = [pair[1] for pair in u]
    sum08, dif08 = re[0] + re[8], re[0] - re[8]
    r26, i26 = re[2] + re[6], im[2] - im[6]
    rd, sd = C2 * (re[2] - re[6]), C2 * (im[2] + im[6])
    top, low = sum08 + re[4], sum08 - re[4]
    dp, dm = dif08 + rd, dif08 - rd
    ip, im4 = sd + im[4], sd - im[4]
    even = [
        top + r26,
        dp - ip,
        low - i26,
        dm - im4,
        top - r26,
        dm + im4,
        low + i26,
        dp + ip,
    ]
    a1p, a1m = re[1] + re[7], re[1] - re[7]
    a3p, a3m = re[3] + re[5], re[3] - re[5]
    j1p, j1m = im[1] + im[7], im[1] - im[7]
    j3p, j3m = im[3] + im[5], im[3] - im[5]
    c1, c3 = C1 * a1m + C3 * a3m, C3 * a1m - C1 * a3m
    c2 = C2 * (a1p - a3p)
    s1, s3 = C3 * j1p + C1 * j3p, C1 * j1p - C3 * j3p
    s2 = C2 * (j1m + j3m)
    odd = [
        a1p + a3p,
        c1 - s1,
        c2 - s2,
        c3 - s3,
        j3m - j1m,
        -(c3 + s3),
        -(c2 + s2),
        -(c1 + s1),
    ]
    return [x + y for x, y in zip(even, odd)]


def rows_loop(rows, body):
    @pl.loop(0, rows // TILE)
    def _(step):
        body(pl.ds(pl.multiple_of(step * TILE, TILE), TILE))


def split_rows(load, mid, rows, width):
    def body(at):
        for r, pair in enumerate(first_stage([load(p, at) for p in range(BLOCKS)])):
            mid[r, at, :width] = pair[0].astype(jnp.bfloat16)
            if pair[1] is not None:
                mid[r, at, width:] = pair[1].astype(jnp.bfloat16)

    rows_loop(rows, body)


def spectrum(mid, table, r, width):
    if r in (0, GROUPS - 1):
        return jnp.dot(mid[r, :, :width], table[r, :width, :], preferred_element_type=jnp.float32)
    return jnp.dot(mid[r], table[r], preferred_element_type=jnp.float32)


def invert_group(product, table, r, width, wide):
    if r in (0, GROUPS - 1):
        wide[r, :, :width] = jnp.dot(product, table[r, :, :width], preferred_element_type=jnp.float32)
    else:
        wide[r] = jnp.dot(product, table[r], preferred_element_type=jnp.float32)


def merge_rows(wide, store, rows, width):
    def body(at):
        parts = []
        for r in range(GROUPS):
            im = None if r in (0, GROUPS - 1) else wide[r, at, width:]
            parts.append((wide[r, at, :width], im))
        for p, value in enumerate(last_stage(parts)):
            store(p, at, value)

    rows_loop(rows, body)


def piece_at(ref, where, k, rows):
    start = pl.multiple_of(lax.bitwise_xor(where[0], k) * rows, rows)
    return ref.at[pl.ds(start, rows), :]


def gate_kernel(order, where, gate, upper, *refs):
    outs, (left, right, sems) = refs[: len(order)], refs[len(order) :]
    rows = outs[0].shape[0]
    loads = []
    for i, k in enumerate(order):
        pair = (
            pltpu.make_async_copy(piece_at(gate, where, k, rows), left.at[i], sems.at[0, i]),
            pltpu.make_async_copy(piece_at(upper, where, k, rows), right.at[i], sems.at[1, i]),
        )
        for copy in pair:
            copy.start()
        loads.append(pair)
    for i, out in enumerate(outs):
        for copy in loads[i]:
            copy.wait()
        out[...] = (left[i].astype(jnp.float32) * right[i].astype(jnp.float32)).astype(jnp.bfloat16)


def finish_kernel(order, scale, where, *refs):
    pieces, shares, (whole, total) = refs[: len(order)], refs[len(order) : -2], refs[-2:]
    added = shares[0][...].astype(jnp.float32)
    for share in shares[1:]:
        added = added + share[...].astype(jnp.float32)
    total[...] = added * scale
    for k, piece in zip(order, pieces):
        whole[lax.bitwise_xor(where[0], k)] = piece[...]


def taps_kernel(order, where, whole, taps, forward, *refs):
    picks, (taps_spec, mid, sems) = refs[: len(order)], refs[len(order) :]
    rows, width = (taps.shape[0], taps.shape[1] // BLOCKS)
    moves = []
    for i, k in enumerate(order):
        moves.append(pltpu.make_async_copy(piece_at(whole, where, k, rows), picks[i], sems.at[i]))
        moves[-1].start()
    split_rows(lambda p, at: taps[at, p * width : (p + 1) * width], mid, rows, width)
    for r in range(GROUPS):
        taps_spec[r] = spectrum(mid, forward, r, width).astype(taps_spec.dtype)
    for copy in moves:
        copy.wait()


def ordered(order, where, refs, held):
    span = refs[0].shape[1]
    for k, ref in zip(order, refs):
        start = pl.multiple_of(lax.bitwise_xor(where[0], k) * span, span)
        held[:, pl.ds(start, span)] = ref[...]


def block_of(held, width):
    return lambda p, at: held[at, p * width : (p + 1) * width].astype(jnp.float32)


def block_into(held, width):
    def store(p, at, value):
        held[at, p * width : (p + 1) * width] = value.astype(jnp.bfloat16)

    return store


def back_kernel(order, back_order, late, where, *refs):
    blocks, refs = refs[: len(order)], refs[len(order) + late :]
    taps_spec, forward, backward, *outs, grad_spec, held, mid, wide = refs
    outs = outs[late:]
    rows, width = held.shape[0], held.shape[1] // BLOCKS
    ordered(order, where, blocks, held)
    split_rows(block_of(held, width), mid, rows, width)
    for r in range(GROUPS):
        grad = spectrum(mid, forward, r, width)
        grad_spec[r] = grad.astype(grad_spec.dtype)
        taps = taps_spec[r].astype(jnp.float32)
        gr, gi, hr, hi = grad[:, :width], grad[:, width:], taps[:, :width], taps[:, width:]
        product = jnp.concatenate([hr * gr + hi * gi, hr * gi - hi * gr], axis=1)
        invert_group(product.astype(jnp.bfloat16), backward, r, width, wide)
    merge_rows(wide, block_into(held, width), rows, width)
    span = outs[0].shape[1]
    for k, out in zip(back_order, outs):
        start = pl.multiple_of(lax.bitwise_xor(where[0], k) * span, span)
        out[...] = held[:, pl.ds(start, span)]


def cross_kernel(order, where, *refs):
    blocks, refs = refs[: len(order)], refs[len(order) :]
    grad_spec, forward, backward, *outs, held, mid, wide = refs
    rows, width = held.shape[0], held.shape[1] // BLOCKS
    ordered(order, where, blocks, held)
    split_rows(block_of(held, width), mid, rows, width)
    for r in range(GROUPS):
        signal = spectrum(mid, forward, r, width)
        grad = grad_spec[r].astype(jnp.float32)
        gr, gi, xr, xi = grad[:, :width], grad[:, width:], signal[:, :width], signal[:, width:]
        product = jnp.concatenate([gr * xr + gi * xi, gi * xr - gr * xi], axis=1)
        invert_group(product.astype(jnp.bfloat16), backward, r, width, wide)
    merge_rows(wide, block_into(held, width), rows, width)
    part = held.shape[1] // len(outs)
    for k, out in zip(far_first(len(outs)), outs):
        start = pl.multiple_of(lax.bitwise_xor(where[1], k) * part, part)
        out[...] = held[:, pl.ds(start, part)]


def call(kernel, operands, outs, scratch=(), flops=0, streams=(), out_streams=(), aliases=None, hbm=()):
    def spec(stream):
        return pl.BlockSpec(memory_space=pl.ANY if stream else pltpu.VMEM)

    size = sum(math.prod(o.shape) * o.dtype.itemsize for o in list(operands) + list(outs))
    specs = [spec(i in streams) for i in range(len(operands))]
    for i in hbm:
        specs[i] = pl.BlockSpec(memory_space=pltpu.HBM)
    if operands[0].dtype == jnp.int32:
        specs[0] = pl.BlockSpec(memory_space=pltpu.SMEM)
    outputs = pl.pallas_call(
        kernel,
        out_shape=list(outs),
        in_specs=specs,
        out_specs=[spec(i in out_streams) for i in range(len(outs))],
        scratch_shapes=list(scratch),
        input_output_aliases=aliases or {},
        compiler_params=pltpu.CompilerParams(vmem_limit_bytes=LIMIT),
        cost_estimate=pl.CostEstimate(flops=flops, bytes_accessed=size, transcendentals=0),
    )(*operands)
    return list(outputs)


def far_first(size):
    return [*range(size // 2, size), *range(1, size // 2), 0]


def spread(size, order):
    part = size // 8
    return [k * part + i for k in order for i in range(part)] + [*range(1, part), 0]


def exchange(pieces, order, axis, size):
    moved = []
    for k, piece in zip(order, pieces):
        moved.append(lax.ppermute(piece, axis, [(i, i ^ k) for i in range(size)]) if k else piece)
    return moved


def on_device(saved_input, out_gate, grad_out, long_filter):
    count, shares = lax.axis_size("ctx"), lax.axis_size("dp")
    channels, span = saved_input.shape[1:]
    rows, length = long_filter.shape
    width = length // BLOCKS
    grad_order, input_order, back_order = (spread(count, o) for o in ((4, 1, 5, 2, 6, 7, 3), (4, 5, 6, 1, 7, 2, 3), (1, 4, 2, 5, 6, 7, 3)))
    late = 3
    at = count - 1 - late
    every = range(count + 8)
    where = jnp.stack([lax.axis_index("ctx"), lax.axis_index("dp")]).astype(jnp.int32)
    forward, backward = (jnp.asarray(t) for t in transform_tables(width))
    half, full = jnp.bfloat16, jnp.float32
    piece = jax.ShapeDtypeStruct((rows, span), half)
    spec = jax.ShapeDtypeStruct((GROUPS, rows, 2 * width), half)
    held = pltpu.VMEM((rows, length), half)
    mid = pltpu.VMEM((GROUPS, rows, 2 * width), half)
    wide = pltpu.VMEM((GROUPS, rows, 2 * width), full)
    slots = pltpu.VMEM((count, rows, span), half)
    sems = pltpu.SemaphoreType.DMA
    work = 2 * GROUPS * rows * 4 * width * width

    stay = [pltpu.with_memory_space_constraint(x[0], pltpu.HBM) for x in (out_gate, grad_out, saved_input)]
    grad_pieces = call(
        functools.partial(gate_kernel, grad_order),
        [where, *stay[:2]],
        [piece] * count,
        [slots, slots, sems((2, count))],
        hbm=(1, 2),
    )
    grad_blocks = exchange(grad_pieces, grad_order, "ctx", count)
    *input_pieces, taps_spec = call(
        functools.partial(taps_kernel, input_order),
        [where, stay[2], long_filter, forward],
        [piece] * count + [spec],
        [mid, sems((count,))],
        flops=work,
        hbm=(1,),
    )
    passed = [*input_pieces[at : at + late]]
    *back, grad_spec = call(
        functools.partial(back_kernel, grad_order, back_order, late),
        [where, *grad_blocks, *passed, taps_spec, forward, backward],
        [piece] * (late + count) + [spec],
        [held, mid, wide],
        flops=2 * work,
        streams=range(1 + count, 1 + count + late),
        out_streams=range(late),
        aliases={1 + count + i: i for i in range(late)},
    )
    input_pieces[at : at + late], back = back[:late], back[late:]
    input_blocks = exchange(input_pieces, input_order, "ctx", count)
    back_blocks = exchange(back, back_order, "ctx", count)
    share = jax.ShapeDtypeStruct((rows, length // shares), half)
    cross = call(
        functools.partial(cross_kernel, input_order),
        [where, *input_blocks, grad_spec, forward, backward],
        [share] * shares,
        [held, mid, wide],
        flops=2 * work,
    )
    cross_blocks = exchange(cross, far_first(shares), "dp", shares)
    scale = 1.0 / math.sqrt(shares * length)
    whole, grad_filter = call(
        functools.partial(finish_kernel, back_order, scale),
        [where, *back_blocks, *cross_blocks],
        [jax.ShapeDtypeStruct((count, rows, span), half), jax.ShapeDtypeStruct((rows, length // shares), full)],
    )
    return (whole.reshape(1, channels, span), grad_filter)


def solution(mesh):
    in_specs = (P("dp", None, "ctx"), P("dp", None, "ctx"), P("dp", None, "ctx"), P("ctx", None))
    out_specs = (P("dp", None, "ctx"), P("ctx", "dp"))
    return jax.shard_map(
        on_device, mesh=mesh, in_specs=in_specs, out_specs=out_specs, check_vma=False
    )
```

```python
import functools
import math

import jax
import jax.numpy as jnp
import ml_dtypes
import numpy as np
from jax import lax
from jax.experimental import pallas as pl
from jax.experimental.pallas import tpu as pltpu
from jax.sharding import PartitionSpec as P

BLOCKS = 8
GROUPS = 9
TILE = 16
C1 = math.cos(math.pi / 8)
C2 = math.cos(math.pi / 4)
C3 = math.cos(3 * math.pi / 8)
LIMIT = 32 * 1024 * 1024


def transform_tables(width):
    points = 2 * BLOCKS * width
    row = np.arange(width)
    forward = np.zeros((GROUPS, 2 * width, 2 * width), np.float64)
    for r in range(GROUPS):
        angle = 2.0 * np.pi * (np.outer(row, 16 * row + r) % points) / points
        cos, sin = np.cos(angle), np.sin(angle)
        forward[r] = np.block([[cos, -sin], [sin, cos]])
    scale = np.full((GROUPS, 1, 1), 2.0 / points)
    scale[0] = scale[-1] = 1.0 / points
    backward = np.swapaxes(forward, 1, 2) * scale
    return forward.astype(ml_dtypes.bfloat16), backward.astype(ml_dtypes.bfloat16)


def first_stage(b):
    e = [b[p] + b[p + 4] for p in range(4)]
    f = [b[p] - b[p + 4] for p in range(4)]
    e02, e13 = e[0] + e[2], e[1] + e[3]
    fd, fs = C2 * (f[1] - f[3]), C2 * (f[1] + f[3])
    d = [None] + [b[p] - b[8 - p] for p in (1, 2, 3)]
    g = [None] + [b[p] + b[8 - p] for p in (1, 2, 3)]
    d2, g2 = C2 * d[2], C2 * g[2]
    re1, re3 = C1 * d[1] + C3 * d[3], C3 * d[1] - C1 * d[3]
    im1, im3 = C3 * g[1] + C1 * g[3], C1 * g[1] - C3 * g[3]
    up, down = b[0] + d2, b[0] - d2
    bp, bm = b[4] + g2, b[4] - g2
    return [
        (e02 + e13, None),
        (up + re1, -(bp + im1)),
        (f[0] + fd, -(f[2] + fs)),
        (down + re3, bm - im3),
        (e[0] - e[2], e[3] - e[1]),
        (down - re3, -(bm + im3)),
        (f[0] - fd, f[2] - fs),
        (up - re1, bp - im1),
        (e02 - e13, None),
    ]


def last_stage(u):
    re = [pair[0] for pair in u]
    im = [pair[1] for pair in u]
    sum08, dif08 = re[0] + re[8], re[0] - re[8]
    r26, i26 = re[2] + re[6], im[2] - im[6]
    rd, sd = C2 * (re[2] - re[6]), C2 * (im[2] + im[6])
    top, low = sum08 + re[4], sum08 - re[4]
    dp, dm = dif08 + rd, dif08 - rd
    ip, im4 = sd + im[4], sd - im[4]
    even = [
        top + r26,
        dp - ip,
        low - i26,
        dm - im4,
        top - r26,
        dm + im4,
        low + i26,
        dp + ip,
    ]
    a1p, a1m = re[1] + re[7], re[1] - re[7]
    a3p, a3m = re[3] + re[5], re[3] - re[5]
    j1p, j1m = im[1] + im[7], im[1] - im[7]
    j3p, j3m = im[3] + im[5], im[3] - im[5]
    c1, c3 = C1 * a1m + C3 * a3m, C3 * a1m - C1 * a3m
    c2 = C2 * (a1p - a3p)
    s1, s3 = C3 * j1p + C1 * j3p, C1 * j1p - C3 * j3p
    s2 = C2 * (j1m + j3m)
    odd = [
        a1p + a3p,
        c1 - s1,
        c2 - s2,
        c3 - s3,
        j3m - j1m,
        -(c3 + s3),
        -(c2 + s2),
        -(c1 + s1),
    ]
    return [x + y for x, y in zip(even, odd)]


def rows_loop(rows, body):
    @pl.loop(0, rows // TILE)
    def _(step):
        body(pl.ds(pl.multiple_of(step * TILE, TILE), TILE))


def split_rows(load, mid, rows, width):
    def body(at):
        for r, pair in enumerate(first_stage([load(p, at) for p in range(BLOCKS)])):
            mid[r, at, :width] = pair[0].astype(jnp.bfloat16)
            if pair[1] is not None:
                mid[r, at, width:] = pair[1].astype(jnp.bfloat16)

    rows_loop(rows, body)


def spectrum(mid, table, r, width):
    if r in (0, GROUPS - 1):
        return jnp.dot(mid[r, :, :width], table[r, :width, :], preferred_element_type=jnp.float32)
    return jnp.dot(mid[r], table[r], preferred_element_type=jnp.float32)


def invert_group(product, table, r, width, wide):
    if r in (0, GROUPS - 1):
        wide[r, :, :width] = jnp.dot(product, table[r, :, :width], preferred_element_type=jnp.float32)
    else:
        wide[r] = jnp.dot(product, table[r], preferred_element_type=jnp.float32)


def merge_rows(wide, store, rows, width):
    def body(at):
        parts = []
        for r in range(GROUPS):
            im = None if r in (0, GROUPS - 1) else wide[r, at, width:]
            parts.append((wide[r, at, :width], im))
        for p, value in enumerate(last_stage(parts)):
            store(p, at, value)

    rows_loop(rows, body)


def piece_at(ref, where, k, rows):
    start = pl.multiple_of(lax.bitwise_xor(where[0], k) * rows, rows)
    return ref.at[pl.ds(start, rows), :]


def gate_kernel(order, where, gate, upper, *refs):
    outs, (left, right, sems) = refs[: len(order)], refs[len(order) :]
    rows = outs[0].shape[0]
    loads = []
    for i, k in enumerate(order):
        pair = (
            pltpu.make_async_copy(piece_at(gate, where, k, rows), left.at[i], sems.at[0, i]),
            pltpu.make_async_copy(piece_at(upper, where, k, rows), right.at[i], sems.at[1, i]),
        )
        for copy in pair:
            copy.start()
        loads.append(pair)
    for i, out in enumerate(outs):
        for copy in loads[i]:
            copy.wait()
        out[...] = (left[i].astype(jnp.float32) * right[i].astype(jnp.float32)).astype(jnp.bfloat16)


def finish_kernel(order, scale, where, *refs):
    pieces, shares, (whole, total) = refs[: len(order)], refs[len(order) : -2], refs[-2:]
    added = shares[0][...].astype(jnp.float32)
    for share in shares[1:]:
        added = added + share[...].astype(jnp.float32)
    total[...] = added * scale
    for k, piece in zip(order, pieces):
        whole[lax.bitwise_xor(where[0], k)] = piece[...]


def taps_kernel(order, where, whole, taps, forward, *refs):
    picks, (taps_spec, mid, sems) = refs[: len(order)], refs[len(order) :]
    rows, width = (taps.shape[0], taps.shape[1] // BLOCKS)
    moves = []
    for i, k in enumerate(order):
        moves.append(pltpu.make_async_copy(piece_at(whole, where, k, rows), picks[i], sems.at[i]))
        moves[-1].start()
    split_rows(lambda p, at: taps[at, p * width : (p + 1) * width], mid, rows, width)
    for r in range(GROUPS):
        taps_spec[r] = spectrum(mid, forward, r, width).astype(taps_spec.dtype)
    for copy in moves:
        copy.wait()


def ordered(order, where, refs, held):
    span = refs[0].shape[1]
    for k, ref in zip(order, refs):
        start = pl.multiple_of(lax.bitwise_xor(where[0], k) * span, span)
        held[:, pl.ds(start, span)] = ref[...]


def block_of(held, width):
    return lambda p, at: held[at, p * width : (p + 1) * width].astype(jnp.float32)


def block_into(held, width):
    def store(p, at, value):
        held[at, p * width : (p + 1) * width] = value.astype(jnp.bfloat16)

    return store


def back_kernel(order, back_order, late, where, *refs):
    blocks, refs = refs[: len(order)], refs[len(order) + late :]
    taps_spec, forward, backward, *outs, grad_spec, held, mid, wide = refs
    outs = outs[late:]
    rows, width = held.shape[0], held.shape[1] // BLOCKS
    ordered(order, where, blocks, held)
    split_rows(block_of(held, width), mid, rows, width)
    for r in range(GROUPS):
        grad = spectrum(mid, forward, r, width)
        grad_spec[r] = grad.astype(grad_spec.dtype)
        taps = taps_spec[r].astype(jnp.float32)
        gr, gi, hr, hi = grad[:, :width], grad[:, width:], taps[:, :width], taps[:, width:]
        product = jnp.concatenate([hr * gr + hi * gi, hr * gi - hi * gr], axis=1)
        invert_group(product.astype(jnp.bfloat16), backward, r, width, wide)
    merge_rows(wide, block_into(held, width), rows, width)
    span = outs[0].shape[1]
    for k, out in zip(back_order, outs):
        start = pl.multiple_of(lax.bitwise_xor(where[0], k) * span, span)
        out[...] = held[:, pl.ds(start, span)]


def cross_kernel(order, where, *refs):
    blocks, refs = refs[: len(order)], refs[len(order) :]
    grad_spec, forward, backward, *outs, held, mid, wide = refs
    rows, width = held.shape[0], held.shape[1] // BLOCKS
    ordered(order, where, blocks, held)
    split_rows(block_of(held, width), mid, rows, width)
    for r in range(GROUPS):
        signal = spectrum(mid, forward, r, width)
        grad = grad_spec[r].astype(jnp.float32)
        gr, gi, xr, xi = grad[:, :width], grad[:, width:], signal[:, :width], signal[:, width:]
        product = jnp.concatenate([gr * xr + gi * xi, gi * xr - gr * xi], axis=1)
        invert_group(product.astype(jnp.bfloat16), backward, r, width, wide)
    merge_rows(wide, block_into(held, width), rows, width)
    part = held.shape[1] // len(outs)
    for k, out in zip(far_first(len(outs)), outs):
        start = pl.multiple_of(lax.bitwise_xor(where[1], k) * part, part)
        out[...] = held[:, pl.ds(start, part)]


def call(kernel, operands, outs, scratch=(), flops=0, streams=(), out_streams=(), aliases=None, hbm=()):
    def spec(stream):
        return pl.BlockSpec(memory_space=pl.ANY if stream else pltpu.VMEM)

    size = sum(math.prod(o.shape) * o.dtype.itemsize for o in list(operands) + list(outs))
    specs = [spec(i in streams) for i in range(len(operands))]
    for i in hbm:
        specs[i] = pl.BlockSpec(memory_space=pltpu.HBM)
    if operands[0].dtype == jnp.int32:
        specs[0] = pl.BlockSpec(memory_space=pltpu.SMEM)
    outputs = pl.pallas_call(
        kernel,
        out_shape=list(outs),
        in_specs=specs,
        out_specs=[spec(i in out_streams) for i in range(len(outs))],
        scratch_shapes=list(scratch),
        input_output_aliases=aliases or {},
        compiler_params=pltpu.CompilerParams(vmem_limit_bytes=LIMIT),
        cost_estimate=pl.CostEstimate(flops=flops, bytes_accessed=size, transcendentals=0),
    )(*operands)
    return list(outputs)


def far_first(size):
    return [*range(size // 2, size), *range(1, size // 2), 0]


def spread(size, order):
    part = size // 8
    return [k * part + i for k in order for i in range(part)] + [*range(1, part), 0]


def exchange(pieces, order, axis, size):
    moved = []
    for k, piece in zip(order, pieces):
        moved.append(lax.ppermute(piece, axis, [(i, i ^ k) for i in range(size)]) if k else piece)
    return moved


def on_device(saved_input, out_gate, grad_out, long_filter):
    count, shares = lax.axis_size("ctx"), lax.axis_size("dp")
    channels, span = saved_input.shape[1:]
    rows, length = long_filter.shape
    width = length // BLOCKS
    grad_order, input_order, back_order = (spread(count, o) for o in ((1, 2, 4, 5, 6, 7, 3), (1, 4, 5, 6, 7, 2, 3), (1, 4, 2, 5, 6, 7, 3)))
    late = 3
    at = count - 1 - late
    every = range(count + 8)
    where = jnp.stack([lax.axis_index("ctx"), lax.axis_index("dp")]).astype(jnp.int32)
    forward, backward = (jnp.asarray(t) for t in transform_tables(width))
    half, full = jnp.bfloat16, jnp.float32
    piece = jax.ShapeDtypeStruct((rows, span), half)
    spec = jax.ShapeDtypeStruct((GROUPS, rows, 2 * width), half)
    held = pltpu.VMEM((rows, length), half)
    mid = pltpu.VMEM((GROUPS, rows, 2 * width), half)
    wide = pltpu.VMEM((GROUPS, rows, 2 * width), full)
    slots = pltpu.VMEM((count, rows, span), half)
    sems = pltpu.SemaphoreType.DMA
    work = 2 * GROUPS * rows * 4 * width * width

    stay = [pltpu.with_memory_space_constraint(x[0], pltpu.HBM) for x in (out_gate, grad_out, saved_input)]
    grad_pieces = call(
        functools.partial(gate_kernel, grad_order),
        [where, *stay[:2]],
        [piece] * count,
        [slots, slots, sems((2, count))],
        hbm=(1, 2),
    )
    grad_blocks = exchange(grad_pieces, grad_order, "ctx", count)
    *input_pieces, taps_spec = call(
        functools.partial(taps_kernel, input_order),
        [where, stay[2], long_filter, forward],
        [piece] * count + [spec],
        [mid, sems((count,))],
        flops=work,
        hbm=(1,),
    )
    passed = [*input_pieces[at : at + late]]
    *back, grad_spec = call(
        functools.partial(back_kernel, grad_order, back_order, late),
        [where, *grad_blocks, *passed, taps_spec, forward, backward],
        [piece] * (late + count) + [spec],
        [held, mid, wide],
        flops=2 * work,
        streams=range(1 + count, 1 + count + late),
        out_streams=range(late),
        aliases={1 + count + i: i for i in range(late)},
    )
    input_pieces[at : at + late], back = back[:late], back[late:]
    input_blocks = exchange(input_pieces, input_order, "ctx", count)
    back_blocks = exchange(back, back_order, "ctx", count)
    share = jax.ShapeDtypeStruct((rows, length // shares), half)
    cross = call(
        functools.partial(cross_kernel, input_order),
        [where, *input_blocks, grad_spec, forward, backward],
        [share] * shares,
        [held, mid, wide],
        flops=2 * work,
    )
    cross_blocks = exchange(cross, far_first(shares), "dp", shares)
    scale = 1.0 / math.sqrt(shares * length)
    whole, grad_filter = call(
        functools.partial(finish_kernel, back_order, scale),
        [where, *back_blocks, *cross_blocks],
        [jax.ShapeDtypeStruct((count, rows, span), half), jax.ShapeDtypeStruct((rows, length // shares), full)],
    )
    return (whole.reshape(1, channels, span), grad_filter)


def solution(mesh):
    in_specs = (P("dp", None, "ctx"), P("dp", None, "ctx"), P("dp", None, "ctx"), P("ctx", None))
    out_specs = (P("dp", None, "ctx"), P("ctx", "dp"))
    return jax.shard_map(
        on_device, mesh=mesh, in_specs=in_specs, out_specs=out_specs, check_vma=False
    )
```

```python
import functools
import math

import jax
import jax.numpy as jnp
import ml_dtypes
import numpy as np
from jax import lax
from jax.experimental import pallas as pl
from jax.experimental.pallas import tpu as pltpu
from jax.sharding import PartitionSpec as P

BLOCKS = 8
GROUPS = 9
TILE = 16
C1 = math.cos(math.pi / 8)
C2 = math.cos(math.pi / 4)
C3 = math.cos(3 * math.pi / 8)
LIMIT = 32 * 1024 * 1024


def transform_tables(width):
    points = 2 * BLOCKS * width
    row = np.arange(width)
    forward = np.zeros((GROUPS, 2 * width, 2 * width), np.float64)
    for r in range(GROUPS):
        angle = 2.0 * np.pi * (np.outer(row, 16 * row + r) % points) / points
        cos, sin = np.cos(angle), np.sin(angle)
        forward[r] = np.block([[cos, -sin], [sin, cos]])
    scale = np.full((GROUPS, 1, 1), 2.0 / points)
    scale[0] = scale[-1] = 1.0 / points
    backward = np.swapaxes(forward, 1, 2) * scale
    return forward.astype(ml_dtypes.bfloat16), backward.astype(ml_dtypes.bfloat16)


def first_stage(b):
    e = [b[p] + b[p + 4] for p in range(4)]
    f = [b[p] - b[p + 4] for p in range(4)]
    e02, e13 = e[0] + e[2], e[1] + e[3]
    fd, fs = C2 * (f[1] - f[3]), C2 * (f[1] + f[3])
    d = [None] + [b[p] - b[8 - p] for p in (1, 2, 3)]
    g = [None] + [b[p] + b[8 - p] for p in (1, 2, 3)]
    d2, g2 = C2 * d[2], C2 * g[2]
    re1, re3 = C1 * d[1] + C3 * d[3], C3 * d[1] - C1 * d[3]
    im1, im3 = C3 * g[1] + C1 * g[3], C1 * g[1] - C3 * g[3]
    up, down = b[0] + d2, b[0] - d2
    bp, bm = b[4] + g2, b[4] - g2
    return [
        (e02 + e13, None),
        (up + re1, -(bp + im1)),
        (f[0] + fd, -(f[2] + fs)),
        (down + re3, bm - im3),
        (e[0] - e[2], e[3] - e[1]),
        (down - re3, -(bm + im3)),
        (f[0] - fd, f[2] - fs),
        (up - re1, bp - im1),
        (e02 - e13, None),
    ]


def last_stage(u):
    re = [pair[0] for pair in u]
    im = [pair[1] for pair in u]
    sum08, dif08 = re[0] + re[8], re[0] - re[8]
    r26, i26 = re[2] + re[6], im[2] - im[6]
    rd, sd = C2 * (re[2] - re[6]), C2 * (im[2] + im[6])
    top, low = sum08 + re[4], sum08 - re[4]
    dp, dm = dif08 + rd, dif08 - rd
    ip, im4 = sd + im[4], sd - im[4]
    even = [
        top + r26,
        dp - ip,
        low - i26,
        dm - im4,
        top - r26,
        dm + im4,
        low + i26,
        dp + ip,
    ]
    a1p, a1m = re[1] + re[7], re[1] - re[7]
    a3p, a3m = re[3] + re[5], re[3] - re[5]
    j1p, j1m = im[1] + im[7], im[1] - im[7]
    j3p, j3m = im[3] + im[5], im[3] - im[5]
    c1, c3 = C1 * a1m + C3 * a3m, C3 * a1m - C1 * a3m
    c2 = C2 * (a1p - a3p)
    s1, s3 = C3 * j1p + C1 * j3p, C1 * j1p - C3 * j3p
    s2 = C2 * (j1m + j3m)
    odd = [
        a1p + a3p,
        c1 - s1,
        c2 - s2,
        c3 - s3,
        j3m - j1m,
        -(c3 + s3),
        -(c2 + s2),
        -(c1 + s1),
    ]
    return [x + y for x, y in zip(even, odd)]


def rows_loop(rows, body):
    @pl.loop(0, rows // TILE)
    def _(step):
        body(pl.ds(pl.multiple_of(step * TILE, TILE), TILE))


def split_rows(load, mid, rows, width):
    def body(at):
        for r, pair in enumerate(first_stage([load(p, at) for p in range(BLOCKS)])):
            mid[r, at, :width] = pair[0].astype(jnp.bfloat16)
            if pair[1] is not None:
                mid[r, at, width:] = pair[1].astype(jnp.bfloat16)

    rows_loop(rows, body)


def spectrum(mid, table, r, width):
    if r in (0, GROUPS - 1):
        return jnp.dot(mid[r, :, :width], table[r, :width, :], preferred_element_type=jnp.float32)
    return jnp.dot(mid[r], table[r], preferred_element_type=jnp.float32)


def invert_group(product, table, r, width, wide):
    if r in (0, GROUPS - 1):
        wide[r, :, :width] = jnp.dot(product, table[r, :, :width], preferred_element_type=jnp.float32)
    else:
        wide[r] = jnp.dot(product, table[r], preferred_element_type=jnp.float32)


def merge_rows(wide, store, rows, width):
    def body(at):
        parts = []
        for r in range(GROUPS):
            im = None if r in (0, GROUPS - 1) else wide[r, at, width:]
            parts.append((wide[r, at, :width], im))
        for p, value in enumerate(last_stage(parts)):
            store(p, at, value)

    rows_loop(rows, body)


def piece_at(ref, where, k, rows):
    start = pl.multiple_of(lax.bitwise_xor(where[0], k) * rows, rows)
    return ref.at[pl.ds(start, rows), :]


def gate_kernel(order, where, gate, upper, *refs):
    outs, (left, right, sems) = refs[: len(order)], refs[len(order) :]
    rows = outs[0].shape[0]
    loads = []
    for i, k in enumerate(order):
        pair = (
            pltpu.make_async_copy(piece_at(gate, where, k, rows), left.at[i], sems.at[0, i]),
            pltpu.make_async_copy(piece_at(upper, where, k, rows), right.at[i], sems.at[1, i]),
        )
        for copy in pair:
            copy.start()
        loads.append(pair)
    for i, out in enumerate(outs):
        for copy in loads[i]:
            copy.wait()
        out[...] = (left[i].astype(jnp.float32) * right[i].astype(jnp.float32)).astype(jnp.bfloat16)


def finish_kernel(order, scale, where, *refs):
    pieces, shares, (whole, total) = refs[: len(order)], refs[len(order) : -2], refs[-2:]
    added = shares[0][...].astype(jnp.float32)
    for share in shares[1:]:
        added = added + share[...].astype(jnp.float32)
    total[...] = added * scale
    for k, piece in zip(order, pieces):
        whole[lax.bitwise_xor(where[0], k)] = piece[...]


def taps_kernel(order, where, whole, taps, forward, *refs):
    picks, (taps_spec, mid, sems) = refs[: len(order)], refs[len(order) :]
    rows, width = (taps.shape[0], taps.shape[1] // BLOCKS)
    moves = []
    for i, k in enumerate(order):
        moves.append(pltpu.make_async_copy(piece_at(whole, where, k, rows), picks[i], sems.at[i]))
        moves[-1].start()
    split_rows(lambda p, at: taps[at, p * width : (p + 1) * width], mid, rows, width)
    for r in range(GROUPS):
        taps_spec[r] = spectrum(mid, forward, r, width).astype(taps_spec.dtype)
    for copy in moves:
        copy.wait()


def ordered(order, where, refs, held):
    span = refs[0].shape[1]
    for k, ref in zip(order, refs):
        start = pl.multiple_of(lax.bitwise_xor(where[0], k) * span, span)
        held[:, pl.ds(start, span)] = ref[...]


def block_of(held, width):
    return lambda p, at: held[at, p * width : (p + 1) * width].astype(jnp.float32)


def block_into(held, width):
    def store(p, at, value):
        held[at, p * width : (p + 1) * width] = value.astype(jnp.bfloat16)

    return store


def back_kernel(order, back_order, late, where, *refs):
    blocks, refs = refs[: len(order)], refs[len(order) + late :]
    taps_spec, forward, backward, *outs, grad_spec, held, mid, wide = refs
    outs = outs[late:]
    rows, width = held.shape[0], held.shape[1] // BLOCKS
    ordered(order, where, blocks, held)
    split_rows(block_of(held, width), mid, rows, width)
    for r in range(GROUPS):
        grad = spectrum(mid, forward, r, width)
        grad_spec[r] = grad.astype(grad_spec.dtype)
        taps = taps_spec[r].astype(jnp.float32)
        gr, gi, hr, hi = grad[:, :width], grad[:, width:], taps[:, :width], taps[:, width:]
        product = jnp.concatenate([hr * gr + hi * gi, hr * gi - hi * gr], axis=1)
        invert_group(product.astype(jnp.bfloat16), backward, r, width, wide)
    merge_rows(wide, block_into(held, width), rows, width)
    span = outs[0].shape[1]
    for k, out in zip(back_order, outs):
        start = pl.multiple_of(lax.bitwise_xor(where[0], k) * span, span)
        out[...] = held[:, pl.ds(start, span)]


def cross_kernel(order, where, *refs):
    blocks, refs = refs[: len(order)], refs[len(order) :]
    grad_spec, forward, backward, *outs, held, mid, wide = refs
    rows, width = held.shape[0], held.shape[1] // BLOCKS
    ordered(order, where, blocks, held)
    split_rows(block_of(held, width), mid, rows, width)
    for r in range(GROUPS):
        signal = spectrum(mid, forward, r, width)
        grad = grad_spec[r].astype(jnp.float32)
        gr, gi, xr, xi = grad[:, :width], grad[:, width:], signal[:, :width], signal[:, width:]
        product = jnp.concatenate([gr * xr + gi * xi, gi * xr - gr * xi], axis=1)
        invert_group(product.astype(jnp.bfloat16), backward, r, width, wide)
    merge_rows(wide, block_into(held, width), rows, width)
    part = held.shape[1] // len(outs)
    for k, out in zip(far_first(len(outs)), outs):
        start = pl.multiple_of(lax.bitwise_xor(where[1], k) * part, part)
        out[...] = held[:, pl.ds(start, part)]


def call(kernel, operands, outs, scratch=(), flops=0, streams=(), out_streams=(), aliases=None, hbm=()):
    def spec(stream):
        return pl.BlockSpec(memory_space=pl.ANY if stream else pltpu.VMEM)

    size = sum(math.prod(o.shape) * o.dtype.itemsize for o in list(operands) + list(outs))
    specs = [spec(i in streams) for i in range(len(operands))]
    for i in hbm:
        specs[i] = pl.BlockSpec(memory_space=pltpu.HBM)
    if operands[0].dtype == jnp.int32:
        specs[0] = pl.BlockSpec(memory_space=pltpu.SMEM)
    outputs = pl.pallas_call(
        kernel,
        out_shape=list(outs),
        in_specs=specs,
        out_specs=[spec(i in out_streams) for i in range(len(outs))],
        scratch_shapes=list(scratch),
        input_output_aliases=aliases or {},
        compiler_params=pltpu.CompilerParams(vmem_limit_bytes=LIMIT),
        cost_estimate=pl.CostEstimate(flops=flops, bytes_accessed=size, transcendentals=0),
    )(*operands)
    return list(outputs)


def far_first(size):
    return [*range(size // 2, size), *range(1, size // 2), 0]


def spread(size, order):
    part = size // 8
    return [k * part + i for k in order for i in range(part)] + [*range(1, part), 0]


def exchange(pieces, order, axis, size):
    moved = []
    for k, piece in zip(order, pieces):
        moved.append(lax.ppermute(piece, axis, [(i, i ^ k) for i in range(size)]) if k else piece)
    return moved


def on_device(saved_input, out_gate, grad_out, long_filter):
    count, shares = lax.axis_size("ctx"), lax.axis_size("dp")
    channels, span = saved_input.shape[1:]
    rows, length = long_filter.shape
    width = length // BLOCKS
    grad_order, input_order, back_order = (spread(count, o) for o in ((4, 1, 5, 2, 6, 7, 3), (4, 5, 6, 1, 7, 2, 3), (1, 4, 2, 5, 6, 7, 3)))
    late = 3
    at = count - 1 - late
    every = range(count + 8)
    where = jnp.stack([lax.axis_index("ctx"), lax.axis_index("dp")]).astype(jnp.int32)
    forward, backward = (jnp.asarray(t) for t in transform_tables(width))
    half, full = jnp.bfloat16, jnp.float32
    piece = jax.ShapeDtypeStruct((rows, span), half)
    spec = jax.ShapeDtypeStruct((GROUPS, rows, 2 * width), half)
    held = pltpu.VMEM((rows, length), half)
    mid = pltpu.VMEM((GROUPS, rows, 2 * width), half)
    wide = pltpu.VMEM((GROUPS, rows, 2 * width), full)
    sems = pltpu.SemaphoreType.DMA
    work = 2 * GROUPS * rows * 4 * width * width

    stay = [pltpu.with_memory_space_constraint(x[0], pltpu.HBM) for x in (out_gate, grad_out, saved_input)]
    grad_pieces, cut = [], 1 * count // 8
    for some in (grad_order[:cut], grad_order[cut:]):
        held_some = pltpu.VMEM((len(some), rows, span), half)
        grad_pieces += call(
            functools.partial(gate_kernel, some),
            [where, *stay[:2]],
            [piece] * len(some),
            [held_some, held_some, sems((2, len(some)))],
            hbm=(1, 2),
        )
    grad_blocks = exchange(grad_pieces, grad_order, "ctx", count)
    *input_pieces, taps_spec = call(
        functools.partial(taps_kernel, input_order),
        [where, stay[2], long_filter, forward],
        [piece] * count + [spec],
        [mid, sems((count,))],
        flops=work,
        hbm=(1,),
    )
    passed = [*input_pieces[at : at + late]]
    *back, grad_spec = call(
        functools.partial(back_kernel, grad_order, back_order, late),
        [where, *grad_blocks, *passed, taps_spec, forward, backward],
        [piece] * (late + count) + [spec],
        [held, mid, wide],
        flops=2 * work,
        streams=range(1 + count, 1 + count + late),
        out_streams=range(late),
        aliases={1 + count + i: i for i in range(late)},
    )
    input_pieces[at : at + late], back = back[:late], back[late:]
    input_blocks = exchange(input_pieces, input_order, "ctx", count)
    back_blocks = exchange(back, back_order, "ctx", count)
    share = jax.ShapeDtypeStruct((rows, length // shares), half)
    cross = call(
        functools.partial(cross_kernel, input_order),
        [where, *input_blocks, grad_spec, forward, backward],
        [share] * shares,
        [held, mid, wide],
        flops=2 * work,
    )
    cross_blocks = exchange(cross, far_first(shares), "dp", shares)
    scale = 1.0 / math.sqrt(shares * length)
    whole, grad_filter = call(
        functools.partial(finish_kernel, back_order, scale),
        [where, *back_blocks, *cross_blocks],
        [jax.ShapeDtypeStruct((count, rows, span), half), jax.ShapeDtypeStruct((rows, length // shares), full)],
    )
    return (whole.reshape(1, channels, span), grad_filter)


def solution(mesh):
    in_specs = (P("dp", None, "ctx"), P("dp", None, "ctx"), P("dp", None, "ctx"), P("ctx", None))
    out_specs = (P("dp", None, "ctx"), P("ctx", "dp"))
    return jax.shard_map(
        on_device, mesh=mesh, in_specs=in_specs, out_specs=out_specs, check_vma=False
    )
```

```python
import functools
import math

import jax
import jax.numpy as jnp
import ml_dtypes
import numpy as np
from jax import lax
from jax.experimental import pallas as pl
from jax.experimental.pallas import tpu as pltpu
from jax.sharding import PartitionSpec as P

BLOCKS = 8
GROUPS = 9
TILE = 16
C1 = math.cos(math.pi / 8)
C2 = math.cos(math.pi / 4)
C3 = math.cos(3 * math.pi / 8)
LIMIT = 32 * 1024 * 1024


def transform_tables(width):
    points = 2 * BLOCKS * width
    row = np.arange(width)
    forward = np.zeros((GROUPS, 2 * width, 2 * width), np.float64)
    for r in range(GROUPS):
        angle = 2.0 * np.pi * (np.outer(row, 16 * row + r) % points) / points
        cos, sin = np.cos(angle), np.sin(angle)
        forward[r] = np.block([[cos, -sin], [sin, cos]])
    scale = np.full((GROUPS, 1, 1), 2.0 / points)
    scale[0] = scale[-1] = 1.0 / points
    backward = np.swapaxes(forward, 1, 2) * scale
    return forward.astype(ml_dtypes.bfloat16), backward.astype(ml_dtypes.bfloat16)


def first_stage(b):
    e = [b[p] + b[p + 4] for p in range(4)]
    f = [b[p] - b[p + 4] for p in range(4)]
    e02, e13 = e[0] + e[2], e[1] + e[3]
    fd, fs = C2 * (f[1] - f[3]), C2 * (f[1] + f[3])
    d = [None] + [b[p] - b[8 - p] for p in (1, 2, 3)]
    g = [None] + [b[p] + b[8 - p] for p in (1, 2, 3)]
    d2, g2 = C2 * d[2], C2 * g[2]
    re1, re3 = C1 * d[1] + C3 * d[3], C3 * d[1] - C1 * d[3]
    im1, im3 = C3 * g[1] + C1 * g[3], C1 * g[1] - C3 * g[3]
    up, down = b[0] + d2, b[0] - d2
    bp, bm = b[4] + g2, b[4] - g2
    return [
        (e02 + e13, None),
        (up + re1, -(bp + im1)),
        (f[0] + fd, -(f[2] + fs)),
        (down + re3, bm - im3),
        (e[0] - e[2], e[3] - e[1]),
        (down - re3, -(bm + im3)),
        (f[0] - fd, f[2] - fs),
        (up - re1, bp - im1),
        (e02 - e13, None),
    ]


def last_stage(u):
    re = [pair[0] for pair in u]
    im = [pair[1] for pair in u]
    sum08, dif08 = re[0] + re[8], re[0] - re[8]
    r26, i26 = re[2] + re[6], im[2] - im[6]
    rd, sd = C2 * (re[2] - re[6]), C2 * (im[2] + im[6])
    top, low = sum08 + re[4], sum08 - re[4]
    dp, dm = dif08 + rd, dif08 - rd
    ip, im4 = sd + im[4], sd - im[4]
    even = [
        top + r26,
        dp - ip,
        low - i26,
        dm - im4,
        top - r26,
        dm + im4,
        low + i26,
        dp + ip,
    ]
    a1p, a1m = re[1] + re[7], re[1] - re[7]
    a3p, a3m = re[3] + re[5], re[3] - re[5]
    j1p, j1m = im[1] + im[7], im[1] - im[7]
    j3p, j3m = im[3] + im[5], im[3] - im[5]
    c1, c3 = C1 * a1m + C3 * a3m, C3 * a1m - C1 * a3m
    c2 = C2 * (a1p - a3p)
    s1, s3 = C3 * j1p + C1 * j3p, C1 * j1p - C3 * j3p
    s2 = C2 * (j1m + j3m)
    odd = [
        a1p + a3p,
        c1 - s1,
        c2 - s2,
        c3 - s3,
        j3m - j1m,
        -(c3 + s3),
        -(c2 + s2),
        -(c1 + s1),
    ]
    return [x + y for x, y in zip(even, odd)]


def rows_loop(rows, body):
    @pl.loop(0, rows // TILE)
    def _(step):
        body(pl.ds(pl.multiple_of(step * TILE, TILE), TILE))


def split_rows(load, mid, rows, width):
    def body(at):
        for r, pair in enumerate(first_stage([load(p, at) for p in range(BLOCKS)])):
            mid[r, at, :width] = pair[0].astype(jnp.bfloat16)
            if pair[1] is not None:
                mid[r, at, width:] = pair[1].astype(jnp.bfloat16)

    rows_loop(rows, body)


def spectrum(mid, table, r, width):
    if r in (0, GROUPS - 1):
        return jnp.dot(mid[r, :, :width], table[r, :width, :], preferred_element_type=jnp.float32)
    return jnp.dot(mid[r], table[r], preferred_element_type=jnp.float32)


def invert_group(product, table, r, width, wide):
    if r in (0, GROUPS - 1):
        wide[r, :, :width] = jnp.dot(product, table[r, :, :width], preferred_element_type=jnp.float32)
    else:
        wide[r] = jnp.dot(product, table[r], preferred_element_type=jnp.float32)


def merge_rows(wide, store, rows, width):
    def body(at):
        parts = []
        for r in range(GROUPS):
            im = None if r in (0, GROUPS - 1) else wide[r, at, width:]
            parts.append((wide[r, at, :width], im))
        for p, value in enumerate(last_stage(parts)):
            store(p, at, value)

    rows_loop(rows, body)


def piece_at(ref, where, k, rows):
    start = pl.multiple_of(lax.bitwise_xor(where[0], k) * rows, rows)
    return ref.at[pl.ds(start, rows), :]


def gate_kernel(order, where, gate, upper, *refs):
    outs, (left, right, sems) = refs[: len(order)], refs[len(order) :]
    rows = outs[0].shape[0]
    loads = []
    for i, k in enumerate(order):
        pair = (
            pltpu.make_async_copy(piece_at(gate, where, k, rows), left.at[i], sems.at[0, i]),
            pltpu.make_async_copy(piece_at(upper, where, k, rows), right.at[i], sems.at[1, i]),
        )
        for copy in pair:
            copy.start()
        loads.append(pair)
    for i, out in enumerate(outs):
        for copy in loads[i]:
            copy.wait()
        out[...] = (left[i].astype(jnp.float32) * right[i].astype(jnp.float32)).astype(jnp.bfloat16)


def finish_kernel(order, scale, where, *refs):
    pieces, shares, (whole, total) = refs[: len(order)], refs[len(order) : -2], refs[-2:]
    added = shares[0][...].astype(jnp.float32)
    for share in shares[1:]:
        added = added + share[...].astype(jnp.float32)
    total[...] = added * scale
    for k, piece in zip(order, pieces):
        whole[lax.bitwise_xor(where[0], k)] = piece[...]


def taps_kernel(order, where, whole, taps, forward, *refs):
    picks, (taps_spec, mid, sems) = refs[: len(order)], refs[len(order) :]
    rows, width = (taps.shape[0], taps.shape[1] // BLOCKS)
    moves = []
    for i, k in enumerate(order):
        moves.append(pltpu.make_async_copy(piece_at(whole, where, k, rows), picks[i], sems.at[i]))
        moves[-1].start()
    split_rows(lambda p, at: taps[at, p * width : (p + 1) * width], mid, rows, width)
    for r in range(GROUPS):
        taps_spec[r] = spectrum(mid, forward, r, width).astype(taps_spec.dtype)
    for copy in moves:
        copy.wait()


def ordered(order, where, refs, held):
    span = refs[0].shape[1]
    for k, ref in zip(order, refs):
        start = pl.multiple_of(lax.bitwise_xor(where[0], k) * span, span)
        held[:, pl.ds(start, span)] = ref[...]


def block_of(held, width):
    return lambda p, at: held[at, p * width : (p + 1) * width].astype(jnp.float32)


def block_into(held, width):
    def store(p, at, value):
        held[at, p * width : (p + 1) * width] = value.astype(jnp.bfloat16)

    return store


def back_kernel(order, back_order, late, where, *refs):
    blocks, refs = refs[: len(order)], refs[len(order) + late :]
    taps_spec, forward, backward, *outs, grad_spec, held, mid, wide = refs
    outs = outs[late:]
    rows, width = held.shape[0], held.shape[1] // BLOCKS
    ordered(order, where, blocks, held)
    split_rows(block_of(held, width), mid, rows, width)
    for r in range(GROUPS):
        grad = spectrum(mid, forward, r, width)
        grad_spec[r] = grad.astype(grad_spec.dtype)
        taps = taps_spec[r].astype(jnp.float32)
        gr, gi, hr, hi = grad[:, :width], grad[:, width:], taps[:, :width], taps[:, width:]
        product = jnp.concatenate([hr * gr + hi * gi, hr * gi - hi * gr], axis=1)
        invert_group(product.astype(jnp.bfloat16), backward, r, width, wide)
    merge_rows(wide, block_into(held, width), rows, width)
    span = outs[0].shape[1]
    for k, out in zip(back_order, outs):
        start = pl.multiple_of(lax.bitwise_xor(where[0], k) * span, span)
        out[...] = held[:, pl.ds(start, span)]


def cross_kernel(order, where, *refs):
    blocks, refs = refs[: len(order)], refs[len(order) :]
    grad_spec, forward, backward, *outs, held, mid, wide = refs
    rows, width = held.shape[0], held.shape[1] // BLOCKS
    ordered(order, where, blocks, held)
    split_rows(block_of(held, width), mid, rows, width)
    for r in range(GROUPS):
        signal = spectrum(mid, forward, r, width)
        grad = grad_spec[r].astype(jnp.float32)
        gr, gi, xr, xi = grad[:, :width], grad[:, width:], signal[:, :width], signal[:, width:]
        product = jnp.concatenate([gr * xr + gi * xi, gi * xr - gr * xi], axis=1)
        invert_group(product.astype(jnp.bfloat16), backward, r, width, wide)
    merge_rows(wide, block_into(held, width), rows, width)
    part = held.shape[1] // len(outs)
    for k, out in zip(far_first(len(outs)), outs):
        start = pl.multiple_of(lax.bitwise_xor(where[1], k) * part, part)
        out[...] = held[:, pl.ds(start, part)]


def call(kernel, operands, outs, scratch=(), flops=0, streams=(), out_streams=(), aliases=None, hbm=()):
    def spec(stream):
        return pl.BlockSpec(memory_space=pl.ANY if stream else pltpu.VMEM)

    size = sum(math.prod(o.shape) * o.dtype.itemsize for o in list(operands) + list(outs))
    specs = [spec(i in streams) for i in range(len(operands))]
    for i in hbm:
        specs[i] = pl.BlockSpec(memory_space=pltpu.HBM)
    if operands[0].dtype == jnp.int32:
        specs[0] = pl.BlockSpec(memory_space=pltpu.SMEM)
    outputs = pl.pallas_call(
        kernel,
        out_shape=list(outs),
        in_specs=specs,
        out_specs=[spec(i in out_streams) for i in range(len(outs))],
        scratch_shapes=list(scratch),
        input_output_aliases=aliases or {},
        compiler_params=pltpu.CompilerParams(vmem_limit_bytes=LIMIT),
        cost_estimate=pl.CostEstimate(flops=flops, bytes_accessed=size, transcendentals=0),
    )(*operands)
    return list(outputs)


def far_first(size):
    return [*range(size // 2, size), *range(1, size // 2), 0]


def spread(size, order):
    part = size // 8
    return [k * part + i for k in order for i in range(part)] + [*range(1, part), 0]


def exchange(pieces, order, axis, size):
    moved = []
    for k, piece in zip(order, pieces):
        moved.append(lax.ppermute(piece, axis, [(i, i ^ k) for i in range(size)]) if k else piece)
    return moved


def on_device(saved_input, out_gate, grad_out, long_filter):
    count, shares = lax.axis_size("ctx"), lax.axis_size("dp")
    channels, span = saved_input.shape[1:]
    rows, length = long_filter.shape
    width = length // BLOCKS
    grad_order, input_order, back_order = (spread(count, o) for o in ((4, 1, 5, 2, 6, 7, 3), (1, 4, 5, 6, 7, 2, 3), (1, 4, 2, 5, 6, 7, 3)))
    late = 3
    at = count - 1 - late
    every = range(count + 8)
    where = jnp.stack([lax.axis_index("ctx"), lax.axis_index("dp")]).astype(jnp.int32)
    forward, backward = (jnp.asarray(t) for t in transform_tables(width))
    half, full = jnp.bfloat16, jnp.float32
    piece = jax.ShapeDtypeStruct((rows, span), half)
    spec = jax.ShapeDtypeStruct((GROUPS, rows, 2 * width), half)
    held = pltpu.VMEM((rows, length), half)
    mid = pltpu.VMEM((GROUPS, rows, 2 * width), half)
    wide = pltpu.VMEM((GROUPS, rows, 2 * width), full)
    slots = pltpu.VMEM((count, rows, span), half)
    sems = pltpu.SemaphoreType.DMA
    work = 2 * GROUPS * rows * 4 * width * width

    stay = [pltpu.with_memory_space_constraint(x[0], pltpu.HBM) for x in (out_gate, grad_out, saved_input)]
    grad_pieces = call(
        functools.partial(gate_kernel, grad_order),
        [where, *stay[:2]],
        [piece] * count,
        [slots, slots, sems((2, count))],
        hbm=(1, 2),
    )
    grad_blocks = exchange(grad_pieces, grad_order, "ctx", count)
    *input_pieces, taps_spec = call(
        functools.partial(taps_kernel, input_order),
        [where, stay[2], long_filter, forward],
        [piece] * count + [spec],
        [mid, sems((count,))],
        flops=work,
        hbm=(1,),
    )
    passed = [*input_pieces[at : at + late]]
    *back, grad_spec = call(
        functools.partial(back_kernel, grad_order, back_order, late),
        [where, *grad_blocks, *passed, taps_spec, forward, backward],
        [piece] * (late + count) + [spec],
        [held, mid, wide],
        flops=2 * work,
        streams=range(1 + count, 1 + count + late),
        out_streams=range(late),
        aliases={1 + count + i: i for i in range(late)},
    )
    input_pieces[at : at + late], back = back[:late], back[late:]
    input_blocks = exchange(input_pieces, input_order, "ctx", count)
    back_blocks = exchange(back, back_order, "ctx", count)
    share = jax.ShapeDtypeStruct((rows, length // shares), half)
    cross = call(
        functools.partial(cross_kernel, input_order),
        [where, *input_blocks, grad_spec, forward, backward],
        [share] * shares,
        [held, mid, wide],
        flops=2 * work,
    )
    cross_blocks = exchange(cross, far_first(shares), "dp", shares)
    scale = 1.0 / math.sqrt(shares * length)
    whole, grad_filter = call(
        functools.partial(finish_kernel, back_order, scale),
        [where, *back_blocks, *cross_blocks],
        [jax.ShapeDtypeStruct((count, rows, span), half), jax.ShapeDtypeStruct((rows, length // shares), full)],
    )
    return (whole.reshape(1, channels, span), grad_filter)


def solution(mesh):
    in_specs = (P("dp", None, "ctx"), P("dp", None, "ctx"), P("dp", None, "ctx"), P("ctx", None))
    out_specs = (P("dp", None, "ctx"), P("ctx", "dp"))
    return jax.shard_map(
        on_device, mesh=mesh, in_specs=in_specs, out_specs=out_specs, check_vma=False
    )
```

```python
import functools
import math

import jax
import jax.numpy as jnp
import ml_dtypes
import numpy as np
from jax import lax
from jax.experimental import pallas as pl
from jax.experimental.pallas import tpu as pltpu
from jax.sharding import PartitionSpec as P

BLOCKS = 8
GROUPS = 9
TILE = 16
C1 = math.cos(math.pi / 8)
C2 = math.cos(math.pi / 4)
C3 = math.cos(3 * math.pi / 8)
LIMIT = 32 * 1024 * 1024


def transform_tables(width):
    points = 2 * BLOCKS * width
    row = np.arange(width)
    forward = np.zeros((GROUPS, 2 * width, 2 * width), np.float64)
    for r in range(GROUPS):
        angle = 2.0 * np.pi * (np.outer(row, 16 * row + r) % points) / points
        cos, sin = np.cos(angle), np.sin(angle)
        forward[r] = np.block([[cos, -sin], [sin, cos]])
    scale = np.full((GROUPS, 1, 1), 2.0 / points)
    scale[0] = scale[-1] = 1.0 / points
    backward = np.swapaxes(forward, 1, 2) * scale
    return forward.astype(ml_dtypes.bfloat16), backward.astype(ml_dtypes.bfloat16)


def first_stage(b):
    e = [b[p] + b[p + 4] for p in range(4)]
    f = [b[p] - b[p + 4] for p in range(4)]
    e02, e13 = e[0] + e[2], e[1] + e[3]
    fd, fs = C2 * (f[1] - f[3]), C2 * (f[1] + f[3])
    d = [None] + [b[p] - b[8 - p] for p in (1, 2, 3)]
    g = [None] + [b[p] + b[8 - p] for p in (1, 2, 3)]
    d2, g2 = C2 * d[2], C2 * g[2]
    re1, re3 = C1 * d[1] + C3 * d[3], C3 * d[1] - C1 * d[3]
    im1, im3 = C3 * g[1] + C1 * g[3], C1 * g[1] - C3 * g[3]
    up, down = b[0] + d2, b[0] - d2
    bp, bm = b[4] + g2, b[4] - g2
    return [
        (e02 + e13, None),
        (up + re1, -(bp + im1)),
        (f[0] + fd, -(f[2] + fs)),
        (down + re3, bm - im3),
        (e[0] - e[2], e[3] - e[1]),
        (down - re3, -(bm + im3)),
        (f[0] - fd, f[2] - fs),
        (up - re1, bp - im1),
        (e02 - e13, None),
    ]


def last_stage(u):
    re = [pair[0] for pair in u]
    im = [pair[1] for pair in u]
    sum08, dif08 = re[0] + re[8], re[0] - re[8]
    r26, i26 = re[2] + re[6], im[2] - im[6]
    rd, sd = C2 * (re[2] - re[6]), C2 * (im[2] + im[6])
    top, low = sum08 + re[4], sum08 - re[4]
    dp, dm = dif08 + rd, dif08 - rd
    ip, im4 = sd + im[4], sd - im[4]
    even = [
        top + r26,
        dp - ip,
        low - i26,
        dm - im4,
        top - r26,
        dm + im4,
        low + i26,
        dp + ip,
    ]
    a1p, a1m = re[1] + re[7], re[1] - re[7]
    a3p, a3m = re[3] + re[5], re[3] - re[5]
    j1p, j1m = im[1] + im[7], im[1] - im[7]
    j3p, j3m = im[3] + im[5], im[3] - im[5]
    c1, c3 = C1 * a1m + C3 * a3m, C3 * a1m - C1 * a3m
    c2 = C2 * (a1p - a3p)
    s1, s3 = C3 * j1p + C1 * j3p, C1 * j1p - C3 * j3p
    s2 = C2 * (j1m + j3m)
    odd = [
        a1p + a3p,
        c1 - s1,
        c2 - s2,
        c3 - s3,
        j3m - j1m,
        -(c3 + s3),
        -(c2 + s2),
        -(c1 + s1),
    ]
    return [x + y for x, y in zip(even, odd)]


def rows_loop(rows, body):
    @pl.loop(0, rows // TILE)
    def _(step):
        body(pl.ds(pl.multiple_of(step * TILE, TILE), TILE))


def split_rows(load, mid, rows, width):
    def body(at):
        for r, pair in enumerate(first_stage([load(p, at) for p in range(BLOCKS)])):
            mid[r, at, :width] = pair[0].astype(jnp.bfloat16)
            if pair[1] is not None:
                mid[r, at, width:] = pair[1].astype(jnp.bfloat16)

    rows_loop(rows, body)


def spectrum(mid, table, r, width):
    if r in (0, GROUPS - 1):
        return jnp.dot(mid[r, :, :width], table[r, :width, :], preferred_element_type=jnp.float32)
    return jnp.dot(mid[r], table[r], preferred_element_type=jnp.float32)


def invert_group(product, table, r, width, wide):
    if r in (0, GROUPS - 1):
        wide[r, :, :width] = jnp.dot(product, table[r, :, :width], preferred_element_type=jnp.float32)
    else:
        wide[r] = jnp.dot(product, table[r], preferred_element_type=jnp.float32)


def merge_rows(wide, store, rows, width):
    def body(at):
        parts = []
        for r in range(GROUPS):
            im = None if r in (0, GROUPS - 1) else wide[r, at, width:]
            parts.append((wide[r, at, :width], im))
        for p, value in enumerate(last_stage(parts)):
            store(p, at, value)

    rows_loop(rows, body)


def piece_at(ref, where, k, rows):
    start = pl.multiple_of(lax.bitwise_xor(where[0], k) * rows, rows)
    return ref.at[pl.ds(start, rows), :]


def gate_kernel(order, where, gate, upper, *refs):
    outs, (left, right, sems) = refs[: len(order)], refs[len(order) :]
    rows = outs[0].shape[0]
    loads = []
    for i, k in enumerate(order):
        pair = (
            pltpu.make_async_copy(piece_at(gate, where, k, rows), left.at[i], sems.at[0, i]),
            pltpu.make_async_copy(piece_at(upper, where, k, rows), right.at[i], sems.at[1, i]),
        )
        for copy in pair:
            copy.start()
        loads.append(pair)
    for i, out in enumerate(outs):
        for copy in loads[i]:
            copy.wait()
        out[...] = (left[i].astype(jnp.float32) * right[i].astype(jnp.float32)).astype(jnp.bfloat16)


def finish_kernel(order, scale, where, *refs):
    pieces, shares, (whole, total) = refs[: len(order)], refs[len(order) : -2], refs[-2:]
    added = shares[0][...].astype(jnp.float32)
    for share in shares[1:]:
        added = added + share[...].astype(jnp.float32)
    total[...] = added * scale
    for k, piece in zip(order, pieces):
        whole[lax.bitwise_xor(where[0], k)] = piece[...]


def taps_kernel(order, where, whole, taps, forward, *refs):
    picks, (taps_spec, mid, sems) = refs[: len(order)], refs[len(order) :]
    rows, width = (taps.shape[0], taps.shape[1] // BLOCKS)
    moves = []
    for i, k in enumerate(order):
        moves.append(pltpu.make_async_copy(piece_at(whole, where, k, rows), picks[i], sems.at[i]))
        moves[-1].start()
    split_rows(lambda p, at: taps[at, p * width : (p + 1) * width], mid, rows, width)
    for r in range(GROUPS):
        taps_spec[r] = spectrum(mid, forward, r, width).astype(taps_spec.dtype)
    for copy in moves:
        copy.wait()


def ordered(order, where, refs, held):
    span = refs[0].shape[1]
    for k, ref in zip(order, refs):
        start = pl.multiple_of(lax.bitwise_xor(where[0], k) * span, span)
        held[:, pl.ds(start, span)] = ref[...]


def block_of(held, width):
    return lambda p, at: held[at, p * width : (p + 1) * width].astype(jnp.float32)


def block_into(held, width):
    def store(p, at, value):
        held[at, p * width : (p + 1) * width] = value.astype(jnp.bfloat16)

    return store


def back_kernel(order, back_order, late, where, *refs):
    blocks, refs = refs[: len(order)], refs[len(order) + late :]
    taps_spec, forward, backward, *outs, grad_spec, held, mid, wide = refs
    outs = outs[late:]
    rows, width = held.shape[0], held.shape[1] // BLOCKS
    ordered(order, where, blocks, held)
    split_rows(block_of(held, width), mid, rows, width)
    for r in range(GROUPS):
        grad = spectrum(mid, forward, r, width)
        grad_spec[r] = grad.astype(grad_spec.dtype)
        taps = taps_spec[r].astype(jnp.float32)
        gr, gi, hr, hi = grad[:, :width], grad[:, width:], taps[:, :width], taps[:, width:]
        product = jnp.concatenate([hr * gr + hi * gi, hr * gi - hi * gr], axis=1)
        invert_group(product.astype(jnp.bfloat16), backward, r, width, wide)
    merge_rows(wide, block_into(held, width), rows, width)
    span = outs[0].shape[1]
    for k, out in zip(back_order, outs):
        start = pl.multiple_of(lax.bitwise_xor(where[0], k) * span, span)
        out[...] = held[:, pl.ds(start, span)]


def cross_kernel(order, where, *refs):
    blocks, refs = refs[: len(order)], refs[len(order) :]
    grad_spec, forward, backward, *outs, held, mid, wide = refs
    rows, width = held.shape[0], held.shape[1] // BLOCKS
    ordered(order, where, blocks, held)
    split_rows(block_of(held, width), mid, rows, width)
    for r in range(GROUPS):
        signal = spectrum(mid, forward, r, width)
        grad = grad_spec[r].astype(jnp.float32)
        gr, gi, xr, xi = grad[:, :width], grad[:, width:], signal[:, :width], signal[:, width:]
        product = jnp.concatenate([gr * xr + gi * xi, gi * xr - gr * xi], axis=1)
        invert_group(product.astype(jnp.bfloat16), backward, r, width, wide)
    merge_rows(wide, block_into(held, width), rows, width)
    part = held.shape[1] // len(outs)
    for k, out in zip(far_first(len(outs)), outs):
        start = pl.multiple_of(lax.bitwise_xor(where[1], k) * part, part)
        out[...] = held[:, pl.ds(start, part)]


def call(kernel, operands, outs, scratch=(), flops=0, streams=(), out_streams=(), aliases=None, hbm=()):
    def spec(stream):
        return pl.BlockSpec(memory_space=pl.ANY if stream else pltpu.VMEM)

    size = sum(math.prod(o.shape) * o.dtype.itemsize for o in list(operands) + list(outs))
    specs = [spec(i in streams) for i in range(len(operands))]
    for i in hbm:
        specs[i] = pl.BlockSpec(memory_space=pltpu.HBM)
    if operands[0].dtype == jnp.int32:
        specs[0] = pl.BlockSpec(memory_space=pltpu.SMEM)
    outputs = pl.pallas_call(
        kernel,
        out_shape=list(outs),
        in_specs=specs,
        out_specs=[spec(i in out_streams) for i in range(len(outs))],
        scratch_shapes=list(scratch),
        input_output_aliases=aliases or {},
        compiler_params=pltpu.CompilerParams(vmem_limit_bytes=LIMIT),
        cost_estimate=pl.CostEstimate(flops=flops, bytes_accessed=size, transcendentals=0),
    )(*operands)
    return list(outputs)


def far_first(size):
    return [*range(size // 2, size), *range(1, size // 2), 0]


def spread(size, order):
    part = size // 8
    return [k * part + i for k in order for i in range(part)] + [*range(1, part), 0]


def exchange(pieces, order, axis, size):
    moved = []
    for k, piece in zip(order, pieces):
        moved.append(lax.ppermute(piece, axis, [(i, i ^ k) for i in range(size)]) if k else piece)
    return moved


def on_device(saved_input, out_gate, grad_out, long_filter):
    count, shares = lax.axis_size("ctx"), lax.axis_size("dp")
    channels, span = saved_input.shape[1:]
    rows, length = long_filter.shape
    width = length // BLOCKS
    grad_order, input_order, back_order = (spread(count, o) for o in ((4, 1, 5, 2, 6, 7, 3), (4, 5, 6, 1, 7, 2, 3), (1, 2, 4, 5, 6, 7, 3)))
    late = 3
    at = count - 1 - late
    every = range(count + 8)
    where = jnp.stack([lax.axis_index("ctx"), lax.axis_index("dp")]).astype(jnp.int32)
    forward, backward = (jnp.asarray(t) for t in transform_tables(width))
    half, full = jnp.bfloat16, jnp.float32
    piece = jax.ShapeDtypeStruct((rows, span), half)
    spec = jax.ShapeDtypeStruct((GROUPS, rows, 2 * width), half)
    held = pltpu.VMEM((rows, length), half)
    mid = pltpu.VMEM((GROUPS, rows, 2 * width), half)
    wide = pltpu.VMEM((GROUPS, rows, 2 * width), full)
    slots = pltpu.VMEM((count, rows, span), half)
    sems = pltpu.SemaphoreType.DMA
    work = 2 * GROUPS * rows * 4 * width * width

    stay = [pltpu.with_memory_space_constraint(x[0], pltpu.HBM) for x in (out_gate, grad_out, saved_input)]
    grad_pieces = call(
        functools.partial(gate_kernel, grad_order),
        [where, *stay[:2]],
        [piece] * count,
        [slots, slots, sems((2, count))],
        hbm=(1, 2),
    )
    grad_blocks = exchange(grad_pieces, grad_order, "ctx", count)
    *input_pieces, taps_spec = call(
        functools.partial(taps_kernel, input_order),
        [where, stay[2], long_filter, forward],
        [piece] * count + [spec],
        [mid, sems((count,))],
        flops=work,
        hbm=(1,),
    )
    passed = [*input_pieces[at : at + late]]
    *back, grad_spec = call(
        functools.partial(back_kernel, grad_order, back_order, late),
        [where, *grad_blocks, *passed, taps_spec, forward, backward],
        [piece] * (late + count) + [spec],
        [held, mid, wide],
        flops=2 * work,
        streams=range(1 + count, 1 + count + late),
        out_streams=range(late),
        aliases={1 + count + i: i for i in range(late)},
    )
    input_pieces[at : at + late], back = back[:late], back[late:]
    input_blocks = exchange(input_pieces, input_order, "ctx", count)
    back_blocks = exchange(back, back_order, "ctx", count)
    share = jax.ShapeDtypeStruct((rows, length // shares), half)
    cross = call(
        functools.partial(cross_kernel, input_order),
        [where, *input_blocks, grad_spec, forward, backward],
        [share] * shares,
        [held, mid, wide],
        flops=2 * work,
    )
    cross_blocks = exchange(cross, far_first(shares), "dp", shares)
    scale = 1.0 / math.sqrt(shares * length)
    whole, grad_filter = call(
        functools.partial(finish_kernel, back_order, scale),
        [where, *back_blocks, *cross_blocks],
        [jax.ShapeDtypeStruct((count, rows, span), half), jax.ShapeDtypeStruct((rows, length // shares), full)],
    )
    return (whole.reshape(1, channels, span), grad_filter)


def solution(mesh):
    in_specs = (P("dp", None, "ctx"), P("dp", None, "ctx"), P("dp", None, "ctx"), P("ctx", None))
    out_specs = (P("dp", None, "ctx"), P("ctx", "dp"))
    return jax.shard_map(
        on_device, mesh=mesh, in_specs=in_specs, out_specs=out_specs, check_vma=False
    )
```

```python
import functools
import math

import jax
import jax.numpy as jnp
import ml_dtypes
import numpy as np
from jax import lax
from jax.experimental import pallas as pl
from jax.experimental.pallas import tpu as pltpu
from jax.sharding import PartitionSpec as P

BLOCKS = 8
GROUPS = 9
TILE = 16
C1 = math.cos(math.pi / 8)
C2 = math.cos(math.pi / 4)
C3 = math.cos(3 * math.pi / 8)
LIMIT = 32 * 1024 * 1024


def transform_tables(width):
    points = 2 * BLOCKS * width
    row = np.arange(width)
    forward = np.zeros((GROUPS, 2 * width, 2 * width), np.float64)
    for r in range(GROUPS):
        angle = 2.0 * np.pi * (np.outer(row, 16 * row + r) % points) / points
        cos, sin = np.cos(angle), np.sin(angle)
        forward[r] = np.block([[cos, -sin], [sin, cos]])
    scale = np.full((GROUPS, 1, 1), 2.0 / points)
    scale[0] = scale[-1] = 1.0 / points
    backward = np.swapaxes(forward, 1, 2) * scale
    return forward.astype(ml_dtypes.bfloat16), backward.astype(ml_dtypes.bfloat16)


def first_stage(b):
    e = [b[p] + b[p + 4] for p in range(4)]
    f = [b[p] - b[p + 4] for p in range(4)]
    e02, e13 = e[0] + e[2], e[1] + e[3]
    fd, fs = C2 * (f[1] - f[3]), C2 * (f[1] + f[3])
    d = [None] + [b[p] - b[8 - p] for p in (1, 2, 3)]
    g = [None] + [b[p] + b[8 - p] for p in (1, 2, 3)]
    d2, g2 = C2 * d[2], C2 * g[2]
    re1, re3 = C1 * d[1] + C3 * d[3], C3 * d[1] - C1 * d[3]
    im1, im3 = C3 * g[1] + C1 * g[3], C1 * g[1] - C3 * g[3]
    up, down = b[0] + d2, b[0] - d2
    bp, bm = b[4] + g2, b[4] - g2
    return [
        (e02 + e13, None),
        (up + re1, -(bp + im1)),
        (f[0] + fd, -(f[2] + fs)),
        (down + re3, bm - im3),
        (e[0] - e[2], e[3] - e[1]),
        (down - re3, -(bm + im3)),
        (f[0] - fd, f[2] - fs),
        (up - re1, bp - im1),
        (e02 - e13, None),
    ]


def last_stage(u):
    re = [pair[0] for pair in u]
    im = [pair[1] for pair in u]
    sum08, dif08 = re[0] + re[8], re[0] - re[8]
    r26, i26 = re[2] + re[6], im[2] - im[6]
    rd, sd = C2 * (re[2] - re[6]), C2 * (im[2] + im[6])
    top, low = sum08 + re[4], sum08 - re[4]
    dp, dm = dif08 + rd, dif08 - rd
    ip, im4 = sd + im[4], sd - im[4]
    even = [
        top + r26,
        dp - ip,
        low - i26,
        dm - im4,
        top - r26,
        dm + im4,
        low + i26,
        dp + ip,
    ]
    a1p, a1m = re[1] + re[7], re[1] - re[7]
    a3p, a3m = re[3] + re[5], re[3] - re[5]
    j1p, j1m = im[1] + im[7], im[1] - im[7]
    j3p, j3m = im[3] + im[5], im[3] - im[5]
    c1, c3 = C1 * a1m + C3 * a3m, C3 * a1m - C1 * a3m
    c2 = C2 * (a1p - a3p)
    s1, s3 = C3 * j1p + C1 * j3p, C1 * j1p - C3 * j3p
    s2 = C2 * (j1m + j3m)
    odd = [
        a1p + a3p,
        c1 - s1,
        c2 - s2,
        c3 - s3,
        j3m - j1m,
        -(c3 + s3),
        -(c2 + s2),
        -(c1 + s1),
    ]
    return [x + y for x, y in zip(even, odd)]


def rows_loop(rows, body):
    @pl.loop(0, rows // TILE)
    def _(step):
        body(pl.ds(pl.multiple_of(step * TILE, TILE), TILE))


def split_rows(load, mid, rows, width):
    def body(at):
        for r, pair in enumerate(first_stage([load(p, at) for p in range(BLOCKS)])):
            mid[r, at, :width] = pair[0].astype(jnp.bfloat16)
            if pair[1] is not None:
                mid[r, at, width:] = pair[1].astype(jnp.bfloat16)

    rows_loop(rows, body)


def spectrum(mid, table, r, width):
    if r in (0, GROUPS - 1):
        return jnp.dot(mid[r, :, :width], table[r, :width, :], preferred_element_type=jnp.float32)
    return jnp.dot(mid[r], table[r], preferred_element_type=jnp.float32)


def invert_group(product, table, r, width, wide):
    if r in (0, GROUPS - 1):
        wide[r, :, :width] = jnp.dot(product, table[r, :, :width], preferred_element_type=jnp.float32)
    else:
        wide[r] = jnp.dot(product, table[r], preferred_element_type=jnp.float32)


def merge_rows(wide, store, rows, width):
    def body(at):
        parts = []
        for r in range(GROUPS):
            im = None if r in (0, GROUPS - 1) else wide[r, at, width:]
            parts.append((wide[r, at, :width], im))
        for p, value in enumerate(last_stage(parts)):
            store(p, at, value)

    rows_loop(rows, body)


def piece_at(ref, where, k, rows):
    start = pl.multiple_of(lax.bitwise_xor(where[0], k) * rows, rows)
    return ref.at[pl.ds(start, rows), :]


def gate_kernel(order, where, gate, upper, *refs):
    outs, (left, right, sems) = refs[: len(order)], refs[len(order) :]
    rows = outs[0].shape[0]
    loads = []
    for i, k in enumerate(order):
        pair = (
            pltpu.make_async_copy(piece_at(gate, where, k, rows), left.at[i], sems.at[0, i]),
            pltpu.make_async_copy(piece_at(upper, where, k, rows), right.at[i], sems.at[1, i]),
        )
        for copy in pair:
            copy.start()
        loads.append(pair)
    for i, out in enumerate(outs):
        for copy in loads[i]:
            copy.wait()
        out[...] = (left[i].astype(jnp.float32) * right[i].astype(jnp.float32)).astype(jnp.bfloat16)


def finish_kernel(order, scale, where, *refs):
    pieces, shares, (whole, total) = refs[: len(order)], refs[len(order) : -2], refs[-2:]
    added = shares[0][...].astype(jnp.float32)
    for share in shares[1:]:
        added = added + share[...].astype(jnp.float32)
    total[...] = added * scale
    for k, piece in zip(order, pieces):
        whole[lax.bitwise_xor(where[0], k)] = piece[...]


def taps_kernel(order, where, whole, taps, forward, *refs):
    picks, (taps_spec, mid, sems) = refs[: len(order)], refs[len(order) :]
    rows, width = (taps.shape[0], taps.shape[1] // BLOCKS)
    moves = []
    for i, k in enumerate(order):
        moves.append(pltpu.make_async_copy(piece_at(whole, where, k, rows), picks[i], sems.at[i]))
        moves[-1].start()
    split_rows(lambda p, at: taps[at, p * width : (p + 1) * width], mid, rows, width)
    for r in range(GROUPS):
        taps_spec[r] = spectrum(mid, forward, r, width).astype(taps_spec.dtype)
    for copy in moves:
        copy.wait()


def ordered(order, where, refs, held):
    span = refs[0].shape[1]
    for k, ref in zip(order, refs):
        start = pl.multiple_of(lax.bitwise_xor(where[0], k) * span, span)
        held[:, pl.ds(start, span)] = ref[...]


def block_of(held, width):
    return lambda p, at: held[at, p * width : (p + 1) * width].astype(jnp.float32)


def block_into(held, width):
    def store(p, at, value):
        held[at, p * width : (p + 1) * width] = value.astype(jnp.bfloat16)

    return store


def back_kernel(order, back_order, late, where, *refs):
    blocks, refs = refs[: len(order)], refs[len(order) + late :]
    taps_spec, forward, backward, *outs, grad_spec, held, mid, wide = refs
    outs = outs[late:]
    rows, width = held.shape[0], held.shape[1] // BLOCKS
    ordered(order, where, blocks, held)
    split_rows(block_of(held, width), mid, rows, width)
    for r in range(GROUPS):
        grad = spectrum(mid, forward, r, width)
        grad_spec[r] = grad.astype(grad_spec.dtype)
        taps = taps_spec[r].astype(jnp.float32)
        gr, gi, hr, hi = grad[:, :width], grad[:, width:], taps[:, :width], taps[:, width:]
        product = jnp.concatenate([hr * gr + hi * gi, hr * gi - hi * gr], axis=1)
        invert_group(product.astype(jnp.bfloat16), backward, r, width, wide)
    merge_rows(wide, block_into(held, width), rows, width)
    span = outs[0].shape[1]
    for k, out in zip(back_order, outs):
        start = pl.multiple_of(lax.bitwise_xor(where[0], k) * span, span)
        out[...] = held[:, pl.ds(start, span)]


def cross_kernel(order, where, *refs):
    blocks, refs = refs[: len(order)], refs[len(order) :]
    grad_spec, forward, backward, *outs, held, mid, wide = refs
    rows, width = held.shape[0], held.shape[1] // BLOCKS
    ordered(order, where, blocks, held)
    split_rows(block_of(held, width), mid, rows, width)
    for r in range(GROUPS):
        signal = spectrum(mid, forward, r, width)
        grad = grad_spec[r].astype(jnp.float32)
        gr, gi, xr, xi = grad[:, :width], grad[:, width:], signal[:, :width], signal[:, width:]
        product = jnp.concatenate([gr * xr + gi * xi, gi * xr - gr * xi], axis=1)
        invert_group(product.astype(jnp.bfloat16), backward, r, width, wide)
    merge_rows(wide, block_into(held, width), rows, width)
    part = held.shape[1] // len(outs)
    for k, out in zip(far_first(len(outs)), outs):
        start = pl.multiple_of(lax.bitwise_xor(where[1], k) * part, part)
        out[...] = held[:, pl.ds(start, part)]


def call(kernel, operands, outs, scratch=(), flops=0, streams=(), out_streams=(), aliases=None, hbm=()):
    def spec(stream):
        return pl.BlockSpec(memory_space=pl.ANY if stream else pltpu.VMEM)

    size = sum(math.prod(o.shape) * o.dtype.itemsize for o in list(operands) + list(outs))
    specs = [spec(i in streams) for i in range(len(operands))]
    for i in hbm:
        specs[i] = pl.BlockSpec(memory_space=pltpu.HBM)
    if operands[0].dtype == jnp.int32:
        specs[0] = pl.BlockSpec(memory_space=pltpu.SMEM)
    outputs = pl.pallas_call(
        kernel,
        out_shape=list(outs),
        in_specs=specs,
        out_specs=[spec(i in out_streams) for i in range(len(outs))],
        scratch_shapes=list(scratch),
        input_output_aliases=aliases or {},
        compiler_params=pltpu.CompilerParams(vmem_limit_bytes=LIMIT),
        cost_estimate=pl.CostEstimate(flops=flops, bytes_accessed=size, transcendentals=0),
    )(*operands)
    return list(outputs)


def far_first(size):
    return [*range(size // 2, size), *range(1, size // 2), 0]


def spread(size, order):
    part = size // 8
    return [k * part + i for k in order for i in range(part)] + [*range(1, part), 0]


def exchange(pieces, order, axis, size):
    moved = []
    for k, piece in zip(order, pieces):
        moved.append(lax.ppermute(piece, axis, [(i, i ^ k) for i in range(size)]) if k else piece)
    return moved


def on_device(saved_input, out_gate, grad_out, long_filter):
    count, shares = lax.axis_size("ctx"), lax.axis_size("dp")
    channels, span = saved_input.shape[1:]
    rows, length = long_filter.shape
    width = length // BLOCKS
    grad_order, input_order, back_order = (spread(count, o) for o in ((4, 1, 5, 2, 6, 7, 3), (4, 5, 6, 7, 1, 2, 3), (1, 4, 2, 5, 6, 7, 3)))
    late = 4
    at = count - 1 - late
    every = range(count + 8)
    where = jnp.stack([lax.axis_index("ctx"), lax.axis_index("dp")]).astype(jnp.int32)
    forward, backward = (jnp.asarray(t) for t in transform_tables(width))
    half, full = jnp.bfloat16, jnp.float32
    piece = jax.ShapeDtypeStruct((rows, span), half)
    spec = jax.ShapeDtypeStruct((GROUPS, rows, 2 * width), half)
    held = pltpu.VMEM((rows, length), half)
    mid = pltpu.VMEM((GROUPS, rows, 2 * width), half)
    wide = pltpu.VMEM((GROUPS, rows, 2 * width), full)
    slots = pltpu.VMEM((count, rows, span), half)
    sems = pltpu.SemaphoreType.DMA
    work = 2 * GROUPS * rows * 4 * width * width

    stay = [pltpu.with_memory_space_constraint(x[0], pltpu.HBM) for x in (out_gate, grad_out, saved_input)]
    grad_pieces = call(
        functools.partial(gate_kernel, grad_order),
        [where, *stay[:2]],
        [piece] * count,
        [slots, slots, sems((2, count))],
        hbm=(1, 2),
    )
    grad_blocks = exchange(grad_pieces, grad_order, "ctx", count)
    *input_pieces, taps_spec = call(
        functools.partial(taps_kernel, input_order),
        [where, stay[2], long_filter, forward],
        [piece] * count + [spec],
        [mid, sems((count,))],
        flops=work,
        hbm=(1,),
    )
    passed = [*input_pieces[at : at + late]]
    *back, grad_spec = call(
        functools.partial(back_kernel, grad_order, back_order, late),
        [where, *grad_blocks, *passed, taps_spec, forward, backward],
        [piece] * (late + count) + [spec],
        [held, mid, wide],
        flops=2 * work,
        streams=range(1 + count, 1 + count + late),
        out_streams=range(late),
        aliases={1 + count + i: i for i in range(late)},
    )
    input_pieces[at : at + late], back = back[:late], back[late:]
    input_blocks = exchange(input_pieces, input_order, "ctx", count)
    back_blocks = exchange(back, back_order, "ctx", count)
    share = jax.ShapeDtypeStruct((rows, length // shares), half)
    cross = call(
        functools.partial(cross_kernel, input_order),
        [where, *input_blocks, grad_spec, forward, backward],
        [share] * shares,
        [held, mid, wide],
        flops=2 * work,
    )
    cross_blocks = exchange(cross, far_first(shares), "dp", shares)
    scale = 1.0 / math.sqrt(shares * length)
    whole, grad_filter = call(
        functools.partial(finish_kernel, back_order, scale),
        [where, *back_blocks, *cross_blocks],
        [jax.ShapeDtypeStruct((count, rows, span), half), jax.ShapeDtypeStruct((rows, length // shares), full)],
    )
    return (whole.reshape(1, channels, span), grad_filter)


def solution(mesh):
    in_specs = (P("dp", None, "ctx"), P("dp", None, "ctx"), P("dp", None, "ctx"), P("ctx", None))
    out_specs = (P("dp", None, "ctx"), P("ctx", "dp"))
    return jax.shard_map(
        on_device, mesh=mesh, in_specs=in_specs, out_specs=out_specs, check_vma=False
    )
```

```python
import functools
import math

import jax
import jax.numpy as jnp
import ml_dtypes
import numpy as np
from jax import lax
from jax.experimental import pallas as pl
from jax.experimental.pallas import tpu as pltpu
from jax.sharding import PartitionSpec as P

BLOCKS = 8
GROUPS = 9
TILE = 16
C1 = math.cos(math.pi / 8)
C2 = math.cos(math.pi / 4)
C3 = math.cos(3 * math.pi / 8)
LIMIT = 32 * 1024 * 1024


def transform_tables(width):
    points = 2 * BLOCKS * width
    row = np.arange(width)
    forward = np.zeros((GROUPS, 2 * width, 2 * width), np.float64)
    for r in range(GROUPS):
        angle = 2.0 * np.pi * (np.outer(row, 16 * row + r) % points) / points
        cos, sin = np.cos(angle), np.sin(angle)
        forward[r] = np.block([[cos, -sin], [sin, cos]])
    scale = np.full((GROUPS, 1, 1), 2.0 / points)
    scale[0] = scale[-1] = 1.0 / points
    backward = np.swapaxes(forward, 1, 2) * scale
    return forward.astype(ml_dtypes.bfloat16), backward.astype(ml_dtypes.bfloat16)


def first_stage(b):
    e = [b[p] + b[p + 4] for p in range(4)]
    f = [b[p] - b[p + 4] for p in range(4)]
    e02, e13 = e[0] + e[2], e[1] + e[3]
    fd, fs = C2 * (f[1] - f[3]), C2 * (f[1] + f[3])
    d = [None] + [b[p] - b[8 - p] for p in (1, 2, 3)]
    g = [None] + [b[p] + b[8 - p] for p in (1, 2, 3)]
    d2, g2 = C2 * d[2], C2 * g[2]
    re1, re3 = C1 * d[1] + C3 * d[3], C3 * d[1] - C1 * d[3]
    im1, im3 = C3 * g[1] + C1 * g[3], C1 * g[1] - C3 * g[3]
    up, down = b[0] + d2, b[0] - d2
    bp, bm = b[4] + g2, b[4] - g2
    return [
        (e02 + e13, None),
        (up + re1, -(bp + im1)),
        (f[0] + fd, -(f[2] + fs)),
        (down + re3, bm - im3),
        (e[0] - e[2], e[3] - e[1]),
        (down - re3, -(bm + im3)),
        (f[0] - fd, f[2] - fs),
        (up - re1, bp - im1),
        (e02 - e13, None),
    ]


def last_stage(u):
    re = [pair[0] for pair in u]
    im = [pair[1] for pair in u]
    sum08, dif08 = re[0] + re[8], re[0] - re[8]
    r26, i26 = re[2] + re[6], im[2] - im[6]
    rd, sd = C2 * (re[2] - re[6]), C2 * (im[2] + im[6])
    top, low = sum08 + re[4], sum08 - re[4]
    dp, dm = dif08 + rd, dif08 - rd
    ip, im4 = sd + im[4], sd - im[4]
    even = [
        top + r26,
        dp - ip,
        low - i26,
        dm - im4,
        top - r26,
        dm + im4,
        low + i26,
        dp + ip,
    ]
    a1p, a1m = re[1] + re[7], re[1] - re[7]
    a3p, a3m = re[3] + re[5], re[3] - re[5]
    j1p, j1m = im[1] + im[7], im[1] - im[7]
    j3p, j3m = im[3] + im[5], im[3] - im[5]
    c1, c3 = C1 * a1m + C3 * a3m, C3 * a1m - C1 * a3m
    c2 = C2 * (a1p - a3p)
    s1, s3 = C3 * j1p + C1 * j3p, C1 * j1p - C3 * j3p
    s2 = C2 * (j1m + j3m)
    odd = [
        a1p + a3p,
        c1 - s1,
        c2 - s2,
        c3 - s3,
        j3m - j1m,
        -(c3 + s3),
        -(c2 + s2),
        -(c1 + s1),
    ]
    return [x + y for x, y in zip(even, odd)]


def rows_loop(rows, body):
    @pl.loop(0, rows // TILE)
    def _(step):
        body(pl.ds(pl.multiple_of(step * TILE, TILE), TILE))


def split_rows(load, mid, rows, width):
    def body(at):
        for r, pair in enumerate(first_stage([load(p, at) for p in range(BLOCKS)])):
            mid[r, at, :width] = pair[0].astype(jnp.bfloat16)
            if pair[1] is not None:
                mid[r, at, width:] = pair[1].astype(jnp.bfloat16)

    rows_loop(rows, body)


def spectrum(mid, table, r, width):
    if r in (0, GROUPS - 1):
        return jnp.dot(mid[r, :, :width], table[r, :width, :], preferred_element_type=jnp.float32)
    return jnp.dot(mid[r], table[r], preferred_element_type=jnp.float32)


def invert_group(product, table, r, width, wide):
    if r in (0, GROUPS - 1):
        wide[r, :, :width] = jnp.dot(product, table[r, :, :width], preferred_element_type=jnp.float32)
    else:
        wide[r] = jnp.dot(product, table[r], preferred_element_type=jnp.float32)


def merge_rows(wide, store, rows, width):
    def body(at):
        parts = []
        for r in range(GROUPS):
            im = None if r in (0, GROUPS - 1) else wide[r, at, width:]
            parts.append((wide[r, at, :width], im))
        for p, value in enumerate(last_stage(parts)):
            store(p, at, value)

    rows_loop(rows, body)


def piece_at(ref, where, k, rows):
    start = pl.multiple_of(lax.bitwise_xor(where[0], k) * rows, rows)
    return ref.at[pl.ds(start, rows), :]


def gate_kernel(order, where, gate, upper, *refs):
    outs, (left, right, sems) = refs[: len(order)], refs[len(order) :]
    rows = outs[0].shape[0]
    loads = []
    for i, k in enumerate(order):
        pair = (
            pltpu.make_async_copy(piece_at(gate, where, k, rows), left.at[i], sems.at[0, i]),
            pltpu.make_async_copy(piece_at(upper, where, k, rows), right.at[i], sems.at[1, i]),
        )
        for copy in pair:
            copy.start()
        loads.append(pair)
    for i, out in enumerate(outs):
        for copy in loads[i]:
            copy.wait()
        out[...] = (left[i].astype(jnp.float32) * right[i].astype(jnp.float32)).astype(jnp.bfloat16)


def finish_kernel(order, scale, where, *refs):
    pieces, shares, (whole, total) = refs[: len(order)], refs[len(order) : -2], refs[-2:]
    added = shares[0][...].astype(jnp.float32)
    for share in shares[1:]:
        added = added + share[...].astype(jnp.float32)
    total[...] = added * scale
    for k, piece in zip(order, pieces):
        whole[lax.bitwise_xor(where[0], k)] = piece[...]


def taps_kernel(order, where, whole, taps, forward, *refs):
    picks, (taps_spec, mid, sems) = refs[: len(order)], refs[len(order) :]
    rows, width = (taps.shape[0], taps.shape[1] // BLOCKS)
    moves = []
    for i, k in enumerate(order):
        moves.append(pltpu.make_async_copy(piece_at(whole, where, k, rows), picks[i], sems.at[i]))
        moves[-1].start()
    split_rows(lambda p, at: taps[at, p * width : (p + 1) * width], mid, rows, width)
    for r in range(GROUPS):
        taps_spec[r] = spectrum(mid, forward, r, width).astype(taps_spec.dtype)
    for copy in moves:
        copy.wait()


def ordered(order, where, refs, held):
    span = refs[0].shape[1]
    for k, ref in zip(order, refs):
        start = pl.multiple_of(lax.bitwise_xor(where[0], k) * span, span)
        held[:, pl.ds(start, span)] = ref[...]


def block_of(held, width):
    return lambda p, at: held[at, p * width : (p + 1) * width].astype(jnp.float32)


def block_into(held, width):
    def store(p, at, value):
        held[at, p * width : (p + 1) * width] = value.astype(jnp.bfloat16)

    return store


def back_kernel(order, back_order, late, where, *refs):
    blocks, refs = refs[: len(order)], refs[len(order) + late :]
    taps_spec, forward, backward, *outs, grad_spec, held, mid, wide = refs
    outs = outs[late:]
    rows, width = held.shape[0], held.shape[1] // BLOCKS
    ordered(order, where, blocks, held)
    split_rows(block_of(held, width), mid, rows, width)
    for r in range(GROUPS):
        grad = spectrum(mid, forward, r, width)
        grad_spec[r] = grad.astype(grad_spec.dtype)
        taps = taps_spec[r].astype(jnp.float32)
        gr, gi, hr, hi = grad[:, :width], grad[:, width:], taps[:, :width], taps[:, width:]
        product = jnp.concatenate([hr * gr + hi * gi, hr * gi - hi * gr], axis=1)
        invert_group(product.astype(jnp.bfloat16), backward, r, width, wide)
    merge_rows(wide, block_into(held, width), rows, width)
    span = outs[0].shape[1]
    for k, out in zip(back_order, outs):
        start = pl.multiple_of(lax.bitwise_xor(where[0], k) * span, span)
        out[...] = held[:, pl.ds(start, span)]


def cross_kernel(order, where, *refs):
    blocks, refs = refs[: len(order)], refs[len(order) :]
    grad_spec, forward, backward, *outs, held, mid, wide = refs
    rows, width = held.shape[0], held.shape[1] // BLOCKS
    ordered(order, where, blocks, held)
    split_rows(block_of(held, width), mid, rows, width)
    for r in range(GROUPS):
        signal = spectrum(mid, forward, r, width)
        grad = grad_spec[r].astype(jnp.float32)
        gr, gi, xr, xi = grad[:, :width], grad[:, width:], signal[:, :width], signal[:, width:]
        product = jnp.concatenate([gr * xr + gi * xi, gi * xr - gr * xi], axis=1)
        invert_group(product.astype(jnp.bfloat16), backward, r, width, wide)
    merge_rows(wide, block_into(held, width), rows, width)
    part = held.shape[1] // len(outs)
    for k, out in zip(far_first(len(outs)), outs):
        start = pl.multiple_of(lax.bitwise_xor(where[1], k) * part, part)
        out[...] = held[:, pl.ds(start, part)]


def call(kernel, operands, outs, scratch=(), flops=0, streams=(), out_streams=(), aliases=None, hbm=()):
    def spec(stream):
        return pl.BlockSpec(memory_space=pl.ANY if stream else pltpu.VMEM)

    size = sum(math.prod(o.shape) * o.dtype.itemsize for o in list(operands) + list(outs))
    specs = [spec(i in streams) for i in range(len(operands))]
    for i in hbm:
        specs[i] = pl.BlockSpec(memory_space=pltpu.HBM)
    if operands[0].dtype == jnp.int32:
        specs[0] = pl.BlockSpec(memory_space=pltpu.SMEM)
    outputs = pl.pallas_call(
        kernel,
        out_shape=list(outs),
        in_specs=specs,
        out_specs=[spec(i in out_streams) for i in range(len(outs))],
        scratch_shapes=list(scratch),
        input_output_aliases=aliases or {},
        compiler_params=pltpu.CompilerParams(vmem_limit_bytes=LIMIT),
        cost_estimate=pl.CostEstimate(flops=flops, bytes_accessed=size, transcendentals=0),
    )(*operands)
    return list(outputs)


def far_first(size):
    return [*range(size // 2, size), *range(1, size // 2), 0]


def spread(size, order):
    part = size // 8
    return [k * part + i for k in order for i in range(part)] + [*range(1, part), 0]


def exchange(pieces, order, axis, size):
    moved = []
    for k, piece in zip(order, pieces):
        moved.append(lax.ppermute(piece, axis, [(i, i ^ k) for i in range(size)]) if k else piece)
    return moved


def on_device(saved_input, out_gate, grad_out, long_filter):
    count, shares = lax.axis_size("ctx"), lax.axis_size("dp")
    channels, span = saved_input.shape[1:]
    rows, length = long_filter.shape
    width = length // BLOCKS
    grad_order, input_order, back_order = (spread(count, o) for o in ((4, 1, 5, 2, 6, 7, 3), (4, 5, 6, 1, 7, 2, 3), (1, 4, 2, 5, 6, 7, 3)))
    late = 3
    at = count - 1 - late
    every = range(count + 8)
    where = jnp.stack([lax.axis_index("ctx"), lax.axis_index("dp")]).astype(jnp.int32)
    forward, backward = (jnp.asarray(t) for t in transform_tables(width))
    half, full = jnp.bfloat16, jnp.float32
    piece = jax.ShapeDtypeStruct((rows, span), half)
    spec = jax.ShapeDtypeStruct((GROUPS, rows, 2 * width), half)
    held = pltpu.VMEM((rows, length), half)
    mid = pltpu.VMEM((GROUPS, rows, 2 * width), half)
    wide = pltpu.VMEM((GROUPS, rows, 2 * width), full)
    slots = pltpu.VMEM((count, rows, span), half)
    sems = pltpu.SemaphoreType.DMA
    work = 2 * GROUPS * rows * 4 * width * width

    stay = [pltpu.with_memory_space_constraint(x[0], pltpu.HBM) for x in (out_gate, grad_out, saved_input)]
    grad_pieces = call(
        functools.partial(gate_kernel, grad_order),
        [where, *stay[:2]],
        [piece] * count,
        [slots, slots, sems((2, count))],
        hbm=(1, 2),
    )
    grad_blocks = exchange(grad_pieces, grad_order, "ctx", count)
    *input_pieces, taps_spec = call(
        functools.partial(taps_kernel, input_order),
        [where, stay[2], pltpu.with_memory_space_constraint(long_filter, pltpu.HBM), forward],
        [piece] * count + [spec],
        [mid, sems((count,))],
        flops=work,
        hbm=(1,),
    )
    passed = [*input_pieces[at : at + late]]
    *back, grad_spec = call(
        functools.partial(back_kernel, grad_order, back_order, late),
        [where, *grad_blocks, *passed, taps_spec, forward, backward],
        [piece] * (late + count) + [spec],
        [held, mid, wide],
        flops=2 * work,
        streams=range(1 + count, 1 + count + late),
        out_streams=range(late),
        aliases={1 + count + i: i for i in range(late)},
    )
    input_pieces[at : at + late], back = back[:late], back[late:]
    input_blocks = exchange(input_pieces, input_order, "ctx", count)
    back_blocks = exchange(back, back_order, "ctx", count)
    share = jax.ShapeDtypeStruct((rows, length // shares), half)
    cross = call(
        functools.partial(cross_kernel, input_order),
        [where, *input_blocks, grad_spec, forward, backward],
        [share] * shares,
        [held, mid, wide],
        flops=2 * work,
    )
    cross_blocks = exchange(cross, far_first(shares), "dp", shares)
    scale = 1.0 / math.sqrt(shares * length)
    whole, grad_filter = call(
        functools.partial(finish_kernel, back_order, scale),
        [where, *back_blocks, *cross_blocks],
        [jax.ShapeDtypeStruct((count, rows, span), half), jax.ShapeDtypeStruct((rows, length // shares), full)],
    )
    return (whole.reshape(1, channels, span), grad_filter)


def solution(mesh):
    in_specs = (P("dp", None, "ctx"), P("dp", None, "ctx"), P("dp", None, "ctx"), P("ctx", None))
    out_specs = (P("dp", None, "ctx"), P("ctx", "dp"))
    return jax.shard_map(
        on_device, mesh=mesh, in_specs=in_specs, out_specs=out_specs, check_vma=False
    )
```

```python
import functools
import math

import jax
import jax.numpy as jnp
import ml_dtypes
import numpy as np
from jax import lax
from jax.experimental import pallas as pl
from jax.experimental.pallas import tpu as pltpu
from jax.sharding import PartitionSpec as P

BLOCKS = 8
GROUPS = 9
TILE = 16
C1 = math.cos(math.pi / 8)
C2 = math.cos(math.pi / 4)
C3 = math.cos(3 * math.pi / 8)
LIMIT = 32 * 1024 * 1024


def transform_tables(width):
    points = 2 * BLOCKS * width
    row = np.arange(width)
    forward = np.zeros((GROUPS, 2 * width, 2 * width), np.float64)
    for r in range(GROUPS):
        angle = 2.0 * np.pi * (np.outer(row, 16 * row + r) % points) / points
        cos, sin = np.cos(angle), np.sin(angle)
        forward[r] = np.block([[cos, -sin], [sin, cos]])
    scale = np.full((GROUPS, 1, 1), 2.0 / points)
    scale[0] = scale[-1] = 1.0 / points
    backward = np.swapaxes(forward, 1, 2) * scale
    return forward.astype(ml_dtypes.bfloat16), backward.astype(ml_dtypes.bfloat16)


def first_stage(b):
    e = [b[p] + b[p + 4] for p in range(4)]
    f = [b[p] - b[p + 4] for p in range(4)]
    e02, e13 = e[0] + e[2], e[1] + e[3]
    fd, fs = C2 * (f[1] - f[3]), C2 * (f[1] + f[3])
    d = [None] + [b[p] - b[8 - p] for p in (1, 2, 3)]
    g = [None] + [b[p] + b[8 - p] for p in (1, 2, 3)]
    d2, g2 = C2 * d[2], C2 * g[2]
    re1, re3 = C1 * d[1] + C3 * d[3], C3 * d[1] - C1 * d[3]
    im1, im3 = C3 * g[1] + C1 * g[3], C1 * g[1] - C3 * g[3]
    up, down = b[0] + d2, b[0] - d2
    bp, bm = b[4] + g2, b[4] - g2
    return [
        (e02 + e13, None),
        (up + re1, -(bp + im1)),
        (f[0] + fd, -(f[2] + fs)),
        (down + re3, bm - im3),
        (e[0] - e[2], e[3] - e[1]),
        (down - re3, -(bm + im3)),
        (f[0] - fd, f[2] - fs),
        (up - re1, bp - im1),
        (e02 - e13, None),
    ]


def last_stage(u):
    re = [pair[0] for pair in u]
    im = [pair[1] for pair in u]
    sum08, dif08 = re[0] + re[8], re[0] - re[8]
    r26, i26 = re[2] + re[6], im[2] - im[6]
    rd, sd = C2 * (re[2] - re[6]), C2 * (im[2] + im[6])
    top, low = sum08 + re[4], sum08 - re[4]
    dp, dm = dif08 + rd, dif08 - rd
    ip, im4 = sd + im[4], sd - im[4]
    even = [
        top + r26,
        dp - ip,
        low - i26,
        dm - im4,
        top - r26,
        dm + im4,
        low + i26,
        dp + ip,
    ]
    a1p, a1m = re[1] + re[7], re[1] - re[7]
    a3p, a3m = re[3] + re[5], re[3] - re[5]
    j1p, j1m = im[1] + im[7], im[1] - im[7]
    j3p, j3m = im[3] + im[5], im[3] - im[5]
    c1, c3 = C1 * a1m + C3 * a3m, C3 * a1m - C1 * a3m
    c2 = C2 * (a1p - a3p)
    s1, s3 = C3 * j1p + C1 * j3p, C1 * j1p - C3 * j3p
    s2 = C2 * (j1m + j3m)
    odd = [
        a1p + a3p,
        c1 - s1,
        c2 - s2,
        c3 - s3,
        j3m - j1m,
        -(c3 + s3),
        -(c2 + s2),
        -(c1 + s1),
    ]
    return [x + y for x, y in zip(even, odd)]


def rows_loop(rows, body):
    @pl.loop(0, rows // TILE)
    def _(step):
        body(pl.ds(pl.multiple_of(step * TILE, TILE), TILE))


def split_rows(load, mid, rows, width):
    def body(at):
        for r, pair in enumerate(first_stage([load(p, at) for p in range(BLOCKS)])):
            mid[r, at, :width] = pair[0].astype(jnp.bfloat16)
            if pair[1] is not None:
                mid[r, at, width:] = pair[1].astype(jnp.bfloat16)

    rows_loop(rows, body)


def spectrum(mid, table, r, width):
    if r in (0, GROUPS - 1):
        return jnp.dot(mid[r, :, :width], table[r, :width, :], preferred_element_type=jnp.float32)
    return jnp.dot(mid[r], table[r], preferred_element_type=jnp.float32)


def invert_group(product, table, r, width, wide):
    if r in (0, GROUPS - 1):
        wide[r, :, :width] = jnp.dot(product, table[r, :, :width], preferred_element_type=jnp.float32)
    else:
        wide[r] = jnp.dot(product, table[r], preferred_element_type=jnp.float32)


def merge_rows(wide, store, rows, width):
    def body(at):
        parts = []
        for r in range(GROUPS):
            im = None if r in (0, GROUPS - 1) else wide[r, at, width:]
            parts.append((wide[r, at, :width], im))
        for p, value in enumerate(last_stage(parts)):
            store(p, at, value)

    rows_loop(rows, body)


def piece_at(ref, where, k, rows):
    start = pl.multiple_of(lax.bitwise_xor(where[0], k) * rows, rows)
    return ref.at[pl.ds(start, rows), :]


def gate_kernel(order, where, gate, upper, *refs):
    outs, (left, right, sems) = refs[: len(order)], refs[len(order) :]
    rows = outs[0].shape[0]
    loads = []
    for i, k in enumerate(order):
        pair = (
            pltpu.make_async_copy(piece_at(gate, where, k, rows), left.at[i], sems.at[0, i]),
            pltpu.make_async_copy(piece_at(upper, where, k, rows), right.at[i], sems.at[1, i]),
        )
        for copy in pair:
            copy.start()
        loads.append(pair)
    for i, out in enumerate(outs):
        for copy in loads[i]:
            copy.wait()
        out[...] = (left[i].astype(jnp.float32) * right[i].astype(jnp.float32)).astype(jnp.bfloat16)


def finish_kernel(order, scale, where, *refs):
    pieces, shares, (whole, total) = refs[: len(order)], refs[len(order) : -2], refs[-2:]
    added = shares[0][...].astype(jnp.float32)
    for share in shares[1:]:
        added = added + share[...].astype(jnp.float32)
    total[...] = added * scale
    for k, piece in zip(order, pieces):
        whole[lax.bitwise_xor(where[0], k)] = piece[...]


def taps_kernel(order, where, whole, taps, forward, *refs):
    picks, (taps_spec, mid, sems) = refs[: len(order)], refs[len(order) :]
    rows, width = (taps.shape[0], taps.shape[1] // BLOCKS)
    moves = []
    for i, k in enumerate(order):
        moves.append(pltpu.make_async_copy(piece_at(whole, where, k, rows), picks[i], sems.at[i]))
        moves[-1].start()
    split_rows(lambda p, at: taps[at, p * width : (p + 1) * width], mid, rows, width)
    for r in range(GROUPS):
        taps_spec[r] = spectrum(mid, forward, r, width).astype(taps_spec.dtype)
    for copy in moves:
        copy.wait()


def ordered(order, where, refs, held):
    span = refs[0].shape[1]
    for k, ref in zip(order, refs):
        start = pl.multiple_of(lax.bitwise_xor(where[0], k) * span, span)
        held[:, pl.ds(start, span)] = ref[...]


def block_of(held, width):
    return lambda p, at: held[at, p * width : (p + 1) * width].astype(jnp.float32)


def block_into(held, width):
    def store(p, at, value):
        held[at, p * width : (p + 1) * width] = value.astype(jnp.bfloat16)

    return store


def back_kernel(order, back_order, late, where, *refs):
    blocks, refs = refs[: len(order)], refs[len(order) + late :]
    taps_spec, forward, backward, *outs, grad_spec, held, mid, wide = refs
    outs = outs[late:]
    rows, width = held.shape[0], held.shape[1] // BLOCKS
    ordered(order, where, blocks, held)
    split_rows(block_of(held, width), mid, rows, width)
    for r in range(GROUPS):
        grad = spectrum(mid, forward, r, width)
        grad_spec[r] = grad.astype(grad_spec.dtype)
        taps = taps_spec[r].astype(jnp.float32)
        gr, gi, hr, hi = grad[:, :width], grad[:, width:], taps[:, :width], taps[:, width:]
        product = jnp.concatenate([hr * gr + hi * gi, hr * gi - hi * gr], axis=1)
        invert_group(product.astype(jnp.bfloat16), backward, r, width, wide)
    merge_rows(wide, block_into(held, width), rows, width)
    span = outs[0].shape[1]
    for k, out in zip(back_order, outs):
        start = pl.multiple_of(lax.bitwise_xor(where[0], k) * span, span)
        out[...] = held[:, pl.ds(start, span)]


def cross_kernel(order, where, *refs):
    blocks, refs = refs[: len(order)], refs[len(order) :]
    grad_spec, forward, backward, *outs, held, mid, wide = refs
    rows, width = held.shape[0], held.shape[1] // BLOCKS
    ordered(order, where, blocks, held)
    split_rows(block_of(held, width), mid, rows, width)
    for r in range(GROUPS):
        signal = spectrum(mid, forward, r, width)
        grad = grad_spec[r].astype(jnp.float32)
        gr, gi, xr, xi = grad[:, :width], grad[:, width:], signal[:, :width], signal[:, width:]
        product = jnp.concatenate([gr * xr + gi * xi, gi * xr - gr * xi], axis=1)
        invert_group(product.astype(jnp.bfloat16), backward, r, width, wide)
    merge_rows(wide, block_into(held, width), rows, width)
    part = held.shape[1] // len(outs)
    for k, out in zip(far_first(len(outs)), outs):
        start = pl.multiple_of(lax.bitwise_xor(where[1], k) * part, part)
        out[...] = held[:, pl.ds(start, part)]


def call(kernel, operands, outs, scratch=(), flops=0, streams=(), out_streams=(), aliases=None, hbm=()):
    def spec(stream):
        return pl.BlockSpec(memory_space=pl.ANY if stream else pltpu.VMEM)

    size = sum(math.prod(o.shape) * o.dtype.itemsize for o in list(operands) + list(outs))
    specs = [spec(i in streams) for i in range(len(operands))]
    for i in hbm:
        specs[i] = pl.BlockSpec(memory_space=pltpu.HBM)
    if operands[0].dtype == jnp.int32:
        specs[0] = pl.BlockSpec(memory_space=pltpu.SMEM)
    outputs = pl.pallas_call(
        kernel,
        out_shape=list(outs),
        in_specs=specs,
        out_specs=[spec(i in out_streams) for i in range(len(outs))],
        scratch_shapes=list(scratch),
        input_output_aliases=aliases or {},
        compiler_params=pltpu.CompilerParams(vmem_limit_bytes=LIMIT),
        cost_estimate=pl.CostEstimate(flops=flops, bytes_accessed=size, transcendentals=0),
    )(*operands)
    return list(outputs)


def far_first(size):
    return [*range(size // 2, size), *range(1, size // 2), 0]


def spread(size, order):
    part = size // 8
    return [k * part + i for k in order for i in range(part)] + [*range(1, part), 0]


def exchange(pieces, order, axis, size):
    moved = []
    for k, piece in zip(order, pieces):
        moved.append(lax.ppermute(piece, axis, [(i, i ^ k) for i in range(size)]) if k else piece)
    return moved


def on_device(saved_input, out_gate, grad_out, long_filter):
    count, shares = lax.axis_size("ctx"), lax.axis_size("dp")
    channels, span = saved_input.shape[1:]
    rows, length = long_filter.shape
    width = length // BLOCKS
    grad_order, input_order, back_order = (spread(count, o) for o in ((4, 1, 5, 6, 2, 7, 3), (4, 5, 6, 1, 7, 2, 3), (1, 4, 2, 5, 6, 7, 3)))
    late = 3
    at = count - 1 - late
    every = range(count + 8)
    where = jnp.stack([lax.axis_index("ctx"), lax.axis_index("dp")]).astype(jnp.int32)
    forward, backward = (jnp.asarray(t) for t in transform_tables(width))
    half, full = jnp.bfloat16, jnp.float32
    piece = jax.ShapeDtypeStruct((rows, span), half)
    spec = jax.ShapeDtypeStruct((GROUPS, rows, 2 * width), half)
    held = pltpu.VMEM((rows, length), half)
    mid = pltpu.VMEM((GROUPS, rows, 2 * width), half)
    wide = pltpu.VMEM((GROUPS, rows, 2 * width), full)
    slots = pltpu.VMEM((count, rows, span), half)
    sems = pltpu.SemaphoreType.DMA
    work = 2 * GROUPS * rows * 4 * width * width

    stay = [pltpu.with_memory_space_constraint(x[0], pltpu.HBM) for x in (out_gate, grad_out, saved_input)]
    grad_pieces = call(
        functools.partial(gate_kernel, grad_order),
        [where, *stay[:2]],
        [piece] * count,
        [slots, slots, sems((2, count))],
        hbm=(1, 2),
    )
    grad_blocks = exchange(grad_pieces, grad_order, "ctx", count)
    *input_pieces, taps_spec = call(
        functools.partial(taps_kernel, input_order),
        [where, stay[2], pltpu.with_memory_space_constraint(long_filter, pltpu.HBM), forward],
        [piece] * count + [spec],
        [mid, sems((count,))],
        flops=work,
        hbm=(1,),
    )
    passed = [*input_pieces[at : at + late]]
    *back, grad_spec = call(
        functools.partial(back_kernel, grad_order, back_order, late),
        [where, *grad_blocks, *passed, taps_spec, forward, backward],
        [piece] * (late + count) + [spec],
        [held, mid, wide],
        flops=2 * work,
        streams=range(1 + count, 1 + count + late),
        out_streams=range(late),
        aliases={1 + count + i: i for i in range(late)},
    )
    input_pieces[at : at + late], back = back[:late], back[late:]
    input_blocks = exchange(input_pieces, input_order, "ctx", count)
    back_blocks = exchange(back, back_order, "ctx", count)
    share = jax.ShapeDtypeStruct((rows, length // shares), half)
    cross = call(
        functools.partial(cross_kernel, input_order),
        [where, *input_blocks, grad_spec, forward, backward],
        [share] * shares,
        [held, mid, wide],
        flops=2 * work,
    )
    cross_blocks = exchange(cross, far_first(shares), "dp", shares)
    scale = 1.0 / math.sqrt(shares * length)
    whole, grad_filter = call(
        functools.partial(finish_kernel, back_order, scale),
        [where, *back_blocks, *cross_blocks],
        [jax.ShapeDtypeStruct((count, rows, span), half), jax.ShapeDtypeStruct((rows, length // shares), full)],
    )
    return (whole.reshape(1, channels, span), grad_filter)


def solution(mesh):
    in_specs = (P("dp", None, "ctx"), P("dp", None, "ctx"), P("dp", None, "ctx"), P("ctx", None))
    out_specs = (P("dp", None, "ctx"), P("ctx", "dp"))
    return jax.shard_map(
        on_device, mesh=mesh, in_specs=in_specs, out_specs=out_specs, check_vma=False
    )
```
